32 devices in a mesh: dp: 4 (over y, x), seq: 8 (over z, core).
Axes of the slice: x: 2, y: 2, z: 4, core: 2. Of those that a mesh axis runs over, the one named last changes fastest.
Arguments:
- qkvu: bfloat16 [4096, 4096], P(('dp', 'seq')), may hold values from -6 to 6
- w_out: bfloat16 [1024, 1024], replicated, may hold values from -0.1875 to 0.1875
- head_coef: bfloat16 [4096, 32], P(('dp', 'seq')), may hold values from -1 to 1
- item_table: bfloat16 [4096, 1024], P('seq'), may hold values from -6 to 6
- neg_ids: int32 [32], P('seq'), may hold values from 0 to 511
- send_order: int32 [32, 128], P(('dp', 'seq')), may hold values from 0 to 127, each once within a row
- recv_order: int32 [32, 128], P(('dp', 'seq')), may hold values from 0 to 127, each once within a row
- tile_len: int32 [4, 8], P('dp'), may hold values from 1 to 128, 341 in all within a row
Outputs:
- layer_out: bfloat16 [4096, 1024], P(('dp', 'seq'))
- d_qkvu: bfloat16 [4096, 4096], P(('dp', 'seq'))
- d_w_out: float32 [1024, 1024], P('seq', 'dp')
The draws below stay inside these ranges and needn't reach their ends.
Inputs may be any that keep to these rules, and one draw needn't show every extreme that they name: Each row of send_order and of recv_order names every number once. `recv_order`: each row names every number once. `tile_len`: in each data group the lengths sum to 341.
All inputs are finite; a program needn't handle non-finite values.
Results may differ from the reference program's by a relative error of at most 0.014.
Values may be sent and summed in bfloat16 or wider, within the bound.
No kernel may reach another device: no remote copies, remote signals or barrier semaphores. Data moves between devices by JAX's collectives and lax.ppermute only.
A program may use at most 64 MiB of HBM per device.

```python
import math
import jax
import jax.numpy as jnp
import numpy as np
from jax import lax

D = 1024
HEADS = 8
TILE = 128
SPAN = 3
NEG = 4
ITEMS_DEV = 512
NEGS = 32
ITEMS = 4096
TOKENS = 4096
N_DP = 4
N_SEQ = 8


def plant(result, rng, least, top_value):
    longest = result.shape.index(max(result.shape))
    spots = []
    for shift in (0, 1):
        where = [jax.random.randint(jax.random.fold_in(rng, axis), (), 0, length) for axis, length in enumerate(result.shape)]
        where[longest] = (where[longest] + shift) % result.shape[longest]
        spots.append(tuple(where))
    return result.at[spots[0]].set(least).at[spots[1]].set(top_value)


def block_levels(key, extent, pieces, smallest, top_value):
    level, own = 1.0, jax.random.fold_in(key, 6)
    for position, blocks in pieces:
        steps = jnp.exp(jax.random.uniform(jax.random.fold_in(own, position), (blocks,), jnp.float32, smallest / len(pieces), top_value / len(pieces)))
        level = level * jnp.repeat(steps, extent[position] // blocks).reshape([-1 if axis == position else 1 for axis in range(len(extent))])
    return level


def length_profile(number_of, total, limit, lean):
    portions = [(1 << 20) // math.isqrt(rank ** lean) + 1 for rank in range(2, number_of + 1)]
    surplus, counts = total - limit - (number_of - 1), [1] * (number_of - 1)
    while surplus > 0:
        free = [i for i in range(number_of - 1) if counts[i] < limit]
        whole, left = sum([portions[i] for i in free]), surplus
        for i in free:
            extra = min(limit - counts[i], max(1, left * portions[i] // whole), surplus)
            counts[i] = counts[i] + extra
            surplus = surplus - extra
    return np.array([limit] + counts)


def ragged_sizes(key, number_of, total, most, slope):
    if number_of == 2:
        one = jax.random.randint(key, (), max(1, total - most), min(most, total - 1) + 1)
        return jnp.stack([one, total - one])
    tallies = jnp.asarray(length_profile(number_of, total, most, slope), jnp.int32)
    couples = (number_of - 1) // 2
    giver, taker = tallies[1:1 + 2 * couples:2], tallies[2:2 + 2 * couples:2]
    margin = jnp.minimum(giver - 1, most - taker)
    passed = jax.random.randint(jax.random.fold_in(key, 1), (couples,), 0, 1 << 20) % (margin + 1)
    tallies = tallies.at[1:1 + 2 * couples:2].set(giver - passed).at[2:2 + 2 * couples:2].set(taker + passed)
    return tallies[jax.random.permutation(jax.random.fold_in(key, 2), number_of)]


def gaussian(rng, shape, deviation, reach, pieces=(), held_as=jnp.bfloat16):
    array = jax.random.normal(rng, shape, jnp.float32) * deviation
    if len(pieces) > 0:
        array = block_levels(rng, shape, pieces, -0.22, 0.18) * array
    return jnp.clip(array, min=-reach, max=reach).astype(held_as)


def setup_inputs(seed: int = 0) -> dict:
    key_of = jax.random.split(jax.random.key(seed), 9)
    return {
        "qkvu": gaussian(key_of[0], (TOKENS, 4 * D), 1.0, 6.0, ((0, 32),)),
        "w_out": gaussian(key_of[1], (D, D), D ** -0.5, 0.1875),
        "head_coef": gaussian(key_of[2], (TOKENS, NEGS), NEGS ** -0.5, 1.0, ((0, 32),)),
        "item_table": gaussian(key_of[3], (ITEMS, D), 1.0, 6.0, ((0, 8),)),
        "neg_ids": plant(jax.random.randint(key_of[4], (NEGS,), 0, ITEMS_DEV), jax.random.fold_in(key_of[4], 1), 0, ITEMS_DEV - 1).astype(jnp.int32),
        "send_order": jax.vmap(lambda own: jax.random.permutation(own, TILE))(jax.random.split(key_of[5], (N_DP * N_SEQ))).reshape((N_DP * N_SEQ, TILE)).astype(jnp.int32),
        "recv_order": jax.vmap(lambda own: jax.random.permutation(own, TILE))(jax.random.split(key_of[6], (N_DP * N_SEQ))).reshape((N_DP * N_SEQ, TILE)).astype(jnp.int32),
        "tile_len": jax.vmap(lambda own: ragged_sizes(own, N_SEQ, N_SEQ * TILE // 3, TILE, 2))(jax.random.split(key_of[7], N_DP)).reshape((N_DP, N_SEQ)).astype(jnp.int32),
    }


eps = 1e-05

def silu_grad(values):
    sigmoid_val = jax.nn.sigmoid(values)
    return sigmoid_val * (1.0 + values * (1.0 - sigmoid_val))

def split_rows(rows_in, width):
    count = rows_in.shape[0]
    head_dim = width // HEADS
    u_part = rows_in[:, :width].astype(jnp.float32)
    value_rows = rows_in[:, width:2 * width].astype(jnp.float32).reshape(count, HEADS, head_dim)
    query_rows = rows_in[:, 2 * width:3 * width].astype(jnp.float32).reshape(count, HEADS, head_dim)
    key_rows = rows_in[:, 3 * width:].astype(jnp.float32).reshape(count, HEADS, head_dim)
    return (u_part, value_rows, query_rows, key_rows)

def pair_mask(count, len_p, len_q, causal):
    positions = jnp.arange(count, dtype=jnp.int32)
    live = (positions[:, None] < len_p) & (positions[None, :] < len_q)
    if causal:
        live = live & (positions[None, :] <= positions[:, None])
    return jnp.where(live, 1.0, 0.0).astype(jnp.float32)

def history_step(bal, coef, lens, neg_rows, w_out):
    tiles = bal.shape[0]
    count = bal.shape[1]
    width = w_out.shape[0]
    head_dim = width // HEADS
    score_scale = 1.0 / math.sqrt(head_dim)
    positions = jnp.arange(count, dtype=jnp.int32)
    split = [split_rows(bal[i], width) for i in range(tiles)]
    sampled = jnp.zeros((width, coef.shape[2]), jnp.float32)
    key_grads = [jnp.zeros((count, HEADS, head_dim), jnp.float32) for i in range(tiles)]
    value_grads = [jnp.zeros((count, HEADS, head_dim), jnp.float32) for i in range(tiles)]
    outputs = []
    u_grads = []
    query_grads = []
    for i in range(tiles):
        u_part, value_i, query_i, key_i = split[i]
        window = list(range(max(0, i - SPAN + 1), i + 1))
        attended = jnp.zeros((count, HEADS, head_dim), jnp.float32)
        saved = []
        for j in window:
            mask = pair_mask(count, lens[i], lens[j], j == i)
            scores = jnp.einsum('phd,qhd->hpq', query_i, split[j][3]) * score_scale
            weights = (jax.nn.silu(scores) * mask[None] / count).astype(jnp.bfloat16)
            attended = attended + jnp.einsum('hpq,qhd->phd', weights.astype(jnp.float32), split[j][1])
            saved.append((j, mask, scores, weights))
        attended = attended.reshape(count, width)
        row_mean = lax.optimization_barrier(jnp.mean(attended, axis=1, keepdims=True))
        centered = attended - row_mean
        variance = lax.optimization_barrier(jnp.mean(centered * centered, axis=1, keepdims=True))
        inv_std = lax.rsqrt(variance + eps)
        normed = centered * inv_std
        mixed_rows = (normed * u_part).astype(jnp.bfloat16)
        outputs.append(jnp.dot(mixed_rows, w_out, preferred_element_type=jnp.float32).astype(jnp.bfloat16))
        live_col = jnp.where(positions < lens[i], 1.0, 0.0).astype(jnp.float32)[:, None]
        coef_live = (coef[i] * live_col).astype(jnp.bfloat16)
        head_grad = jnp.dot(coef_live, neg_rows, preferred_element_type=jnp.float32).astype(jnp.bfloat16)
        sampled = sampled + lax.dot_general(mixed_rows, coef_live, (((0,), (0,)), ((), ())), preferred_element_type=jnp.float32)
        d_mixed = lax.dot_general(head_grad, w_out, (((1,), (1,)), ((), ())), preferred_element_type=jnp.float32)
        u_grads.append(d_mixed * normed)
        d_normed = d_mixed * u_part
        d_att = (d_normed - lax.optimization_barrier(jnp.mean(d_normed, axis=1, keepdims=True)) - normed * lax.optimization_barrier(jnp.mean(d_normed * normed, axis=1, keepdims=True))) * inv_std
        d_att = d_att.astype(jnp.bfloat16).astype(jnp.float32).reshape(count, HEADS, head_dim)
        d_query = jnp.zeros((count, HEADS, head_dim), jnp.float32)
        for j, mask, scores, weights in saved:
            d_weights = jnp.einsum('phd,qhd->hpq', d_att, split[j][1])
            d_scores = (d_weights * mask[None] / count * silu_grad(scores) * score_scale).astype(jnp.bfloat16).astype(jnp.float32)
            d_query = d_query + jnp.einsum('hpq,qhd->phd', d_scores, split[j][3])
            part_keys = jnp.einsum('hpq,phd->qhd', d_scores, query_i)
            part_values = jnp.einsum('hpq,phd->qhd', weights.astype(jnp.float32), d_att)
            if j < i:
                part_keys = part_keys.astype(jnp.bfloat16).astype(jnp.float32)
                part_values = part_values.astype(jnp.bfloat16).astype(jnp.float32)
            key_grads[j] = key_grads[j] + part_keys
            value_grads[j] = value_grads[j] + part_values
        query_grads.append(d_query.reshape(count, width))
    grads = []
    for i in range(tiles):
        grads.append(jnp.concatenate([u_grads[i], value_grads[i].reshape(count, width), query_grads[i], key_grads[i].reshape(count, width)], axis=1).astype(jnp.bfloat16))
    return (jnp.stack(outputs), jnp.stack(grads), sampled)

def place_rows(values, indices):
    return jnp.zeros_like(values).at[indices].set(values)

def reference(qkvu, w_out, head_coef, item_table, neg_ids, send_order, recv_order, tile_len):
    groups = N_DP
    peer_count = N_SEQ
    slot_cap = TILE // N_SEQ
    full_width = 4 * D
    home_rows = qkvu.reshape(groups, peer_count, TILE, full_width)
    send_list = send_order.reshape(groups, peer_count, TILE).astype(jnp.int32)
    recv_list = recv_order.reshape(groups, peer_count, TILE).astype(jnp.int32)
    sent_rows = jnp.take_along_axis(home_rows, send_list[..., None], axis=2)
    sent_rows = sent_rows.reshape(groups, peer_count, peer_count, slot_cap, full_width)
    received = jnp.swapaxes(sent_rows, 1, 2).reshape(groups, peer_count, TILE, full_width)
    balanced = jnp.take_along_axis(received, recv_list[..., None], axis=2)
    table_shards = item_table.reshape(peer_count, ITEMS_DEV, D)
    id_shards = neg_ids.reshape(peer_count, NEG).astype(jnp.int32)
    neg_rows = jnp.take_along_axis(table_shards, id_shards[..., None], axis=1).reshape(peer_count * NEG, D)
    device_count = groups * peer_count
    hist_coef = head_coef.reshape(groups, peer_count, TILE, NEG * peer_count)
    hist_len = tile_len.reshape(groups, peer_count).astype(jnp.int32)

    def per_history(running_sum, inputs):
        bal_rows, coef_rows, lens = inputs
        outs, grads, sampled = history_step(bal_rows, coef_rows, lens, neg_rows, w_out)
        return (running_sum + sampled, (outs, grads))
    sampled_total, (outputs, grads_bal) = lax.scan(per_history, jnp.zeros((D, NEG * peer_count), jnp.float32), (balanced, hist_coef, hist_len))
    d_w_out = jnp.dot(sampled_total, neg_rows.astype(jnp.float32), precision=lax.Precision.HIGHEST)
    grads_bal = grads_bal.reshape(device_count, TILE, full_width)
    slot_grads = jax.vmap(place_rows)(grads_bal, recv_list.reshape(device_count, TILE))
    slot_grads = slot_grads.reshape(groups, peer_count, peer_count, slot_cap, full_width)
    slot_grads = jnp.swapaxes(slot_grads, 1, 2).reshape(device_count, TILE, full_width)
    d_home = jax.vmap(place_rows)(slot_grads, send_list.reshape(device_count, TILE))
    return (outputs.reshape(TILE * device_count, D), d_home.reshape(TILE * device_count, full_width), d_w_out)
```

```python
import functools
import math

import jax
import jax.numpy as jnp
from jax import lax
from jax.experimental import pallas as pl
from jax.experimental.pallas import tpu as pltpu
from jax.sharding import PartitionSpec as P

HEADS = 8
SPAN = 3
PARTS = 4
SLOTS = 64
IDX_ROWS = 16


eps = 1e-05

VMEM = pl.BlockSpec(memory_space=pltpu.VMEM)
SMEM = pl.BlockSpec(memory_space=pltpu.SMEM)
F32 = jnp.float32
BF16 = jnp.bfloat16


def shifted(block, axis, distance):
    devices = range(lax.axis_size(axis))
    route = [(i - distance, i) for i in devices if i - distance in devices]
    return lax.ppermute(block, axis, route)


def silu_grad(values):
    sigmoid_val = jax.nn.sigmoid(values)
    return sigmoid_val * (1.0 + values * (1.0 - sigmoid_val))


def pair_mask(count, len_p, len_q, allowed, causal):
    positions = jnp.arange(count, dtype=jnp.int32)
    live = (positions[:, None] < len_p) & (positions[None, :] < len_q) & allowed
    if causal:
        live = live & (positions[None, :] <= positions[:, None])
    return jnp.where(live, 1.0, 0.0).astype(jnp.float32)


def head_major(flat, count, head_dim):
    return flat.reshape(count, HEADS, head_dim).transpose(1, 0, 2)


def row_major(heads_first, count, width):
    return heads_first.transpose(1, 0, 2).reshape(count, width)


def tile_plan(qkvu, w_out, head_coef, item_table, neg_ids, send_order, recv_order, tile_len):
    row_count = qkvu.shape[0]
    model_width = w_out.shape[0]
    head_dim = model_width // HEADS
    score_scale = 1.0 / math.sqrt(head_dim)
    send_list = send_order[0]
    recv_list = recv_order[0]
    own_index = lax.axis_index("seq")
    lengths_row = tile_len[0]
    own_len = jnp.take(lengths_row, own_index)
    outgoing = jnp.take(qkvu, send_list, axis=0)
    received = lax.all_to_all(outgoing, "seq", split_axis=0, concat_axis=0, tiled=True)
    balanced = jnp.take(received, recv_list, axis=0)
    neg_all = lax.all_gather(jnp.take(item_table, neg_ids, axis=0), "seq", axis=0, tiled=True)
    u_part = balanced[:, :model_width].astype(jnp.float32)
    value_heads = head_major(balanced[:, model_width : 2 * model_width], row_count, head_dim)
    query_heads = head_major(balanced[:, 2 * model_width : 3 * model_width], row_count, head_dim)
    key_heads = head_major(balanced[:, 3 * model_width :], row_count, head_dim)
    lagged = []
    carried = (value_heads, key_heads)
    for lag in range(1, SPAN):
        carried = shifted((carried[0], carried[1]), "seq", 1)
        lagged.append(carried)
    value_list = [value_heads]
    key_list = [key_heads]
    mask_list = [pair_mask(row_count, own_len, own_len, True, True)]
    for lag in range(1, SPAN):
        earlier_len = jnp.take(lengths_row, jnp.maximum(own_index - lag, 0))
        value_list.append(lagged[lag - 1][0])
        key_list.append(lagged[lag - 1][1])
        mask_list.append(pair_mask(row_count, own_len, earlier_len, own_index >= lag, False))
    values_all = jnp.concatenate(value_list, axis=1)
    keys_all = jnp.concatenate(key_list, axis=1)
    mask_all = jnp.concatenate(mask_list, axis=1)
    scores = (
        jnp.einsum("hpd,hqd->hpq", query_heads, keys_all, preferred_element_type=jnp.float32)
        * score_scale
    )
    weights = (jax.nn.silu(scores) * mask_all[None] / row_count).astype(jnp.bfloat16)
    attended_heads = jnp.einsum(
        "hpq,hqd->hpd", weights, values_all, preferred_element_type=jnp.float32
    )
    attended = row_major(attended_heads, row_count, model_width)
    row_mean = jnp.mean(attended, axis=1, keepdims=True)
    centered = attended - row_mean
    variance = jnp.mean(centered * centered, axis=1, keepdims=True)
    inv_std = lax.rsqrt(variance + eps)
    normed = centered * inv_std
    mixed_rows = (normed * u_part).astype(jnp.bfloat16)
    layer_out = jnp.dot(mixed_rows, w_out, preferred_element_type=jnp.float32).astype(jnp.bfloat16)
    positions = jnp.arange(row_count, dtype=jnp.int32)
    live_col = jnp.where(positions < own_len, 1.0, 0.0).astype(jnp.float32)[:, None]
    coef_live = (head_coef * live_col).astype(jnp.bfloat16)
    head_grad = jnp.dot(coef_live, neg_all, preferred_element_type=jnp.float32).astype(jnp.bfloat16)
    d_mixed = lax.dot_general(
        head_grad, w_out, (((1,), (1,)), ((), ())), preferred_element_type=jnp.float32
    )
    d_u_part = d_mixed * normed
    d_normed = d_mixed * u_part
    d_att = (
        d_normed
        - jnp.mean(d_normed, axis=1, keepdims=True)
        - normed * jnp.mean(d_normed * normed, axis=1, keepdims=True)
    ) * inv_std
    d_att_heads = head_major(d_att.astype(jnp.bfloat16), row_count, head_dim)
    d_weights = jnp.einsum(
        "hpd,hqd->hpq", d_att_heads, values_all, preferred_element_type=jnp.float32
    )
    d_scores = (d_weights * mask_all[None] / row_count * silu_grad(scores) * score_scale).astype(
        jnp.bfloat16
    )
    d_query = jnp.einsum("hpq,hqd->hpd", d_scores, keys_all, preferred_element_type=jnp.float32)
    part_keys = jnp.einsum(
        "hpq,hpd->hqd", d_scores, query_heads, preferred_element_type=jnp.float32
    )
    part_values = jnp.einsum(
        "hpq,hpd->hqd", weights, d_att_heads, preferred_element_type=jnp.float32
    )
    key_grad = part_keys[:, :row_count]
    value_grad = part_values[:, :row_count]
    for lag in range(1, SPAN):
        block_keys = part_keys[:, lag * row_count : (lag + 1) * row_count].astype(jnp.bfloat16)
        block_values = part_values[:, lag * row_count : (lag + 1) * row_count].astype(jnp.bfloat16)
        back_values, back_keys = shifted((block_values, block_keys), "seq", -lag)
        key_grad = key_grad + back_keys.astype(jnp.float32)
        value_grad = value_grad + back_values.astype(jnp.float32)
    tile_grads = jnp.concatenate(
        [
            d_u_part,
            row_major(value_grad, row_count, model_width),
            row_major(d_query, row_count, model_width),
            row_major(key_grad, row_count, model_width),
        ],
        axis=1,
    ).astype(jnp.bfloat16)
    slot_grads = jnp.zeros_like(tile_grads).at[recv_list].set(tile_grads)
    returned = lax.all_to_all(slot_grads, "seq", split_axis=0, concat_axis=0, tiled=True)
    d_home = jnp.zeros_like(returned).at[send_list].set(returned)
    coef_sums = lax.psum_scatter(
        lax.dot_general(
            mixed_rows, coef_live, (((0,), (0,)), ((), ())), preferred_element_type=jnp.float32
        ),
        "seq",
        scatter_dimension=0,
        tiled=True,
    )
    row_grad = jnp.dot(coef_sums, neg_all.astype(jnp.float32), precision=lax.Precision.HIGHEST)
    d_w_out = lax.psum_scatter(
        row_grad.astype(jnp.bfloat16), "dp", scatter_dimension=1, tiled=True
    ).astype(jnp.float32)
    return (layer_out, d_home, d_w_out)


def dot(a, b, dims=((1,), (0,))):
    return lax.dot_general(a, b, (dims, ((), ())), preferred_element_type=F32)


def iota(shape, dim):
    return lax.broadcasted_iota(jnp.int32, shape, dim)


def starts_of(len_ref, count):
    starts = [jnp.int32(0)]
    for t in range(count):
        starts.append(starts[-1] + len_ref[t])
    return starts


def tile_of(position, starts):
    tile = jnp.zeros(position.shape, jnp.int32)
    for start in starts[1:-1]:
        tile = tile + jnp.where(position >= start, 1, 0)
    return tile


def one_hot(condition):
    return jnp.where(condition, 1.0, 0.0).astype(BF16)


def index_kernel(sizes, me_ref, len_ref, gathered, w_rows, place, rank, most, coef_c, d_mixed, negatives, neg_rows):
    n, rows, live_cap, negs, per = sizes
    cell = rows // n
    me = me_ref[0]
    starts = starts_of(len_ref, n)
    blocks = [gathered[me ^ s].astype(F32) for s in range(n)]
    order = jnp.concatenate([b[0:8] for b in blocks], axis=0)
    order = jnp.concatenate([order, jnp.zeros((rows - 8 * n, rows), F32)], axis=0)
    order_t = jnp.transpose(order)
    lane = iota((rows, rows), 1)
    sub = iota((rows, rows), 0)
    slot_rows = []
    for t in range(n):
        recv_col = order_t[:, 8 * t : 8 * t + 1].astype(jnp.int32)
        target = jnp.where(sub < len_ref[t], sub + starts[t] + 1, 0)
        hit = jnp.where(recv_col == lane, target, 0)
        slot_rows.append(jnp.sum(hit.astype(F32), axis=0, keepdims=True))
    slots = jnp.concatenate(slot_rows + [jnp.zeros((rows - n, rows), F32)], axis=0)
    slots_t = jnp.transpose(slots)
    home_rows = []
    for s in range(n):
        send_col = order_t[:, 8 * s + 1 : 8 * s + 2].astype(jnp.int32)
        target = jnp.concatenate([jnp.broadcast_to(slots_t[s * cell : (s + 1) * cell, t : t + 1], (cell, rows)) for t in range(n)], axis=0)
        home_rows.append(jnp.sum(jnp.where(send_col == lane, target, 0.0), axis=0, keepdims=True))
    home = jnp.concatenate(home_rows, axis=0)
    place[...] = home - 1.0
    live = home > 0.5
    before = dot(one_hot(live), one_hot(sub < lane))
    rank[...] = jnp.where(live, before, -1.0)
    most[...] = jnp.broadcast_to(jnp.max(jnp.sum(jnp.where(live, 1.0, 0.0), axis=1, keepdims=True)), most.shape)
    total = jnp.zeros((negs, live_cap), F32)
    wide = iota((live_cap, rows), 0)
    pos = iota((live_cap, rows), 1)
    for t in range(n):
        pick = one_hot((wide == pos + starts[t]) & (pos < len_ref[t]))
        total = total + dot(blocks[t][IDX_ROWS : IDX_ROWS + negs].astype(BF16), pick, ((1,), (1,)))
    coef_t = total.astype(BF16)
    coef_c[...] = coef_t
    base = IDX_ROWS + negs
    width = neg_rows.shape[1]
    for s in range(n):
        for b in range(width // rows):
            neg_rows[per * s : per * (s + 1), b * rows : (b + 1) * rows] = blocks[s][base + per * b : base + per * (b + 1)]
    neg = neg_rows[...].astype(BF16)
    negatives[...] = neg
    head_grad = dot(coef_t, neg, ((0,), (0,))).astype(BF16)
    d_mixed[...] = dot(head_grad, w_rows[...], ((1,), (1,)))


def pair_live(live_cap, starts):
    row = iota((live_cap, 1), 0)
    col = iota((1, live_cap), 1)
    return (col <= row) & (tile_of(col, starts) > tile_of(row, starts) - SPAN) & (row < starts[-1])


def forward_kernel(sizes, len_ref, received, place, d_mixed, compact, weights, att, stats):
    n, rows, live_cap = sizes
    head_dim = att.shape[1]
    starts = starts_of(len_ref, n)
    wide = iota((live_cap, rows), 0)
    home = place[...].astype(jnp.int32)
    pick = jnp.concatenate([one_hot(wide == home[s : s + 1]) for s in range(n)], axis=1)
    both = dot(pick, received[...].reshape(n * rows, PARTS * head_dim)).astype(BF16)
    compact[...] = both
    u, v, q, k = (both[:, i * head_dim : (i + 1) * head_dim] for i in range(PARTS))
    scores = dot(q, k, ((1,), (1,))) * (1.0 / math.sqrt(head_dim))
    sig = jax.nn.sigmoid(scores)
    w = jnp.where(pair_live(live_cap, starts), scores * sig * (1.0 / rows), 0.0).astype(BF16)
    weights[...] = w
    a = dot(w, v)
    att[...] = a
    dn = d_mixed[...] * u.astype(F32)
    mean = jnp.sum(a, axis=1, keepdims=True) * (1.0 / head_dim)
    cen = a - mean
    lane = iota((live_cap, 128), 1)
    cols = jnp.where(lane == 0, mean, 0.0)
    cols = jnp.where(lane == 1, jnp.sum(cen * cen, axis=1, keepdims=True), cols)
    cols = jnp.where(lane == 2, jnp.sum(dn, axis=1, keepdims=True), cols)
    cols = jnp.where(lane == 3, jnp.sum(dn * cen, axis=1, keepdims=True), cols)
    stats[...] = jnp.transpose(cols)[0:8]


def merge_stats(a, b, count):
    gap = b[0] - a[0]
    return (
        (a[0] + b[0]) * 0.5,
        a[1] + b[1] + gap * gap * (0.5 * count),
        a[2] + b[2],
        a[3] + b[3] + (b[2] - a[2]) * gap * 0.5,
    )


def backward_kernel(sizes, len_ref, compact, weights, att, d_mixed, st0, st1, st2, st3, place, rank, coef_c, message, grads, d_sums):
    n, rows, live_cap, slots = sizes
    head_dim = att.shape[1]
    width = head_dim * n
    starts = starts_of(len_ref, n)
    quad = [[st[i : i + 1] for i in range(4)] for st in (st0, st1, st2, st3)]
    ab = merge_stats(quad[0], quad[1], 2 * head_dim)
    cd = merge_stats(quad[2], quad[3], 2 * head_dim)
    mean, m2, s_dn, s_dna = merge_stats(ab, cd, 4 * head_dim)
    inv = lax.rsqrt(m2 * (1.0 / width) + eps)
    table = jnp.concatenate([mean, inv, s_dn * (1.0 / width), s_dna * inv * (1.0 / width), jnp.zeros((124, live_cap), F32)], axis=0)
    table = jnp.transpose(table)
    mean, inv, mean_dn, mean_dnn = (table[:, i : i + 1] for i in range(4))
    both = compact[...]
    u, v, q, k = (both[:, i * head_dim : (i + 1) * head_dim] for i in range(PARTS))
    u = u.astype(F32)
    dm = d_mixed[...]
    normed = (att[...] - mean) * inv
    mixed = (normed * u).astype(BF16)
    dn = dm * u
    d_att = ((dn - mean_dn - normed * mean_dnn) * inv).astype(BF16)
    scale = 1.0 / math.sqrt(head_dim)
    scores = dot(q, k, ((1,), (1,))) * scale
    sig = jax.nn.sigmoid(scores)
    slope = sig * (1.0 + scores * (1.0 - sig)) * (scale / rows)
    ds = jnp.where(pair_live(live_cap, starts), dot(d_att, v, ((1,), (1,))) * slope, 0.0).astype(BF16)
    grad = jnp.concatenate(
        [dm * normed, dot(weights[...], d_att, ((0,), (0,))), dot(ds, k), dot(ds, q, ((0,), (0,)))], axis=1
    ).astype(BF16)
    grads[...] = grad
    d_sums[...] = dot(coef_c[...], mixed)
    fill_slots(n, rows, slots, 0, place, rank, grad, message)
    quarter = rows // PARTS
    col = iota((rows, live_cap), 1)
    row = iota((rows, live_cap), 0)
    for t in range(n):
        tile = dot(one_hot((col == row + starts[t]) & (row < len_ref[t])), mixed).astype(BF16)
        for b in range(PARTS):
            message[t, slots : slots + quarter, b * head_dim : (b + 1) * head_dim] = tile[b * quarter : (b + 1) * quarter]


def fill_slots(n, rows, slots, first, place, rank, grad, message):
    live_cap = grad.shape[0]
    slot = iota((slots, rows), 0) + first
    col = iota((slots, live_cap), 1)
    for s in range(n):
        hit = rank[s : s + 1].astype(jnp.int32) == slot
        source = jnp.sum(jnp.where(hit, place[s : s + 1] + 1.0, 0.0), axis=1, keepdims=True) - 1.0
        message[s, 0:slots] = dot(one_hot(source.astype(jnp.int32) == col), grad).astype(BF16)


def rest_kernel(sizes, place, rank, grad, message):
    n, rows, slots = sizes
    fill_slots(n, rows, slots, slots, place, rank, grad[...], message)


def finish_kernel(sizes, extra, me_ref, *refs):
    n, rows, slots = sizes
    rank, w_out, message = refs[:3]
    d_home, layer_out = refs[-2:]
    head_dim = message.shape[2] // PARTS
    width = head_dim * n
    quarter = rows // PARTS
    own = rank[pl.ds(me_ref[0], 1), :].astype(jnp.int32)
    total = slots * (1 + extra)
    pick = one_hot(own == iota((total, rows), 0))
    mixed = []
    for h in range(n):
        block = message[h, 0:slots]
        if extra:
            block = jnp.concatenate([block, refs[3][h]], axis=0)
        full = dot(pick, block, ((0,), (0,))).astype(BF16)
        for i in range(PARTS):
            d_home[:, i * width + h * head_dim : i * width + (h + 1) * head_dim] = full[:, i * head_dim : (i + 1) * head_dim]
        mixed.append(
            jnp.concatenate([message[h, slots : slots + quarter, b * head_dim : (b + 1) * head_dim] for b in range(PARTS)], axis=0)
        )
    layer_out[...] = dot(jnp.concatenate(mixed, axis=1), w_out[...]).astype(BF16)


def kernel_call(body, shapes, specs, scratch=(), cost=None):
    return pl.pallas_call(
        body,
        out_shape=shapes,
        in_specs=specs,
        out_specs=jax.tree.map(lambda _: VMEM, shapes),
        scratch_shapes=scratch,
        compiler_params=pltpu.CompilerParams(vmem_limit_bytes=40 * 1024 * 1024),
        cost_estimate=cost,
    )


def swap(block, axis, distance):
    return lax.ppermute(block, axis, [(i, i ^ distance) for i in range(lax.axis_size(axis))])


def head_plan(qkvu, w_out, head_coef, item_table, neg_ids, send_order, recv_order, tile_len):
    n = lax.axis_size("seq")
    groups = lax.axis_size("dp")
    rows = qkvu.shape[0]
    width = w_out.shape[0]
    head_dim = width // HEADS
    negs = head_coef.shape[1]
    per = neg_ids.shape[0]
    live_cap = -(-(n * rows // 3) // 128) * 128
    sds = jax.ShapeDtypeStruct
    me = lax.axis_index("seq")
    me_arr = me.astype(jnp.int32).reshape(1)
    lens = tile_len[0]
    outgoing = qkvu.reshape(rows, PARTS, n, head_dim).transpose(2, 0, 1, 3).reshape(n, rows, PARTS * head_dim)
    received = lax.all_to_all(outgoing, "seq", split_axis=0, concat_axis=0, tiled=True)

    negatives = jnp.take(item_table, neg_ids, axis=0)
    small = jnp.concatenate(
        [
            recv_order.astype(BF16),
            send_order.astype(BF16),
            jnp.zeros((IDX_ROWS - 2, rows), BF16),
            head_coef.T,
            negatives.reshape(per, width // rows, rows).transpose(1, 0, 2).reshape(-1, rows),
        ],
        axis=0,
    )[None]
    distance = 1
    while distance < n:
        small = jnp.concatenate([small, swap(small, "seq", distance)], axis=0)
        distance *= 2
    w_rows = lax.dynamic_slice_in_dim(w_out, me * head_dim, head_dim, axis=0)
    place, rank, most, coef_c, d_mixed, neg_all = kernel_call(
        functools.partial(index_kernel, (n, rows, live_cap, negs, per)),
        (
            sds((n, rows), F32),
            sds((n, rows), F32),
            sds((8, 128), F32),
            sds((negs, live_cap), BF16),
            sds((live_cap, head_dim), F32),
            sds((negs, width), BF16),
        ),
        [SMEM, SMEM, VMEM, VMEM],
        [pltpu.VMEM((negs, width), F32)],
    )(me_arr, lens, small, w_rows)
    distance = 1
    while distance < groups:
        most = jnp.maximum(most, swap(most, "dp", distance))
        distance *= 2

    compact, weights, att, stats = kernel_call(
        functools.partial(forward_kernel, (n, rows, live_cap)),
        (
            sds((live_cap, PARTS * head_dim), BF16),
            sds((live_cap, live_cap), BF16),
            sds((live_cap, head_dim), F32),
            sds((8, live_cap), F32),
        ),
        [SMEM, VMEM, VMEM, VMEM],
    )(lens, received, place, d_mixed)
    other = swap(stats, "seq", 1)
    first = jnp.where(me % 2 == 0, 1.0, 0.0)
    low, high = (stats, other)
    gap = high[0] - low[0]
    paired = jnp.stack(
        [
            (low[0] + high[0]) * 0.5,
            low[1] + high[1] + gap * gap * (0.5 * head_dim),
            low[2] + high[2],
            low[3] + high[3] + (high[2] - low[2]) * gap * 0.5,
        ]
        + [jnp.zeros_like(gap)] * 4
    )
    far = [swap(paired, "seq", d) for d in (2, 4, 6)]
    message, grads, d_sums = kernel_call(
        functools.partial(backward_kernel, (n, rows, live_cap, SLOTS)),
        (
            sds((n, SLOTS + rows // PARTS, PARTS * head_dim), BF16),
            sds((live_cap, PARTS * head_dim), BF16),
            sds((negs, head_dim), F32),
        ),
        [SMEM] + [VMEM] * 11,
    )(lens, compact, weights, att, d_mixed, paired, *far, place, rank, coef_c)
    returned = lax.all_to_all(message, "seq", split_axis=0, concat_axis=0, tiled=True)
    total = d_sums
    for d in range(1, groups):
        total = total + swap(d_sums, "dp", d)
    neg_cols = lax.dynamic_slice_in_dim(neg_all, lax.axis_index("dp") * (width // groups), width // groups, axis=1)
    d_w_out = lax.dot_general(
        total, neg_cols.astype(F32), (((0,), (0,)), ((), ())), precision=lax.Precision.HIGHEST
    )

    out_shapes = (sds((rows, PARTS * width), BF16), sds((rows, width), BF16))

    def finish_one(message, place, rank, grads):
        return kernel_call(functools.partial(finish_kernel, (n, rows, SLOTS), 0), out_shapes, [SMEM] + [VMEM] * 3)(
            me_arr, rank, w_out, message
        )

    def finish_two(message, place, rank, grads):
        rest = kernel_call(
            functools.partial(rest_kernel, (n, rows, SLOTS)), sds((n, SLOTS, PARTS * head_dim), BF16), [VMEM] * 3
        )(place, rank, grads)
        rest = lax.all_to_all(rest, "seq", split_axis=0, concat_axis=0, tiled=True)
        return kernel_call(functools.partial(finish_kernel, (n, rows, SLOTS), 1), out_shapes, [SMEM] + [VMEM] * 4)(
            me_arr, rank, w_out, message, rest
        )

    d_home, layer_out = lax.cond(most[0, 0] > SLOTS, finish_two, finish_one, returned, place, rank, grads)
    return (layer_out, d_home, d_w_out)


def solution(mesh):
    placed = (
        P(("dp", "seq"), None),
        P(),
        P(("dp", "seq"), None),
        P("seq", None),
        P("seq"),
        P(("dp", "seq"), None),
        P(("dp", "seq"), None),
        P("dp", None),
    )
    return jax.shard_map(
        head_plan if mesh.shape["seq"] == HEADS else tile_plan,
        mesh=mesh,
        in_specs=placed,
        out_specs=(P(("dp", "seq"), None), P(("dp", "seq"), None), P("seq", "dp")),
        check_vma=False,
    )
```

```python
import functools
import math

import jax
import jax.numpy as jnp
from jax import lax
from jax.experimental import pallas as pl
from jax.experimental.pallas import tpu as pltpu
from jax.sharding import PartitionSpec as P

HEADS = 8
SPAN = 3
PARTS = 4
SLOTS = 64
IDX_ROWS = 16
LIMIT = 60 * 1024 * 1024


eps = 1e-05

VMEM = pl.BlockSpec(memory_space=pltpu.VMEM)
SMEM = pl.BlockSpec(memory_space=pltpu.SMEM)
ANY = pl.BlockSpec(memory_space=pl.ANY)
F32 = jnp.float32
BF16 = jnp.bfloat16


def shifted(block, axis, distance):
    devices = range(lax.axis_size(axis))
    route = [(i - distance, i) for i in devices if i - distance in devices]
    return lax.ppermute(block, axis, route)


def silu_grad(values):
    sigmoid_val = jax.nn.sigmoid(values)
    return sigmoid_val * (1.0 + values * (1.0 - sigmoid_val))


def pair_mask(count, len_p, len_q, allowed, causal):
    positions = jnp.arange(count, dtype=jnp.int32)
    live = (positions[:, None] < len_p) & (positions[None, :] < len_q) & allowed
    if causal:
        live = live & (positions[None, :] <= positions[:, None])
    return jnp.where(live, 1.0, 0.0).astype(jnp.float32)


def head_major(flat, count, head_dim):
    return flat.reshape(count, HEADS, head_dim).transpose(1, 0, 2)


def row_major(heads_first, count, width):
    return heads_first.transpose(1, 0, 2).reshape(count, width)


def tile_plan(qkvu, w_out, head_coef, item_table, neg_ids, send_order, recv_order, tile_len):
    row_count = qkvu.shape[0]
    model_width = w_out.shape[0]
    head_dim = model_width // HEADS
    score_scale = 1.0 / math.sqrt(head_dim)
    send_list = send_order[0]
    recv_list = recv_order[0]
    own_index = lax.axis_index("seq")
    lengths_row = tile_len[0]
    own_len = jnp.take(lengths_row, own_index)
    outgoing = jnp.take(qkvu, send_list, axis=0)
    received = lax.all_to_all(outgoing, "seq", split_axis=0, concat_axis=0, tiled=True)
    balanced = jnp.take(received, recv_list, axis=0)
    neg_all = lax.all_gather(jnp.take(item_table, neg_ids, axis=0), "seq", axis=0, tiled=True)
    u_part = balanced[:, :model_width].astype(jnp.float32)
    value_heads = head_major(balanced[:, model_width : 2 * model_width], row_count, head_dim)
    query_heads = head_major(balanced[:, 2 * model_width : 3 * model_width], row_count, head_dim)
    key_heads = head_major(balanced[:, 3 * model_width :], row_count, head_dim)
    lagged = []
    carried = (value_heads, key_heads)
    for lag in range(1, SPAN):
        carried = shifted((carried[0], carried[1]), "seq", 1)
        lagged.append(carried)
    value_list = [value_heads]
    key_list = [key_heads]
    mask_list = [pair_mask(row_count, own_len, own_len, True, True)]
    for lag in range(1, SPAN):
        earlier_len = jnp.take(lengths_row, jnp.maximum(own_index - lag, 0))
        value_list.append(lagged[lag - 1][0])
        key_list.append(lagged[lag - 1][1])
        mask_list.append(pair_mask(row_count, own_len, earlier_len, own_index >= lag, False))
    values_all = jnp.concatenate(value_list, axis=1)
    keys_all = jnp.concatenate(key_list, axis=1)
    mask_all = jnp.concatenate(mask_list, axis=1)
    scores = (
        jnp.einsum("hpd,hqd->hpq", query_heads, keys_all, preferred_element_type=jnp.float32)
        * score_scale
    )
    weights = (jax.nn.silu(scores) * mask_all[None] / row_count).astype(jnp.bfloat16)
    attended_heads = jnp.einsum(
        "hpq,hqd->hpd", weights, values_all, preferred_element_type=jnp.float32
    )
    attended = row_major(attended_heads, row_count, model_width)
    row_mean = jnp.mean(attended, axis=1, keepdims=True)
    centered = attended - row_mean
    variance = jnp.mean(centered * centered, axis=1, keepdims=True)
    inv_std = lax.rsqrt(variance + eps)
    normed = centered * inv_std
    mixed_rows = (normed * u_part).astype(jnp.bfloat16)
    layer_out = jnp.dot(mixed_rows, w_out, preferred_element_type=jnp.float32).astype(jnp.bfloat16)
    positions = jnp.arange(row_count, dtype=jnp.int32)
    live_col = jnp.where(positions < own_len, 1.0, 0.0).astype(jnp.float32)[:, None]
    coef_live = (head_coef * live_col).astype(jnp.bfloat16)
    head_grad = jnp.dot(coef_live, neg_all, preferred_element_type=jnp.float32).astype(jnp.bfloat16)
    d_mixed = lax.dot_general(
        head_grad, w_out, (((1,), (1,)), ((), ())), preferred_element_type=jnp.float32
    )
    d_u_part = d_mixed * normed
    d_normed = d_mixed * u_part
    d_att = (
        d_normed
        - jnp.mean(d_normed, axis=1, keepdims=True)
        - normed * jnp.mean(d_normed * normed, axis=1, keepdims=True)
    ) * inv_std
    d_att_heads = head_major(d_att.astype(jnp.bfloat16), row_count, head_dim)
    d_weights = jnp.einsum(
        "hpd,hqd->hpq", d_att_heads, values_all, preferred_element_type=jnp.float32
    )
    d_scores = (d_weights * mask_all[None] / row_count * silu_grad(scores) * score_scale).astype(
        jnp.bfloat16
    )
    d_query = jnp.einsum("hpq,hqd->hpd", d_scores, keys_all, preferred_element_type=jnp.float32)
    part_keys = jnp.einsum(
        "hpq,hpd->hqd", d_scores, query_heads, preferred_element_type=jnp.float32
    )
    part_values = jnp.einsum(
        "hpq,hpd->hqd", weights, d_att_heads, preferred_element_type=jnp.float32
    )
    key_grad = part_keys[:, :row_count]
    value_grad = part_values[:, :row_count]
    for lag in range(1, SPAN):
        block_keys = part_keys[:, lag * row_count : (lag + 1) * row_count].astype(jnp.bfloat16)
        block_values = part_values[:, lag * row_count : (lag + 1) * row_count].astype(jnp.bfloat16)
        back_values, back_keys = shifted((block_values, block_keys), "seq", -lag)
        key_grad = key_grad + back_keys.astype(jnp.float32)
        value_grad = value_grad + back_values.astype(jnp.float32)
    tile_grads = jnp.concatenate(
        [
            d_u_part,
            row_major(value_grad, row_count, model_width),
            row_major(d_query, row_count, model_width),
            row_major(key_grad, row_count, model_width),
        ],
        axis=1,
    ).astype(jnp.bfloat16)
    slot_grads = jnp.zeros_like(tile_grads).at[recv_list].set(tile_grads)
    returned = lax.all_to_all(slot_grads, "seq", split_axis=0, concat_axis=0, tiled=True)
    d_home = jnp.zeros_like(returned).at[send_list].set(returned)
    coef_sums = lax.psum_scatter(
        lax.dot_general(
            mixed_rows, coef_live, (((0,), (0,)), ((), ())), preferred_element_type=jnp.float32
        ),
        "seq",
        scatter_dimension=0,
        tiled=True,
    )
    row_grad = jnp.dot(coef_sums, neg_all.astype(jnp.float32), precision=lax.Precision.HIGHEST)
    d_w_out = lax.psum_scatter(
        row_grad.astype(jnp.bfloat16), "dp", scatter_dimension=1, tiled=True
    ).astype(jnp.float32)
    return (layer_out, d_home, d_w_out)


def dot(a, b, dims=((1,), (0,))):
    return lax.dot_general(a, b, (dims, ((), ())), preferred_element_type=F32)


def iota(shape, dim):
    return lax.broadcasted_iota(jnp.int32, shape, dim)


def starts_of(len_ref, count):
    starts = [jnp.int32(0)]
    for t in range(count):
        starts.append(starts[-1] + len_ref[0, t])
    return starts


def tile_of(position, starts):
    tile = jnp.zeros(position.shape, jnp.int32)
    for start in starts[1:-1]:
        tile = tile + jnp.where(position >= start, 1, 0)
    return tile


def one_hot(condition):
    return jnp.where(condition, 1.0, 0.0).astype(BF16)


def prep_kernel(neg_ids, recv, coef_t, lens, table, small, meta, ids, recv_row, coef_rows, held, neg_rows, lines, sems):
    per, chunk, width = held.shape
    rows = small.shape[1]
    negs = coef_t.shape[0]
    first = [
        pltpu.make_async_copy(neg_ids, ids, sems.at[0]),
        pltpu.make_async_copy(recv, recv_row, sems.at[1]),
        pltpu.make_async_copy(coef_t, coef_rows, sems.at[2]),
        pltpu.make_async_copy(lens, meta, sems.at[3]),
    ]
    for copy in first:
        copy.start()
    first[0].wait()
    copies = []
    for j in range(per):
        start = pl.multiple_of((ids[j] // chunk) * chunk, chunk)
        copies.append(pltpu.make_async_copy(table.at[pl.ds(start, chunk)], held.at[j], sems.at[4 + j]))
        copies[-1].start()
    for copy in first[1:]:
        copy.wait()
    head = jnp.where(iota((IDX_ROWS, rows), 0) == 0, recv_row[...].astype(F32), 0.0)
    small[0:IDX_ROWS] = head.astype(BF16)
    small[IDX_ROWS : IDX_ROWS + negs] = coef_rows[...]
    for j in range(per):
        copies[j].wait()
        own = iota((chunk, width), 0) == ids[j] % chunk
        neg_rows[j : j + 1] = jnp.sum(jnp.where(own, held[j].astype(F32), 0.0), axis=0, keepdims=True)
    for b in range(width // rows):
        lines[per * b : per * (b + 1)] = neg_rows[0:per, b * rows : (b + 1) * rows]
    small[IDX_ROWS + negs :] = lines[...].astype(BF16)


def slot_table(me, len_ref, blocks, order_ref):
    n, _, rows = order_ref.shape
    cell = rows // n
    for b in range(n):
        order_ref[me ^ b] = blocks[b // 2][b % 2, 0:IDX_ROWS].astype(F32)[0:8]
    starts = starts_of(len_ref, n)
    pos = iota((cell, rows), 1)
    filled = [jnp.broadcast_to(order_ref[t, 0:1], (cell, rows)) for t in range(n)]
    value = [jnp.where(pos < len_ref[0, t], pos + starts[t] + 1, 0).astype(F32) for t in range(n)]
    return jnp.concatenate(filled, axis=0), jnp.concatenate(value, axis=0)


def slot_places(filled, value, source, cell):
    slot = (iota(filled.shape, 0) % cell + source * cell).astype(F32)
    return jnp.sum(jnp.where(filled == slot, value, 0.0), axis=1, keepdims=True)


def slot_ranks(places):
    rows = places.shape[0]
    live = places > 0.5
    before = dot(one_hot(iota((rows, rows), 1) < iota((rows, rows), 0)), one_hot(live))
    return jnp.where(live, before, -1.0)


def put_rows(me, head_dim, picked, outs):
    width = picked.shape[1] // PARTS
    for x in range(2 * len(outs)):
        first = pl.multiple_of((me ^ x) * head_dim, head_dim)
        outs[x // 2][x % 2] = jnp.concatenate([picked[:, pl.ds(i * width + first, head_dim)] for i in range(PARTS)], axis=1)


def pack_kernel(sizes, me_ref, len_ref, b0, b1, b2, b3, send, qkvu, *refs):
    n, rows, slots = sizes
    pairs = n // 2
    outs = refs[:pairs]
    pick, order_ref, send_row, held, picked, sems = refs[pairs:]
    cell = rows // n
    me = me_ref[0]
    copies = [pltpu.make_async_copy(send, send_row, sems.at[0]), pltpu.make_async_copy(qkvu, held, sems.at[1])]
    for copy in copies:
        copy.start()
    filled, value = slot_table(me, len_ref, (b0, b1, b2, b3), order_ref)
    places = jnp.broadcast_to(slot_places(filled, value, me, cell), (rows, rows))
    lane = iota((rows, rows), 1)
    sub = iota((rows, rows), 0)
    by_rank = one_hot(slot_ranks(places) == lane.astype(F32))
    copies[0].wait()
    home = jnp.sum(jnp.where(lane == sub, send_row[...].astype(F32), 0.0), axis=1, keepdims=True)
    chosen = dot(by_rank, one_hot(home == lane.astype(F32)), ((0,), (0,))).astype(BF16)
    pick[...] = chosen
    copies[1].wait()
    picked[...] = dot(chosen[0:slots], held[...]).astype(BF16)
    put_rows(me, held.shape[1] // (PARTS * n), picked, outs)


def index_kernel(sizes, me_ref, len_ref, b0, b1, b2, b3, w_out, place, most, coef_c, d_mixed, negatives, order_ref, small_ref, neg_rows, w_rows, sem):
    n, rows, live_cap, negs, per = sizes
    cell = rows // n
    me = me_ref[0]
    blocks = (b0, b1, b2, b3)
    span = w_rows.shape[0]
    copy = pltpu.make_async_copy(w_out.at[pl.ds(pl.multiple_of(me * span, span), span)], w_rows, sem)
    copy.start()
    filled, value = slot_table(me, len_ref, blocks, order_ref)
    lane = iota((rows, rows), 1)
    places = jnp.zeros((rows, rows), F32)
    columns = [slot_places(filled, value, s, cell) for s in range(n)]
    for s in range(n):
        places = jnp.where(lane == s, columns[s], places)
    ranks = slot_ranks(places)
    count = jnp.sum(jnp.where(places > 0.5, 1.0, 0.0), axis=0, keepdims=True)
    most[...] = jnp.broadcast_to(jnp.max(count), most.shape)
    for s in range(n):
        hit = jnp.where(ranks[:, s : s + 1] == lane.astype(F32), columns[s], 0.0)
        place[pl.ds(me ^ s, 1), :] = jnp.sum(hit, axis=0, keepdims=True) - 1.0
    for b in range(n):
        small_ref[me ^ b] = blocks[b // 2][b % 2, IDX_ROWS:].astype(F32)
    starts = starts_of(len_ref, n)
    total = jnp.zeros((negs, live_cap), F32)
    wide = iota((live_cap, rows), 0)
    pos = iota((live_cap, rows), 1)
    for t in range(n):
        pick = one_hot((wide == pos + starts[t]) & (pos < len_ref[0, t]))
        total = total + dot(small_ref[t, 0:negs].astype(BF16), pick, ((1,), (1,)))
    coef_t = total.astype(BF16)
    coef_c[...] = coef_t
    width = neg_rows.shape[1]
    for s in range(n):
        for b in range(width // rows):
            neg_rows[per * s : per * (s + 1), b * rows : (b + 1) * rows] = small_ref[s, negs + per * b : negs + per * (b + 1)]
    neg = neg_rows[...].astype(BF16)
    negatives[...] = neg
    head_grad = dot(coef_t, neg, ((0,), (0,))).astype(BF16)
    copy.wait()
    d_mixed[...] = dot(head_grad, w_rows[...], ((1,), (1,)))


def pair_live(live_cap, starts):
    row = iota((live_cap, 1), 0)
    col = iota((1, live_cap), 1)
    return (col <= row) & (tile_of(col, starts) > tile_of(row, starts) - SPAN) & (row < starts[-1])


def slot_pick(live_cap, place, slots):
    if slots < place.shape[1]:
        pairs = [
            jnp.concatenate([place[x : x + 1, :slots], place[x + 1 : x + 2, :slots]], axis=1)
            for x in range(0, place.shape[0], 2)
        ]
    else:
        pairs = [place[x : x + 1] for x in range(place.shape[0])]
    row = iota((live_cap, pairs[0].shape[1]), 0).astype(F32)
    return jnp.concatenate([one_hot(row == pair) for pair in pairs], axis=1)


def by_distance(blocks):
    return [block[i % 2] for i, block in enumerate(blocks)]


def forward_kernel(sizes, len_ref, place, d_mixed, *refs):
    n, rows, live_cap, slots = sizes
    compact, weights, att, stats = refs[n:]
    head_dim = att.shape[1]
    starts = starts_of(len_ref, n)
    both = dot(slot_pick(live_cap, place[...], slots), jnp.concatenate(by_distance(refs[:n]), axis=0)).astype(BF16)
    compact[...] = both
    u, v, q, k = (both[:, i * head_dim : (i + 1) * head_dim] for i in range(PARTS))
    scores = dot(q, k, ((1,), (1,))) * (1.0 / math.sqrt(head_dim))
    sig = jax.nn.sigmoid(scores)
    w = jnp.where(pair_live(live_cap, starts), scores * sig * (1.0 / rows), 0.0).astype(BF16)
    weights[...] = w
    a = dot(w, v)
    att[...] = a
    dn = d_mixed[...] * u.astype(F32)
    mean = jnp.sum(a, axis=1, keepdims=True) * (1.0 / head_dim)
    cen = a - mean
    lane = iota((live_cap, 128), 1)
    cols = jnp.where(lane == 0, mean, 0.0)
    cols = jnp.where(lane == 1, jnp.sum(cen * cen, axis=1, keepdims=True), cols)
    cols = jnp.where(lane == 2, jnp.sum(dn, axis=1, keepdims=True), cols)
    cols = jnp.where(lane == 3, jnp.sum(dn * cen, axis=1, keepdims=True), cols)
    stats[...] = jnp.transpose(cols)[0:8]


def merge_stats(a, b, count):
    gap = b[0] - a[0]
    return (
        (a[0] + b[0]) * 0.5,
        a[1] + b[1] + gap * gap * (0.5 * count),
        a[2] + b[2],
        a[3] + b[3] + (b[2] - a[2]) * gap * 0.5,
    )


def start_of(len_ref, n, tile):
    start = jnp.int32(0)
    for t in range(n):
        start = start + jnp.where(t < tile, len_ref[0, t], 0)
    return start


def backward_kernel(sizes, me_ref, len_ref, compact, weights, att, d_mixed, st0, st1, st2, st3, place, *refs):
    n, rows, live_cap, slots = sizes
    outs = refs[: n // 2]
    mixed_ref = refs[n // 2]
    head_dim = att.shape[1]
    width = head_dim * n
    me = me_ref[0]
    starts = starts_of(len_ref, n)
    quad = [[st[i : i + 1] for i in range(4)] for st in (st0, st1, st2, st3)]
    ab = merge_stats(quad[0], quad[1], 2 * head_dim)
    cd = merge_stats(quad[2], quad[3], 2 * head_dim)
    mean, m2, s_dn, s_dna = merge_stats(ab, cd, 4 * head_dim)
    inv = lax.rsqrt(m2 * (1.0 / width) + eps)
    table = jnp.concatenate([mean, inv, s_dn * (1.0 / width), s_dna * inv * (1.0 / width), jnp.zeros((124, live_cap), F32)], axis=0)
    table = jnp.transpose(table)
    mean, inv, mean_dn, mean_dnn = (table[:, i : i + 1] for i in range(4))
    both = compact[...]
    u, v, q, k = (both[:, i * head_dim : (i + 1) * head_dim] for i in range(PARTS))
    u = u.astype(F32)
    dm = d_mixed[...]
    normed = (att[...] - mean) * inv
    mixed = (normed * u).astype(BF16)
    dn = dm * u
    d_att = ((dn - mean_dn - normed * mean_dnn) * inv).astype(BF16)
    scale = 1.0 / math.sqrt(head_dim)
    scores = dot(q, k, ((1,), (1,))) * scale
    sig = jax.nn.sigmoid(scores)
    slope = sig * (1.0 + scores * (1.0 - sig)) * (scale / rows)
    ds = jnp.where(pair_live(live_cap, starts), dot(d_att, v, ((1,), (1,))) * slope, 0.0).astype(BF16)
    grad = jnp.concatenate(
        [dm * normed, dot(weights[...], d_att, ((0,), (0,))), dot(ds, k), dot(ds, q, ((0,), (0,)))], axis=1
    ).astype(BF16)
    mixed_ref[...] = mixed
    sent = dot(slot_pick(live_cap, place[...], slots), grad, ((0,), (0,))).astype(BF16)
    quarter = rows // PARTS
    col = iota((rows, live_cap), 1)
    row = iota((rows, live_cap), 0)
    for x in range(n):
        outs[x // 2][x % 2, 0:slots] = sent[x * slots : (x + 1) * slots]
        t = me ^ x
        tile = dot(one_hot((col == row + start_of(len_ref, n, t)) & (row < len_ref[0, t])), mixed).astype(BF16)
        outs[x // 2][x % 2, slots : slots + quarter] = jnp.concatenate(
            [tile[b * quarter : (b + 1) * quarter] for b in range(PARTS)], axis=1
        )


def sums_kernel(coef_c, mixed, most, later, sums):
    negs = coef_c.shape[0]
    sums[0:negs] = dot(coef_c[...], mixed[...])
    sums[negs:] = most[...]


def finish_kernel(sizes, me_ref, pick_ref, w_out, negatives, *refs):
    n, rows, slots, groups = sizes
    sums = refs[:groups]
    blocks = refs[groups : groups + n]
    d_home, layer_out, d_w_out, mixed = refs[groups + n :]
    me = me_ref[0]
    wide = blocks[0].shape[2]
    head_dim = wide // PARTS
    width = head_dim * n
    quarter = rows // PARTS
    pick = pick_ref[0:slots]
    for x, block in enumerate(by_distance(blocks)):
        first = pl.multiple_of((me ^ x) * head_dim, head_dim)
        full = dot(pick, block[0:slots], ((0,), (0,))).astype(BF16)
        for i in range(PARTS):
            d_home[:, pl.ds(i * width + first, head_dim)] = full[:, i * head_dim : (i + 1) * head_dim]
        mixed[:, pl.ds(first, head_dim)] = jnp.concatenate(
            [block[slots : slots + quarter, b * head_dim : (b + 1) * head_dim] for b in range(PARTS)], axis=0
        )
    layer_out[...] = dot(mixed[...], w_out[...]).astype(BF16)
    negs = negatives.shape[0]
    rest = functools.reduce(jnp.add, [part[0:negs] for part in sums])
    columns = width // groups
    neg = negatives[:, pl.ds(pl.multiple_of(me_ref[1] * columns, columns), columns)]
    grad = jnp.zeros((head_dim, columns), F32)
    for _ in range(3):
        piece = rest.astype(BF16)
        grad = grad + dot(piece, neg, ((0,), (0,)))
        rest = rest - piece.astype(F32)
    d_w_out[...] = grad


def kernel_call(body, shapes, specs, scratch=(), limit=40):
    return pl.pallas_call(
        body,
        out_shape=shapes,
        in_specs=specs,
        out_specs=jax.tree.map(lambda _: VMEM, shapes),
        scratch_shapes=scratch,
        compiler_params=pltpu.CompilerParams(vmem_limit_bytes=limit * 1024 * 1024),
    )


def swap(block, axis, distance):
    return lax.ppermute(block, axis, [(i, i ^ distance) for i in range(lax.axis_size(axis))])


def exchange(message, between):
    far = [swap(own, "seq", 2 * d) for d, own in enumerate(message) if d > 0]
    near = swap(message[0], "seq", 1)
    made = between(near)
    blocks = [message[0], near]
    for own in far:
        own, made = lax.optimization_barrier((own, made))
        blocks += [own, swap(own, "seq", 1)]
    return blocks, made


def gather_small(block):
    pair = jnp.stack([block, swap(block, "seq", 1)])
    return [pair] + [swap(pair, "seq", d) for d in range(2, lax.axis_size("seq"), 2)]


def head_plan(qkvu, w_out, head_coef, item_table, neg_ids, send_order, recv_order, tile_len):
    n = lax.axis_size("seq")
    groups = lax.axis_size("dp")
    rows = qkvu.shape[0]
    width = w_out.shape[0]
    head_dim = width // HEADS
    negs = head_coef.shape[1]
    per = neg_ids.shape[0]
    wide = PARTS * head_dim
    live_cap = -(-(n * rows // 3) // 128) * 128
    lines = per * width // rows
    sds = jax.ShapeDtypeStruct
    me = lax.axis_index("seq")
    me_arr = jnp.stack([me, lax.axis_index("dp")]).astype(jnp.int32)
    head_coef_t = head_coef.T

    small, lens = pl.pallas_call(
        prep_kernel,
        out_shape=(sds((IDX_ROWS + negs + lines, rows), BF16), sds(tile_len.shape, jnp.int32)),
        in_specs=[ANY] * 5,
        out_specs=(VMEM, SMEM),
        scratch_shapes=[
            pltpu.SMEM((per,), jnp.int32),
            pltpu.VMEM((1, rows), jnp.int32),
            pltpu.VMEM((negs, rows), BF16),
            pltpu.VMEM((per, 16, width), BF16),
            pltpu.VMEM((8, width), F32),
            pltpu.VMEM((lines, rows), F32),
            pltpu.SemaphoreType.DMA((4 + per,)),
        ],
        compiler_params=pltpu.CompilerParams(vmem_limit_bytes=LIMIT),
    )(neg_ids, recv_order, head_coef_t, tile_len, item_table)
    blocks = gather_small(small)
    def passes(slots):
        *message, pick = kernel_call(
            functools.partial(pack_kernel, (n, rows, slots)),
            (sds((2, slots, wide), BF16),) * (n // 2) + (sds((rows, rows), BF16),),
            [SMEM, SMEM] + [VMEM] * 4 + [ANY] * 2,
            [
                pltpu.VMEM((n, 8, rows), F32),
                pltpu.VMEM((1, rows), jnp.int32),
                pltpu.VMEM(qkvu.shape, BF16),
                pltpu.VMEM((slots, PARTS * width), BF16),
                pltpu.SemaphoreType.DMA((2,)),
            ],
        )(me_arr, lens, *blocks, send_order, qkvu)

        def index(_):
            return kernel_call(
                functools.partial(index_kernel, (n, rows, live_cap, negs, per)),
                (
                    sds((n, rows), F32),
                    sds((8, 128), F32),
                    sds((negs, live_cap), BF16),
                    sds((live_cap, head_dim), F32),
                    sds((negs, width), BF16),
                ),
                [SMEM, SMEM] + [VMEM] * 4 + [ANY],
                [
                    pltpu.VMEM((n, 8, rows), F32),
                    pltpu.VMEM((n, negs + lines, rows), F32),
                    pltpu.VMEM((negs, width), F32),
                    pltpu.VMEM((head_dim, width), BF16),
                    pltpu.SemaphoreType.DMA,
                ],
            )(me_arr, lens, *blocks, w_out)

        received, (place, most, coef_c, d_mixed, negatives) = exchange(message, index)
        compact, weights, att, stats = kernel_call(
            functools.partial(forward_kernel, (n, rows, live_cap, slots)),
            (
                sds((live_cap, wide), BF16),
                sds((live_cap, live_cap), BF16),
                sds((live_cap, head_dim), F32),
                sds((8, live_cap), F32),
            ),
            [SMEM] + [VMEM] * (2 + n),
        )(lens, place, d_mixed, *received)
        other = swap(stats, "seq", 1)
        paired = jnp.stack(
            list(merge_stats([stats[i] for i in range(4)], [other[i] for i in range(4)], head_dim))
            + [jnp.zeros_like(stats[0])] * 4
        )
        far = [swap(paired, "seq", d) for d in range(2, n, 2)]
        *back, mixed = kernel_call(
            functools.partial(backward_kernel, (n, rows, live_cap, slots)),
            (sds((2, slots + rows // PARTS, wide), BF16),) * (n // 2) + (sds((live_cap, head_dim), BF16),),
            [SMEM] * 2 + [VMEM] * 9,
        )(me_arr, lens, compact, weights, att, d_mixed, paired, *far, place)

        def group_sums(later):
            sums = kernel_call(sums_kernel, sds((negs + 8, head_dim), F32), [VMEM] * 3 + [ANY])(
                coef_c, mixed, most, later
            )
            sums = [sums] + [swap(sums, "dp", d) for d in range(1, groups)]
            return sums, functools.reduce(jnp.maximum, sums)[negs, 0] > slots

        returned, (sums, overflow) = exchange(back, group_sums)
        return overflow, (pick, negatives, *sums, *returned)

    def finish(slots, *parts):
        return kernel_call(
            functools.partial(finish_kernel, (n, rows, slots, groups)),
            (sds((rows, PARTS * width), BF16), sds((rows, width), BF16), sds((head_dim, width // groups), F32)),
            [SMEM] + [VMEM] * (3 + groups + n),
            [pltpu.VMEM((rows, width), BF16)],
        )(me_arr, parts[0], w_out, *parts[1:])

    overflow, parts = passes(SLOTS)
    d_home, layer_out, d_w_out = lax.cond(
        overflow, lambda *_: finish(rows, *passes(rows)[1]), lambda *parts: finish(SLOTS, *parts), *parts
    )
    return (layer_out, d_home, d_w_out)


def solution(mesh):
    placed = (
        P(("dp", "seq"), None),
        P(),
        P(("dp", "seq"), None),
        P("seq", None),
        P("seq"),
        P(("dp", "seq"), None),
        P(("dp", "seq"), None),
        P("dp", None),
    )
    return jax.shard_map(
        head_plan if mesh.shape["seq"] == HEADS else tile_plan,
        mesh=mesh,
        in_specs=placed,
        out_specs=(P(("dp", "seq"), None), P(("dp", "seq"), None), P("seq", "dp")),
        check_vma=False,
    )
```

```python
import functools
import math

import jax
import jax.numpy as jnp
from jax import lax
from jax.experimental import pallas as pl
from jax.experimental.pallas import tpu as pltpu
from jax.sharding import PartitionSpec as P

HEADS = 8
SPAN = 3
PARTS = 4
SLOTS = 64
EXTRA = 8
LENS = 2


eps = 1e-05

VMEM = pl.BlockSpec(memory_space=pltpu.VMEM)
SMEM = pl.BlockSpec(memory_space=pltpu.SMEM)
ANY = pl.BlockSpec(memory_space=pl.ANY)
F32 = jnp.float32
BF16 = jnp.bfloat16


def shifted(block, axis, distance):
    devices = range(lax.axis_size(axis))
    route = [(i - distance, i) for i in devices if i - distance in devices]
    return lax.ppermute(block, axis, route)


def silu_grad(values):
    sigmoid_val = jax.nn.sigmoid(values)
    return sigmoid_val * (1.0 + values * (1.0 - sigmoid_val))


def pair_mask(count, len_p, len_q, allowed, causal):
    positions = jnp.arange(count, dtype=jnp.int32)
    live = (positions[:, None] < len_p) & (positions[None, :] < len_q) & allowed
    if causal:
        live = live & (positions[None, :] <= positions[:, None])
    return jnp.where(live, 1.0, 0.0).astype(jnp.float32)


def head_major(flat, count, head_dim):
    return flat.reshape(count, HEADS, head_dim).transpose(1, 0, 2)


def row_major(heads_first, count, width):
    return heads_first.transpose(1, 0, 2).reshape(count, width)


def tile_plan(qkvu, w_out, head_coef, item_table, neg_ids, send_order, recv_order, tile_len):
    row_count = qkvu.shape[0]
    model_width = w_out.shape[0]
    head_dim = model_width // HEADS
    score_scale = 1.0 / math.sqrt(head_dim)
    send_list = send_order[0]
    recv_list = recv_order[0]
    own_index = lax.axis_index("seq")
    lengths_row = tile_len[0]
    own_len = jnp.take(lengths_row, own_index)
    outgoing = jnp.take(qkvu, send_list, axis=0)
    received = lax.all_to_all(outgoing, "seq", split_axis=0, concat_axis=0, tiled=True)
    balanced = jnp.take(received, recv_list, axis=0)
    neg_all = lax.all_gather(jnp.take(item_table, neg_ids, axis=0), "seq", axis=0, tiled=True)
    u_part = balanced[:, :model_width].astype(jnp.float32)
    value_heads = head_major(balanced[:, model_width : 2 * model_width], row_count, head_dim)
    query_heads = head_major(balanced[:, 2 * model_width : 3 * model_width], row_count, head_dim)
    key_heads = head_major(balanced[:, 3 * model_width :], row_count, head_dim)
    lagged = []
    carried = (value_heads, key_heads)
    for lag in range(1, SPAN):
        carried = shifted((carried[0], carried[1]), "seq", 1)
        lagged.append(carried)
    value_list = [value_heads]
    key_list = [key_heads]
    mask_list = [pair_mask(row_count, own_len, own_len, True, True)]
    for lag in range(1, SPAN):
        earlier_len = jnp.take(lengths_row, jnp.maximum(own_index - lag, 0))
        value_list.append(lagged[lag - 1][0])
        key_list.append(lagged[lag - 1][1])
        mask_list.append(pair_mask(row_count, own_len, earlier_len, own_index >= lag, False))
    values_all = jnp.concatenate(value_list, axis=1)
    keys_all = jnp.concatenate(key_list, axis=1)
    mask_all = jnp.concatenate(mask_list, axis=1)
    scores = (
        jnp.einsum("hpd,hqd->hpq", query_heads, keys_all, preferred_element_type=jnp.float32)
        * score_scale
    )
    weights = (jax.nn.silu(scores) * mask_all[None] / row_count).astype(jnp.bfloat16)
    attended_heads = jnp.einsum(
        "hpq,hqd->hpd", weights, values_all, preferred_element_type=jnp.float32
    )
    attended = row_major(attended_heads, row_count, model_width)
    row_mean = jnp.mean(attended, axis=1, keepdims=True)
    centered = attended - row_mean
    variance = jnp.mean(centered * centered, axis=1, keepdims=True)
    inv_std = lax.rsqrt(variance + eps)
    normed = centered * inv_std
    mixed_rows = (normed * u_part).astype(jnp.bfloat16)
    layer_out = jnp.dot(mixed_rows, w_out, preferred_element_type=jnp.float32).astype(jnp.bfloat16)
    positions = jnp.arange(row_count, dtype=jnp.int32)
    live_col = jnp.where(positions < own_len, 1.0, 0.0).astype(jnp.float32)[:, None]
    coef_live = (head_coef * live_col).astype(jnp.bfloat16)
    head_grad = jnp.dot(coef_live, neg_all, preferred_element_type=jnp.float32).astype(jnp.bfloat16)
    d_mixed = lax.dot_general(
        head_grad, w_out, (((1,), (1,)), ((), ())), preferred_element_type=jnp.float32
    )
    d_u_part = d_mixed * normed
    d_normed = d_mixed * u_part
    d_att = (
        d_normed
        - jnp.mean(d_normed, axis=1, keepdims=True)
        - normed * jnp.mean(d_normed * normed, axis=1, keepdims=True)
    ) * inv_std
    d_att_heads = head_major(d_att.astype(jnp.bfloat16), row_count, head_dim)
    d_weights = jnp.einsum(
        "hpd,hqd->hpq", d_att_heads, values_all, preferred_element_type=jnp.float32
    )
    d_scores = (d_weights * mask_all[None] / row_count * silu_grad(scores) * score_scale).astype(
        jnp.bfloat16
    )
    d_query = jnp.einsum("hpq,hqd->hpd", d_scores, keys_all, preferred_element_type=jnp.float32)
    part_keys = jnp.einsum(
        "hpq,hpd->hqd", d_scores, query_heads, preferred_element_type=jnp.float32
    )
    part_values = jnp.einsum(
        "hpq,hpd->hqd", weights, d_att_heads, preferred_element_type=jnp.float32
    )
    key_grad = part_keys[:, :row_count]
    value_grad = part_values[:, :row_count]
    for lag in range(1, SPAN):
        block_keys = part_keys[:, lag * row_count : (lag + 1) * row_count].astype(jnp.bfloat16)
        block_values = part_values[:, lag * row_count : (lag + 1) * row_count].astype(jnp.bfloat16)
        back_values, back_keys = shifted((block_values, block_keys), "seq", -lag)
        key_grad = key_grad + back_keys.astype(jnp.float32)
        value_grad = value_grad + back_values.astype(jnp.float32)
    tile_grads = jnp.concatenate(
        [
            d_u_part,
            row_major(value_grad, row_count, model_width),
            row_major(d_query, row_count, model_width),
            row_major(key_grad, row_count, model_width),
        ],
        axis=1,
    ).astype(jnp.bfloat16)
    slot_grads = jnp.zeros_like(tile_grads).at[recv_list].set(tile_grads)
    returned = lax.all_to_all(slot_grads, "seq", split_axis=0, concat_axis=0, tiled=True)
    d_home = jnp.zeros_like(returned).at[send_list].set(returned)
    coef_sums = lax.psum_scatter(
        lax.dot_general(
            mixed_rows, coef_live, (((0,), (0,)), ((), ())), preferred_element_type=jnp.float32
        ),
        "seq",
        scatter_dimension=0,
        tiled=True,
    )
    row_grad = jnp.dot(coef_sums, neg_all.astype(jnp.float32), precision=lax.Precision.HIGHEST)
    d_w_out = lax.psum_scatter(
        row_grad.astype(jnp.bfloat16), "dp", scatter_dimension=1, tiled=True
    ).astype(jnp.float32)
    return (layer_out, d_home, d_w_out)


def dot(a, b, dims=((1,), (0,))):
    return lax.dot_general(a, b, (dims, ((), ())), preferred_element_type=F32)


def iota(shape, dim):
    return lax.broadcasted_iota(jnp.int32, shape, dim)


def starts_of(meta, count):
    starts = [jnp.int32(0)]
    for t in range(count):
        starts.append(starts[-1] + meta[LENS + t])
    return starts


def tile_of(position, starts):
    tile = jnp.zeros(position.shape, jnp.int32)
    for start in starts[1:-1]:
        tile = tile + jnp.where(position >= start, 1, 0)
    return tile


def one_hot(condition):
    return jnp.where(condition, 1.0, 0.0).astype(BF16)


def slot_table(meta, blocks, order_ref):
    n, _, rows = order_ref.shape
    cell = rows // n
    for b in range(n):
        order_ref[meta[0] ^ b] = blocks[b // 2][b % 2].astype(F32)
    starts = starts_of(meta, n)
    pos = iota((cell, rows), 1)
    filled = [jnp.broadcast_to(order_ref[t], (cell, rows)) for t in range(n)]
    value = [jnp.where(pos < meta[LENS + t], pos + starts[t] + 1, 0).astype(F32) for t in range(n)]
    return jnp.concatenate(filled, axis=0), jnp.concatenate(value, axis=0)


def slot_places(filled, value, source, cell):
    slot = (iota(filled.shape, 0) % cell + source * cell).astype(F32)
    return jnp.sum(jnp.where(filled == slot, value, 0.0), axis=1, keepdims=True)


def slot_ranks(places):
    rows = places.shape[0]
    live = places > 0.5
    before = dot(one_hot(iota((rows, rows), 1) < iota((rows, rows), 0)), one_hot(live))
    return jnp.where(live, before, -1.0)


def put_rows(me, head_dim, picked, outs):
    width = picked.shape[1] // PARTS
    for x in range(2 * len(outs)):
        first = pl.multiple_of((me ^ x) * head_dim, head_dim)
        outs[x // 2][x % 2] = jnp.concatenate([picked[:, pl.ds(i * width + first, head_dim)] for i in range(PARTS)], axis=1)


def pack_kernel(sizes, meta, b0, b1, b2, b3, send, neg_ids, coef_t, table, qkvu, *refs):
    n, rows, slots = sizes
    pairs = n // 2
    outs = refs[:pairs]
    pick, order_ref, send_row, ids, coef_rows, items, neg_rows, held, picked, sems = refs[pairs:]
    per, chunk, width = items.shape
    wide = outs[0].shape[2]
    cell = rows // n
    me = meta[0]
    copies = [
        pltpu.make_async_copy(source, target, sems.at[i])
        for i, (source, target) in enumerate(((neg_ids, ids), (send, send_row), (coef_t, coef_rows), (qkvu, held)))
    ]
    for copy in copies:
        copy.start()
    copies[0].wait()
    item_copies = []
    for j in range(per):
        start = pl.multiple_of((ids[j] // chunk) * chunk, chunk)
        item_copies.append(pltpu.make_async_copy(table.at[pl.ds(start, chunk)], items.at[j], sems.at[4 + j]))
        item_copies[-1].start()
    filled, value = slot_table(meta, (b0, b1, b2, b3), order_ref)
    places = jnp.broadcast_to(slot_places(filled, value, me, cell), (rows, rows))
    lane = iota((rows, rows), 1)
    sub = iota((rows, rows), 0)
    by_rank = one_hot(slot_ranks(places) == lane.astype(F32))
    copies[1].wait()
    home = jnp.sum(jnp.where(lane == sub, send_row[...].astype(F32), 0.0), axis=1, keepdims=True)
    chosen = dot(by_rank, one_hot(home == lane.astype(F32)), ((0,), (0,))).astype(BF16)
    pick[...] = chosen
    copies[2].wait()
    copies[3].wait()
    picked[...] = dot(chosen[0:slots], held[...]).astype(BF16)
    for j in range(per):
        item_copies[j].wait()
        own = iota((chunk, width), 0) == ids[j] % chunk
        neg_rows[j : j + 1] = jnp.sum(jnp.where(own, items[j].astype(F32), 0.0), axis=0, keepdims=True)
    step = coef_rows.shape[0] * rows // wide
    coefs = jnp.concatenate([coef_rows[b * step : (b + 1) * step].astype(F32) for b in range(wide // rows)], axis=1)
    negs = jnp.concatenate([neg_rows[0:per, b * wide : (b + 1) * wide] for b in range(width // wide)], axis=0)
    head_dim = wide // PARTS
    for x in range(n):
        first = pl.multiple_of((me ^ x) * head_dim, head_dim)
        out = outs[x // 2]
        out[x % 2, 0:slots] = jnp.concatenate([picked[:, pl.ds(i * width + first, head_dim)] for i in range(PARTS)], axis=1)
        out[x % 2, slots:] = (coefs, negs)[x % 2].astype(BF16)


def index_kernel(sizes, meta, b0, b1, b2, b3, place, most, order_ref):
    n, rows = sizes
    cell = rows // n
    me = meta[0]
    filled, value = slot_table(meta, (b0, b1, b2, b3), order_ref)
    lane = iota((rows, rows), 1)
    places = jnp.zeros((rows, rows), F32)
    columns = [slot_places(filled, value, s, cell) for s in range(n)]
    for s in range(n):
        places = jnp.where(lane == s, columns[s], places)
    ranks = slot_ranks(places)
    count = jnp.sum(jnp.where(places > 0.5, 1.0, 0.0), axis=0, keepdims=True)
    most[...] = jnp.broadcast_to(jnp.max(count), most.shape)
    for s in range(n):
        hit = jnp.where(ranks[:, s : s + 1] == lane.astype(F32), columns[s], 0.0)
        place[pl.ds(me ^ s, 1), :] = jnp.sum(hit, axis=0, keepdims=True) - 1.0


def pair_live(live_cap, starts):
    row = iota((live_cap, 1), 0)
    col = iota((1, live_cap), 1)
    return (col <= row) & (tile_of(col, starts) > tile_of(row, starts) - SPAN) & (row < starts[-1])


def slot_pick(live_cap, place, slots, after):
    n, rows = place.shape
    padded = jnp.concatenate([place, jnp.full((n, rows), -1.0, F32)], axis=1)
    padded = jnp.where(iota(padded.shape, 1) < slots, padded, -1.0)
    line = jnp.concatenate([padded[x : x + 1, : slots + after] for x in range(n)], axis=1)
    return one_hot(iota((live_cap, line.shape[1]), 0).astype(F32) == line)


def by_distance(blocks):
    return [block[i % 2] for i, block in enumerate(blocks)]


def forward_kernel(sizes, meta, place, w_out, *refs):
    n, rows, live_cap, slots, per = sizes
    blocks = refs[:n]
    compact, weights, att, stats, coef_c, d_mixed, negatives, neg_rows, w_rows, sem = refs[n:]
    head_dim = att.shape[1]
    negs = coef_c.shape[0]
    wide = blocks[0].shape[2]
    me = meta[0]
    copy = pltpu.make_async_copy(w_out.at[pl.ds(pl.multiple_of(me * head_dim, head_dim), head_dim)], w_rows, sem)
    copy.start()
    starts = starts_of(meta, n)
    both = dot(slot_pick(live_cap, place[...], slots, EXTRA), jnp.concatenate(by_distance(blocks), axis=0)).astype(BF16)
    compact[...] = both
    total = jnp.zeros((negs, live_cap), F32)
    tall = iota((live_cap, rows), 0)
    pos = iota((live_cap, rows), 1)
    for x in range(n):
        t = me ^ x
        hit = one_hot((tall == pos + start_of(meta, n, t)) & (pos < meta[LENS + t]))
        coefs = blocks[x][0, slots:].astype(F32)
        coefs = jnp.concatenate([coefs[:, b * rows : (b + 1) * rows] for b in range(wide // rows)], axis=0).astype(BF16)
        total = total + dot(coefs, hit, ((1,), (1,)))
        items = blocks[x][1, slots:].astype(F32)
        for b in range(n * head_dim // wide):
            neg_rows[t, 0:per, b * wide : (b + 1) * wide] = items[b * per : (b + 1) * per]
    coef_t = total.astype(BF16)
    coef_c[...] = coef_t
    neg = jnp.concatenate([neg_rows[s, 0:per] for s in range(n)], axis=0).astype(BF16)
    negatives[...] = neg
    head_grad = dot(coef_t, neg, ((0,), (0,))).astype(BF16)
    copy.wait()
    dm = dot(head_grad, w_rows[...], ((1,), (1,)))
    d_mixed[...] = dm
    u, v, q, k = (both[:, i * head_dim : (i + 1) * head_dim] for i in range(PARTS))
    scores = dot(q, k, ((1,), (1,))) * (1.0 / math.sqrt(head_dim))
    sig = jax.nn.sigmoid(scores)
    w = jnp.where(pair_live(live_cap, starts), scores * sig * (1.0 / rows), 0.0).astype(BF16)
    weights[...] = w
    a = dot(w, v)
    att[...] = a
    dn = dm * u.astype(F32)
    mean = jnp.sum(a, axis=1, keepdims=True) * (1.0 / head_dim)
    cen = a - mean
    lane = iota((live_cap, 128), 1)
    cols = jnp.where(lane == 0, mean, 0.0)
    cols = jnp.where(lane == 1, jnp.sum(cen * cen, axis=1, keepdims=True), cols)
    cols = jnp.where(lane == 2, jnp.sum(dn, axis=1, keepdims=True), cols)
    cols = jnp.where(lane == 3, jnp.sum(dn * cen, axis=1, keepdims=True), cols)
    stats[...] = jnp.transpose(cols)[0:8]


def merge_stats(a, b, count):
    gap = b[0] - a[0]
    return (
        (a[0] + b[0]) * 0.5,
        a[1] + b[1] + gap * gap * (0.5 * count),
        a[2] + b[2],
        a[3] + b[3] + (b[2] - a[2]) * gap * 0.5,
    )


def start_of(meta, n, tile):
    start = jnp.int32(0)
    for t in range(n):
        start = start + jnp.where(t < tile, meta[LENS + t], 0)
    return start


def backward_kernel(sizes, meta, compact, weights, att, d_mixed, st0, st1, st2, st3, place, *refs):
    n, rows, live_cap, slots = sizes
    outs = refs[: n // 2]
    mixed_ref = refs[n // 2]
    head_dim = att.shape[1]
    width = head_dim * n
    me = meta[0]
    starts = starts_of(meta, n)
    quad = [[st[i : i + 1] for i in range(4)] for st in (st0, st1, st2, st3)]
    ab = merge_stats(quad[0], quad[1], 2 * head_dim)
    cd = merge_stats(quad[2], quad[3], 2 * head_dim)
    mean, m2, s_dn, s_dna = merge_stats(ab, cd, 4 * head_dim)
    inv = lax.rsqrt(m2 * (1.0 / width) + eps)
    table = jnp.concatenate([mean, inv, s_dn * (1.0 / width), s_dna * inv * (1.0 / width), jnp.zeros((124, live_cap), F32)], axis=0)
    table = jnp.transpose(table)
    mean, inv, mean_dn, mean_dnn = (table[:, i : i + 1] for i in range(4))
    both = compact[...]
    u, v, q, k = (both[:, i * head_dim : (i + 1) * head_dim] for i in range(PARTS))
    u = u.astype(F32)
    dm = d_mixed[...]
    normed = (att[...] - mean) * inv
    mixed = (normed * u).astype(BF16)
    dn = dm * u
    d_att = ((dn - mean_dn - normed * mean_dnn) * inv).astype(BF16)
    scale = 1.0 / math.sqrt(head_dim)
    scores = dot(q, k, ((1,), (1,))) * scale
    sig = jax.nn.sigmoid(scores)
    slope = sig * (1.0 + scores * (1.0 - sig)) * (scale / rows)
    ds = jnp.where(pair_live(live_cap, starts), dot(d_att, v, ((1,), (1,))) * slope, 0.0).astype(BF16)
    grad = jnp.concatenate(
        [dm * normed, dot(weights[...], d_att, ((0,), (0,))), dot(ds, k), dot(ds, q, ((0,), (0,)))], axis=1
    ).astype(BF16)
    mixed_ref[...] = mixed
    sent = dot(slot_pick(live_cap, place[...], slots, 0), grad, ((0,), (0,))).astype(BF16)
    quarter = rows // PARTS
    col = iota((rows, live_cap), 1)
    row = iota((rows, live_cap), 0)
    for x in range(n):
        outs[x // 2][x % 2, quarter:] = sent[x * slots : (x + 1) * slots]
        t = me ^ x
        tile = dot(one_hot((col == row + start_of(meta, n, t)) & (row < meta[LENS + t])), mixed).astype(BF16)
        outs[x // 2][x % 2, 0:quarter] = jnp.concatenate(
            [tile[b * quarter : (b + 1) * quarter] for b in range(PARTS)], axis=1
        )


def sums_kernel(coef_c, mixed, most, sums):
    negs = coef_c.shape[0]
    sums[0:negs] = dot(coef_c[...], mixed[...])
    sums[negs:] = most[...]


def total_kernel(*refs):
    sums, (total, most) = refs[:-2], refs[-2:]
    negs = total.shape[0]
    total[...] = functools.reduce(jnp.add, [part[0:negs] for part in sums])
    most[...] = functools.reduce(jnp.maximum, [part[negs:] for part in sums])


def finish_kernel(sizes, meta, pick_ref, w_out, negatives, total, *refs):
    n, rows, slots, groups = sizes
    blocks = refs[:n]
    d_home, layer_out, d_w_out, mixed = refs[n:]
    me = meta[0]
    wide = blocks[0].shape[2]
    head_dim = wide // PARTS
    width = head_dim * n
    quarter = rows // PARTS
    pick = pick_ref[0:slots]
    for x, block in enumerate(by_distance(blocks)):
        first = pl.multiple_of((me ^ x) * head_dim, head_dim)
        full = dot(pick, block[quarter:], ((0,), (0,))).astype(BF16)
        for i in range(PARTS):
            d_home[:, pl.ds(i * width + first, head_dim)] = full[:, i * head_dim : (i + 1) * head_dim]
        mixed[:, pl.ds(first, head_dim)] = jnp.concatenate(
            [block[0:quarter, b * head_dim : (b + 1) * head_dim] for b in range(PARTS)], axis=0
        )
    layer_out[...] = dot(mixed[...], w_out[...]).astype(BF16)
    columns = width // groups
    neg = negatives[:, pl.ds(pl.multiple_of(meta[1] * columns, columns), columns)]
    rest = total[...]
    grad = jnp.zeros((head_dim, columns), F32)
    for _ in range(3):
        piece = rest.astype(BF16)
        grad = grad + dot(piece, neg, ((0,), (0,)))
        rest = rest - piece.astype(F32)
    d_w_out[...] = grad


def kernel_call(body, shapes, specs, scratch=(), limit=40):
    return pl.pallas_call(
        body,
        out_shape=shapes,
        in_specs=specs,
        out_specs=jax.tree.map(lambda _: VMEM, shapes),
        scratch_shapes=scratch,
        compiler_params=pltpu.CompilerParams(vmem_limit_bytes=limit * 1024 * 1024),
    )


def swap(block, axis, distance):
    return lax.ppermute(block, axis, [(i, i ^ distance) for i in range(lax.axis_size(axis))])


def exchange(message, between):
    far = [swap(own, "seq", 2 * d) for d, own in enumerate(message) if d > 0]
    made = between()
    blocks = [message[0], swap(message[0], "seq", 1)]
    for own in far:
        own, made = lax.optimization_barrier((own, made))
        blocks += [own, swap(own, "seq", 1)]
    return blocks, made


def gather_small(block):
    pair = jnp.stack([block, swap(block, "seq", 1)])
    return [pair] + [swap(pair, "seq", d) for d in range(2, lax.axis_size("seq"), 2)]


def head_plan(qkvu, w_out, head_coef, item_table, neg_ids, send_order, recv_order, tile_len):
    n = lax.axis_size("seq")
    groups = lax.axis_size("dp")
    rows = qkvu.shape[0]
    width = w_out.shape[0]
    head_dim = width // HEADS
    negs = head_coef.shape[1]
    per = neg_ids.shape[0]
    wide = PARTS * head_dim
    live_cap = -(-(n * rows // 3) // 128) * 128
    sds = jax.ShapeDtypeStruct
    me = lax.axis_index("seq")
    meta = jnp.concatenate([jnp.stack([me, lax.axis_index("dp")]).astype(jnp.int32), tile_len[0]])
    head_coef_t = head_coef.T

    def passes(slots):
        orders = gather_small(recv_order)
        *message, pick = kernel_call(
            functools.partial(pack_kernel, (n, rows, slots)),
            (sds((2, slots + EXTRA, wide), BF16),) * (n // 2) + (sds((rows, rows), BF16),),
            [SMEM] + [VMEM] * 4 + [ANY] * 5,
            [
                pltpu.VMEM((n, 1, rows), F32),
                pltpu.VMEM((1, rows), jnp.int32),
                pltpu.SMEM((per,), jnp.int32),
                pltpu.VMEM((negs, rows), BF16),
                pltpu.VMEM((per, 16, width), BF16),
                pltpu.VMEM((8, width), F32),
                pltpu.VMEM(qkvu.shape, BF16),
                pltpu.VMEM((slots, PARTS * width), BF16),
                pltpu.SemaphoreType.DMA((4 + per,)),
            ],
        )(meta, *orders, send_order, neg_ids, head_coef_t, item_table, qkvu)

        def index():
            return kernel_call(
                functools.partial(index_kernel, (n, rows)),
                (sds((n, rows), F32), sds((8, 128), F32)),
                [SMEM] + [VMEM] * 4,
                [pltpu.VMEM((n, 1, rows), F32)],
            )(meta, *orders)

        received, (place, most) = exchange(message, index)
        compact, weights, att, stats, coef_c, d_mixed, negatives = kernel_call(
            functools.partial(forward_kernel, (n, rows, live_cap, slots, per)),
            (
                sds((live_cap, wide), BF16),
                sds((live_cap, live_cap), BF16),
                sds((live_cap, head_dim), F32),
                sds((8, live_cap), F32),
                sds((negs, live_cap), BF16),
                sds((live_cap, head_dim), F32),
                sds((negs, width), BF16),
            ),
            [SMEM, VMEM, ANY] + [VMEM] * n,
            [pltpu.VMEM((n, 8, width), F32), pltpu.VMEM((head_dim, width), BF16), pltpu.SemaphoreType.DMA],
        )(meta, place, w_out, *received)
        other = swap(stats, "seq", 1)
        paired = jnp.stack(
            list(merge_stats([stats[i] for i in range(4)], [other[i] for i in range(4)], head_dim))
            + [jnp.zeros_like(stats[0])] * 4
        )
        far = [swap(paired, "seq", d) for d in range(2, n, 2)]
        *back, mixed = kernel_call(
            functools.partial(backward_kernel, (n, rows, live_cap, slots)),
            (sds((2, slots + rows // PARTS, wide), BF16),) * (n // 2) + (sds((live_cap, head_dim), BF16),),
            [SMEM] + [VMEM] * 9,
        )(meta, compact, weights, att, d_mixed, paired, *far, place)

        def group_sums():
            sums = kernel_call(sums_kernel, sds((negs + 8, head_dim), F32), [VMEM] * 3)(coef_c, mixed, most)
            sums = [sums] + [swap(sums, "dp", d) for d in range(1, groups)]
            total, most_of_all = kernel_call(
                total_kernel, (sds((negs, head_dim), F32), sds((8, 128), F32)), [VMEM] * groups
            )(*sums)
            return total, most_of_all[0, 0] > slots

        returned, (total, overflow) = exchange(back, group_sums)
        return overflow, (pick, negatives, total, *returned)

    def finish(slots, *parts):
        return kernel_call(
            functools.partial(finish_kernel, (n, rows, slots, groups)),
            (sds((rows, PARTS * width), BF16), sds((rows, width), BF16), sds((head_dim, width // groups), F32)),
            [SMEM] + [VMEM] * (4 + n),
            [pltpu.VMEM((rows, width), BF16)],
        )(meta, parts[0], w_out, *parts[1:])

    overflow, parts = passes(SLOTS)
    d_home, layer_out, d_w_out = lax.cond(
        overflow, lambda *_: finish(rows, *passes(rows)[1]), lambda *parts: finish(SLOTS, *parts), *parts
    )
    return (layer_out, d_home, d_w_out)


def solution(mesh):
    placed = (
        P(("dp", "seq"), None),
        P(),
        P(("dp", "seq"), None),
        P("seq", None),
        P("seq"),
        P(("dp", "seq"), None),
        P(("dp", "seq"), None),
        P("dp", None),
    )
    return jax.shard_map(
        head_plan if mesh.shape["seq"] == HEADS else tile_plan,
        mesh=mesh,
        in_specs=placed,
        out_specs=(P(("dp", "seq"), None), P(("dp", "seq"), None), P("seq", "dp")),
        check_vma=False,
    )
```

```python
import functools
import math

import jax
import jax.numpy as jnp
from jax import lax
from jax.experimental import pallas as pl
from jax.experimental.pallas import tpu as pltpu
from jax.sharding import PartitionSpec as P

HEADS = 8
SPAN = 3
PARTS = 4
SLOTS = 60
POOL = 104
LENS = 2


eps = 1e-05

VMEM = pl.BlockSpec(memory_space=pltpu.VMEM)
SMEM = pl.BlockSpec(memory_space=pltpu.SMEM)
ANY = pl.BlockSpec(memory_space=pl.ANY)
F32 = jnp.float32
BF16 = jnp.bfloat16


def shifted(block, axis, distance):
    devices = range(lax.axis_size(axis))
    route = [(i - distance, i) for i in devices if i - distance in devices]
    return lax.ppermute(block, axis, route)


def silu_grad(values):
    sigmoid_val = jax.nn.sigmoid(values)
    return sigmoid_val * (1.0 + values * (1.0 - sigmoid_val))


def pair_mask(count, len_p, len_q, allowed, causal):
    positions = jnp.arange(count, dtype=jnp.int32)
    live = (positions[:, None] < len_p) & (positions[None, :] < len_q) & allowed
    if causal:
        live = live & (positions[None, :] <= positions[:, None])
    return jnp.where(live, 1.0, 0.0).astype(jnp.float32)


def head_major(flat, count, head_dim):
    return flat.reshape(count, HEADS, head_dim).transpose(1, 0, 2)


def row_major(heads_first, count, width):
    return heads_first.transpose(1, 0, 2).reshape(count, width)


def tile_plan(qkvu, w_out, head_coef, item_table, neg_ids, send_order, recv_order, tile_len):
    row_count = qkvu.shape[0]
    model_width = w_out.shape[0]
    head_dim = model_width // HEADS
    score_scale = 1.0 / math.sqrt(head_dim)
    send_list = send_order[0]
    recv_list = recv_order[0]
    own_index = lax.axis_index("seq")
    lengths_row = tile_len[0]
    own_len = jnp.take(lengths_row, own_index)
    outgoing = jnp.take(qkvu, send_list, axis=0)
    received = lax.all_to_all(outgoing, "seq", split_axis=0, concat_axis=0, tiled=True)
    balanced = jnp.take(received, recv_list, axis=0)
    neg_all = lax.all_gather(jnp.take(item_table, neg_ids, axis=0), "seq", axis=0, tiled=True)
    u_part = balanced[:, :model_width].astype(jnp.float32)
    value_heads = head_major(balanced[:, model_width : 2 * model_width], row_count, head_dim)
    query_heads = head_major(balanced[:, 2 * model_width : 3 * model_width], row_count, head_dim)
    key_heads = head_major(balanced[:, 3 * model_width :], row_count, head_dim)
    lagged = []
    carried = (value_heads, key_heads)
    for lag in range(1, SPAN):
        carried = shifted((carried[0], carried[1]), "seq", 1)
        lagged.append(carried)
    value_list = [value_heads]
    key_list = [key_heads]
    mask_list = [pair_mask(row_count, own_len, own_len, True, True)]
    for lag in range(1, SPAN):
        earlier_len = jnp.take(lengths_row, jnp.maximum(own_index - lag, 0))
        value_list.append(lagged[lag - 1][0])
        key_list.append(lagged[lag - 1][1])
        mask_list.append(pair_mask(row_count, own_len, earlier_len, own_index >= lag, False))
    values_all = jnp.concatenate(value_list, axis=1)
    keys_all = jnp.concatenate(key_list, axis=1)
    mask_all = jnp.concatenate(mask_list, axis=1)
    scores = (
        jnp.einsum("hpd,hqd->hpq", query_heads, keys_all, preferred_element_type=jnp.float32)
        * score_scale
    )
    weights = (jax.nn.silu(scores) * mask_all[None] / row_count).astype(jnp.bfloat16)
    attended_heads = jnp.einsum(
        "hpq,hqd->hpd", weights, values_all, preferred_element_type=jnp.float32
    )
    attended = row_major(attended_heads, row_count, model_width)
    row_mean = jnp.mean(attended, axis=1, keepdims=True)
    centered = attended - row_mean
    variance = jnp.mean(centered * centered, axis=1, keepdims=True)
    inv_std = lax.rsqrt(variance + eps)
    normed = centered * inv_std
    mixed_rows = (normed * u_part).astype(jnp.bfloat16)
    layer_out = jnp.dot(mixed_rows, w_out, preferred_element_type=jnp.float32).astype(jnp.bfloat16)
    positions = jnp.arange(row_count, dtype=jnp.int32)
    live_col = jnp.where(positions < own_len, 1.0, 0.0).astype(jnp.float32)[:, None]
    coef_live = (head_coef * live_col).astype(jnp.bfloat16)
    head_grad = jnp.dot(coef_live, neg_all, preferred_element_type=jnp.float32).astype(jnp.bfloat16)
    d_mixed = lax.dot_general(
        head_grad, w_out, (((1,), (1,)), ((), ())), preferred_element_type=jnp.float32
    )
    d_u_part = d_mixed * normed
    d_normed = d_mixed * u_part
    d_att = (
        d_normed
        - jnp.mean(d_normed, axis=1, keepdims=True)
        - normed * jnp.mean(d_normed * normed, axis=1, keepdims=True)
    ) * inv_std
    d_att_heads = head_major(d_att.astype(jnp.bfloat16), row_count, head_dim)
    d_weights = jnp.einsum(
        "hpd,hqd->hpq", d_att_heads, values_all, preferred_element_type=jnp.float32
    )
    d_scores = (d_weights * mask_all[None] / row_count * silu_grad(scores) * score_scale).astype(
        jnp.bfloat16
    )
    d_query = jnp.einsum("hpq,hqd->hpd", d_scores, keys_all, preferred_element_type=jnp.float32)
    part_keys = jnp.einsum(
        "hpq,hpd->hqd", d_scores, query_heads, preferred_element_type=jnp.float32
    )
    part_values = jnp.einsum(
        "hpq,hpd->hqd", weights, d_att_heads, preferred_element_type=jnp.float32
    )
    key_grad = part_keys[:, :row_count]
    value_grad = part_values[:, :row_count]
    for lag in range(1, SPAN):
        block_keys = part_keys[:, lag * row_count : (lag + 1) * row_count].astype(jnp.bfloat16)
        block_values = part_values[:, lag * row_count : (lag + 1) * row_count].astype(jnp.bfloat16)
        back_values, back_keys = shifted((block_values, block_keys), "seq", -lag)
        key_grad = key_grad + back_keys.astype(jnp.float32)
        value_grad = value_grad + back_values.astype(jnp.float32)
    tile_grads = jnp.concatenate(
        [
            d_u_part,
            row_major(value_grad, row_count, model_width),
            row_major(d_query, row_count, model_width),
            row_major(key_grad, row_count, model_width),
        ],
        axis=1,
    ).astype(jnp.bfloat16)
    slot_grads = jnp.zeros_like(tile_grads).at[recv_list].set(tile_grads)
    returned = lax.all_to_all(slot_grads, "seq", split_axis=0, concat_axis=0, tiled=True)
    d_home = jnp.zeros_like(returned).at[send_list].set(returned)
    coef_sums = lax.psum_scatter(
        lax.dot_general(
            mixed_rows, coef_live, (((0,), (0,)), ((), ())), preferred_element_type=jnp.float32
        ),
        "seq",
        scatter_dimension=0,
        tiled=True,
    )
    row_grad = jnp.dot(coef_sums, neg_all.astype(jnp.float32), precision=lax.Precision.HIGHEST)
    d_w_out = lax.psum_scatter(
        row_grad.astype(jnp.bfloat16), "dp", scatter_dimension=1, tiled=True
    ).astype(jnp.float32)
    return (layer_out, d_home, d_w_out)


def dot(a, b, dims=((1,), (0,))):
    return lax.dot_general(a, b, (dims, ((), ())), preferred_element_type=F32)


def iota(shape, dim):
    return lax.broadcasted_iota(jnp.int32, shape, dim)


def starts_of(meta, count):
    starts = [jnp.int32(0)]
    for t in range(count):
        starts.append(starts[-1] + meta[LENS + t])
    return starts


def tile_of(position, starts):
    tile = jnp.zeros(position.shape, jnp.int32)
    for start in starts[1:-1]:
        tile = tile + jnp.where(position >= start, 1, 0)
    return tile


def one_hot(condition):
    return jnp.where(condition, 1.0, 0.0).astype(BF16)


def slot_table(meta, blocks, order_ref):
    n, _, rows = order_ref.shape
    cell = rows // n
    for b in range(n):
        order_ref[meta[0] ^ b] = blocks[b // 2][b % 2].astype(F32)
    starts = starts_of(meta, n)
    pos = iota((cell, rows), 1)
    filled = [jnp.broadcast_to(order_ref[t], (cell, rows)) for t in range(n)]
    value = [jnp.where(pos < meta[LENS + t], pos + starts[t] + 1, 0).astype(F32) for t in range(n)]
    return jnp.concatenate(filled, axis=0), jnp.concatenate(value, axis=0)


def slot_places(filled, value, source, cell):
    slot = (iota(filled.shape, 0) % cell + source * cell).astype(F32)
    return jnp.sum(jnp.where(filled == slot, value, 0.0), axis=1, keepdims=True)


def slot_ranks(places):
    rows = places.shape[0]
    live = places > 0.5
    before = dot(one_hot(iota((rows, rows), 1) < iota((rows, rows), 0)), one_hot(live))
    return jnp.where(live, before, -1.0)


def put_rows(me, head_dim, picked, outs):
    width = picked.shape[1] // PARTS
    for x in range(2 * len(outs)):
        first = pl.multiple_of((me ^ x) * head_dim, head_dim)
        outs[x // 2][x % 2] = jnp.concatenate([picked[:, pl.ds(i * width + first, head_dim)] for i in range(PARTS)], axis=1)


def pack_kernel(sizes, meta, b0, b1, b2, b3, send, neg_ids, coef_t, table, qkvu, *refs):
    n, rows, slots = sizes
    pairs = n // 2
    outs = refs[:pairs]
    pick, order_ref, send_row, ids, coef_rows, items, neg_rows, held, sems = refs[pairs:]
    per, chunk, width = items.shape
    wide = outs[0].shape[1]
    head_dim = wide // PARTS
    cell = rows // n
    me = meta[0]
    copies = [
        pltpu.make_async_copy(source, target, sems.at[i])
        for i, (source, target) in enumerate(((neg_ids, ids), (send, send_row), (coef_t, coef_rows), (qkvu, held)))
    ]
    for copy in copies:
        copy.start()
    copies[0].wait()
    item_copies = []
    for j in range(per):
        start = pl.multiple_of((ids[j] // chunk) * chunk, chunk)
        item_copies.append(pltpu.make_async_copy(table.at[pl.ds(start, chunk)], items.at[j], sems.at[4 + j]))
        item_copies[-1].start()
    filled, value = slot_table(meta, (b0, b1, b2, b3), order_ref)
    places = jnp.broadcast_to(slot_places(filled, value, me, cell), (rows, rows))
    lane = iota((rows, rows), 1)
    sub = iota((rows, rows), 0)
    by_rank = one_hot(slot_ranks(places) == lane.astype(F32))
    copies[1].wait()
    home = jnp.sum(jnp.where(lane == sub, send_row[...].astype(F32), 0.0), axis=1, keepdims=True)
    chosen = dot(by_rank, one_hot(home == lane.astype(F32)), ((0,), (0,)))
    pick[...] = chosen.astype(BF16)
    none = jnp.zeros((slots, rows), F32)
    both = jnp.concatenate(
        [jnp.concatenate([chosen[0:slots], none], axis=1), jnp.concatenate([none, chosen[0:slots]], axis=1)], axis=0
    ).astype(BF16)
    copies[2].wait()
    copies[3].wait()
    for j in range(per):
        item_copies[j].wait()
        own = iota((chunk, width), 0) == ids[j] % chunk
        neg_rows[j : j + 1] = jnp.sum(jnp.where(own, items[j].astype(F32), 0.0), axis=0, keepdims=True)
    step = coef_rows.shape[0] * rows // wide
    coefs = jnp.concatenate([coef_rows[b * step : (b + 1) * step].astype(F32) for b in range(wide // rows)], axis=1)
    negs = jnp.concatenate([neg_rows[0:per, b * wide : (b + 1) * wide] for b in range(width // wide)], axis=0)
    below = jnp.concatenate([coefs, negs], axis=0).astype(BF16)
    for d in range(pairs):
        columns = []
        for x in (2 * d, 2 * d + 1):
            first = pl.multiple_of((me ^ x) * head_dim, head_dim)
            columns.append(jnp.concatenate([held[:, pl.ds(i * width + first, head_dim)] for i in range(PARTS)], axis=1))
        outs[d][0 : 2 * slots] = dot(both, jnp.concatenate(columns, axis=0)).astype(BF16)
        outs[d][2 * slots :] = below


def index_kernel(sizes, meta, b0, b1, b2, b3, pick, pick_in, pick_out, home_even, home_odd, live, most, order_ref):
    n, rows, slots, pool = sizes
    cell = rows // n
    live_cap = live.shape[0]
    span = pick_in.shape[1] // n
    me = meta[0]
    filled, value = slot_table(meta, (b0, b1, b2, b3), order_ref)
    lane = iota((rows, rows), 1)
    columns = [slot_places(filled, value, me ^ x, cell) for x in range(n)]
    places = jnp.zeros((rows, rows), F32)
    for x in range(n):
        places = jnp.where(lane == x, columns[x], places)
    ranks = slot_ranks(places)
    count = jnp.sum(jnp.where(places > 0.5, 1.0, 0.0), axis=0, keepdims=True)
    counts = [count[:, x : x + 1] for x in range(n)]
    excess = [c - slots for c in counts] + [counts[2 * d] + counts[2 * d + 1] - pool for d in range(n // 2)]
    most[...] = jnp.broadcast_to(functools.reduce(jnp.maximum, excess), most.shape)

    def placed(x, first, width):
        at = ranks[:, x : x + 1] + first
        hit = jnp.where(at == iota((rows, width), 1).astype(F32), columns[x], 0.0)
        return jnp.sum(hit, axis=0, keepdims=True)

    lines = []
    for x in range(n):
        first = span - slots if x % 2 else 0
        line = placed(x, first, max(span, rows))[:, :span]
        at = iota((1, span), 1)
        lines.append(jnp.where((at >= first) & (at < first + slots), line, 0.0))
    line = jnp.concatenate(lines, axis=1) - 1.0
    pick_in[...] = one_hot(iota((live_cap, line.shape[1]), 0).astype(F32) == line)
    reach = -(-pool // rows) * rows
    for d in range(n // 2):
        line = placed(2 * d, 0.0, reach) + placed(2 * d + 1, counts[2 * d], reach) - 1.0
        hit = one_hot(iota((live_cap, reach), 0).astype(F32) == line)
        pick_out[:, d * pool : (d + 1) * pool] = hit[:, :pool]
    slot = iota((reach, rows), 0).astype(F32)
    home_even[...] = dot(one_hot(slot == lane[0:1].astype(F32)), pick[...]).astype(BF16)[:pool]
    home_odd[...] = dot(one_hot(slot == lane[0:1].astype(F32) + counts[1]), pick[...]).astype(BF16)[:pool]
    live[...] = jnp.where(pair_live(live_cap, starts_of(meta, n)), 1.0 / rows, 0.0)


def pair_live(live_cap, starts):
    row = iota((live_cap, 1), 0)
    col = iota((1, live_cap), 1)
    return (col <= row) & (tile_of(col, starts) > tile_of(row, starts) - SPAN) & (row < starts[-1])


def forward_kernel(sizes, meta, pick, live, w_out, *refs):
    n, rows, slots, per = sizes
    blocks = refs[:n]
    compact, weights, att, stats, coef_c, d_mixed, negatives, neg_rows, w_rows, sem = refs[n:]
    live_cap, head_dim = att.shape
    negs = coef_c.shape[0]
    wide = blocks[0].shape[1]
    span = pick.shape[1] // n
    me = meta[0]
    copy = pltpu.make_async_copy(w_out.at[pl.ds(pl.multiple_of(me * head_dim, head_dim), head_dim)], w_rows, sem)
    copy.start()
    received = [block[2 * slots - span : 2 * slots] if x % 2 else block[0:span] for x, block in enumerate(blocks)]
    both = dot(pick[...], jnp.concatenate(received, axis=0)).astype(BF16)
    compact[...] = both
    total = jnp.zeros((negs, live_cap), F32)
    lane = iota((negs, live_cap), 1)
    step = negs * rows // wide
    for x in range(n):
        t = me ^ x
        start = start_of(meta, n, t)
        below = blocks[x][2 * slots :].astype(F32)
        coefs = jnp.concatenate([below[0:step, b * rows : (b + 1) * rows] for b in range(wide // rows)], axis=0)
        coefs = jnp.concatenate([coefs, jnp.zeros((negs, live_cap - rows), F32)], axis=1)
        total = jnp.where((lane >= start) & (lane < start + meta[LENS + t]), pltpu.roll(coefs, start, 1), total)
        for b in range(n * head_dim // wide):
            neg_rows[t, 0:per, b * wide : (b + 1) * wide] = below[step + b * per : step + (b + 1) * per]
    coef_t = total.astype(BF16)
    coef_c[...] = coef_t
    neg = jnp.concatenate([neg_rows[s, 0:per] for s in range(n)], axis=0).astype(BF16)
    negatives[...] = neg
    head_grad = dot(coef_t, neg, ((0,), (0,))).astype(BF16)
    copy.wait()
    dm = dot(head_grad, w_rows[...], ((1,), (1,)))
    d_mixed[...] = dm
    u, v, q, k = (both[:, i * head_dim : (i + 1) * head_dim] for i in range(PARTS))
    scores = dot(q, k, ((1,), (1,))) * (1.0 / math.sqrt(head_dim))
    sig = jax.nn.sigmoid(scores)
    w = (scores * sig * live[...]).astype(BF16)
    weights[...] = w
    a = dot(w, v)
    att[...] = a
    dn = dm * u.astype(F32)
    mean = jnp.sum(a, axis=1, keepdims=True) * (1.0 / head_dim)
    cen = a - mean
    lane = iota((live_cap, 128), 1)
    cols = jnp.where(lane == 0, mean, 0.0)
    cols = jnp.where(lane == 1, jnp.sum(cen * cen, axis=1, keepdims=True), cols)
    cols = jnp.where(lane == 2, jnp.sum(dn, axis=1, keepdims=True), cols)
    cols = jnp.where(lane == 3, jnp.sum(dn * cen, axis=1, keepdims=True), cols)
    stats[...] = jnp.transpose(cols)[0:8]


def merge_stats(a, b, count):
    gap = b[0] - a[0]
    return (
        (a[0] + b[0]) * 0.5,
        a[1] + b[1] + gap * gap * (0.5 * count),
        a[2] + b[2],
        a[3] + b[3] + (b[2] - a[2]) * gap * 0.5,
    )


def start_of(meta, n, tile):
    start = jnp.int32(0)
    for t in range(n):
        start = start + jnp.where(t < tile, meta[LENS + t], 0)
    return start


def backward_kernel(sizes, meta, compact, weights, att, d_mixed, st0, st1, st2, st3, pick, live, *refs):
    n, rows, pool = sizes
    outs = refs[: n // 2]
    mixed_ref, mixed_rows = refs[n // 2 :]
    live_cap, head_dim = att.shape
    width = head_dim * n
    me = meta[0]
    quad = [[st[i : i + 1] for i in range(4)] for st in (st0, st1, st2, st3)]
    ab = merge_stats(quad[0], quad[1], 2 * head_dim)
    cd = merge_stats(quad[2], quad[3], 2 * head_dim)
    mean, m2, s_dn, s_dna = merge_stats(ab, cd, 4 * head_dim)
    inv = lax.rsqrt(m2 * (1.0 / width) + eps)
    table = jnp.concatenate([mean, inv, s_dn * (1.0 / width), s_dna * inv * (1.0 / width), jnp.zeros((124, live_cap), F32)], axis=0)
    table = jnp.transpose(table)
    mean, inv, mean_dn, mean_dnn = (table[:, i : i + 1] for i in range(4))
    both = compact[...]
    u, v, q, k = (both[:, i * head_dim : (i + 1) * head_dim] for i in range(PARTS))
    u = u.astype(F32)
    dm = d_mixed[...]
    normed = (att[...] - mean) * inv
    mixed = (normed * u).astype(BF16)
    dn = dm * u
    d_att = ((dn - mean_dn - normed * mean_dnn) * inv).astype(BF16)
    scale = 1.0 / math.sqrt(head_dim)
    scores = dot(q, k, ((1,), (1,))) * scale
    sig = jax.nn.sigmoid(scores)
    slope = sig * (1.0 + scores * (1.0 - sig)) * scale * live[...]
    ds = (dot(d_att, v, ((1,), (1,))) * slope).astype(BF16)
    grad = jnp.concatenate(
        [dm * normed, dot(weights[...], d_att, ((0,), (0,))), dot(ds, k), dot(ds, q, ((0,), (0,)))], axis=1
    ).astype(BF16)
    mixed_ref[...] = mixed
    sent = dot(pick[...], grad, ((0,), (0,))).astype(BF16)
    mixed_rows[0:live_cap] = mixed.astype(F32)
    mixed_rows[live_cap:] = jnp.zeros((rows, head_dim), F32)
    quarter = rows // PARTS
    row = iota((rows, head_dim), 0)
    for x in range(n):
        t = me ^ x
        tile = mixed_rows[pl.ds(start_of(meta, n, t), rows), :]
        tile = jnp.where(row < meta[LENS + t], tile, 0.0)
        first = quarter * (x % 2)
        outs[x // 2][first : first + quarter] = jnp.concatenate(
            [tile[b * quarter : (b + 1) * quarter] for b in range(PARTS)], axis=1
        ).astype(BF16)
    for d in range(n // 2):
        outs[d][2 * quarter :] = sent[d * pool : (d + 1) * pool]


def sums_kernel(coef_c, mixed, most, sums):
    negs = coef_c.shape[0]
    sums[0:negs] = dot(coef_c[...], mixed[...])
    sums[negs:] = most[...]


def total_kernel(*refs):
    sums, (total, most) = refs[:-2], refs[-2:]
    negs = total.shape[0]
    total[...] = functools.reduce(jnp.add, [part[0:negs] for part in sums])
    most[...] = functools.reduce(jnp.maximum, [part[negs:] for part in sums])


def finish_kernel(sizes, meta, even, odd, w_out, negatives, total, *refs):
    n, rows, groups = sizes
    blocks, (d_home, layer_out, d_w_out) = refs[:n], refs[n:]
    width = w_out.shape[0]
    head_dim = width // n
    quarter = rows // PARTS
    layer = jnp.zeros((rows, width), F32)
    for d in range(0, n, 2):
        mixed, weights = [], []
        for x in (d, d + 1):
            head = pl.multiple_of((meta[0] ^ x) * head_dim, head_dim)
            block = blocks[x]
            part = dot((odd if x % 2 else even)[...], block[2 * quarter :], ((0,), (0,))).astype(BF16)
            for i in range(PARTS):
                d_home[:, pl.ds(i * width + head, head_dim)] = part[:, i * head_dim : (i + 1) * head_dim]
            lines = block[quarter * (x % 2) : quarter * (x % 2 + 1)]
            mixed.append(jnp.concatenate([lines[:, b * head_dim : (b + 1) * head_dim] for b in range(PARTS)], axis=0))
            weights.append(w_out[pl.ds(head, head_dim), :])
        layer = layer + dot(jnp.concatenate(mixed, axis=1), jnp.concatenate(weights, axis=0))
    layer_out[...] = layer.astype(BF16)
    columns = width // groups
    neg = negatives[:, pl.ds(pl.multiple_of(meta[1] * columns, columns), columns)]
    rest = total[...]
    grad = jnp.zeros((head_dim, columns), F32)
    for _ in range(3):
        piece = rest.astype(BF16)
        grad = grad + dot(piece, neg, ((0,), (0,)))
        rest = rest - piece.astype(F32)
    d_w_out[...] = grad


def kernel_call(body, shapes, specs, scratch=(), limit=40):
    return pl.pallas_call(
        body,
        out_shape=shapes,
        in_specs=specs,
        out_specs=jax.tree.map(lambda _: VMEM, shapes),
        scratch_shapes=scratch,
        compiler_params=pltpu.CompilerParams(vmem_limit_bytes=limit * 1024 * 1024),
    )


def swap(block, axis, distance):
    return lax.ppermute(block, axis, [(i, i ^ distance) for i in range(lax.axis_size(axis))])


def exchange(message, between):
    far = [swap(own, "seq", 2 * d) for d, own in enumerate(message) if d > 0]
    made = between()
    blocks = [message[0], swap(message[0], "seq", 1)]
    for own in far:
        own, made = lax.optimization_barrier((own, made))
        blocks += [own, swap(own, "seq", 1)]
    return blocks, made


def gather_small(block):
    pair = jnp.stack([block, swap(block, "seq", 1)])
    return [pair] + [swap(pair, "seq", d) for d in range(2, lax.axis_size("seq"), 2)]


def head_plan(qkvu, w_out, head_coef, item_table, neg_ids, send_order, recv_order, tile_len):
    n = lax.axis_size("seq")
    groups = lax.axis_size("dp")
    rows = qkvu.shape[0]
    width = w_out.shape[0]
    head_dim = width // HEADS
    negs = head_coef.shape[1]
    per = neg_ids.shape[0]
    wide = PARTS * head_dim
    live_cap = -(-(n * rows // 3) // 128) * 128
    sds = jax.ShapeDtypeStruct
    me = lax.axis_index("seq")
    meta = jnp.concatenate([jnp.stack([me, lax.axis_index("dp")]).astype(jnp.int32), tile_len[0]])
    head_coef_t = head_coef.T

    half = n // 2
    quarter = rows // PARTS
    below = (negs * rows + per * width) // wide

    def passes(slots, pool):
        span = -(-slots // 8) * 8
        orders = gather_small(recv_order)
        *message, pick = kernel_call(
            functools.partial(pack_kernel, (n, rows, slots)),
            (sds((2 * slots + below, wide), BF16),) * half + (sds((rows, rows), BF16),),
            [SMEM] + [VMEM] * 4 + [ANY] * 5,
            [
                pltpu.VMEM((n, 1, rows), F32),
                pltpu.VMEM((1, rows), jnp.int32),
                pltpu.SMEM((per,), jnp.int32),
                pltpu.VMEM((negs, rows), BF16),
                pltpu.VMEM((per, 16, width), BF16),
                pltpu.VMEM((8, width), F32),
                pltpu.VMEM(qkvu.shape, BF16),
                pltpu.SemaphoreType.DMA((4 + per,)),
            ],
        )(meta, *orders, send_order, neg_ids, head_coef_t, item_table, qkvu)

        def index():
            return kernel_call(
                functools.partial(index_kernel, (n, rows, slots, pool)),
                (
                    sds((live_cap, n * span), BF16),
                    sds((live_cap, half * pool), BF16),
                    sds((pool, rows), BF16),
                    sds((pool, rows), BF16),
                    sds((live_cap, live_cap), F32),
                    sds((8, 128), F32),
                ),
                [SMEM] + [VMEM] * 5,
                [pltpu.VMEM((n, 1, rows), F32)],
            )(meta, *orders, pick)

        received, (pick_in, pick_out, even, odd, live, most) = exchange(message, index)
        compact, weights, att, stats, coef_c, d_mixed, negatives = kernel_call(
            functools.partial(forward_kernel, (n, rows, slots, per)),
            (
                sds((live_cap, wide), BF16),
                sds((live_cap, live_cap), BF16),
                sds((live_cap, head_dim), F32),
                sds((8, live_cap), F32),
                sds((negs, live_cap), BF16),
                sds((live_cap, head_dim), F32),
                sds((negs, width), BF16),
            ),
            [SMEM, VMEM, VMEM, ANY] + [VMEM] * n,
            [pltpu.VMEM((n, 8, width), F32), pltpu.VMEM((head_dim, width), BF16), pltpu.SemaphoreType.DMA],
        )(meta, pick_in, live, w_out, *received)
        other = swap(stats, "seq", 1)
        paired = jnp.stack(
            list(merge_stats([stats[i] for i in range(4)], [other[i] for i in range(4)], head_dim))
            + [jnp.zeros_like(stats[0])] * 4
        )
        far = [swap(paired, "seq", d) for d in range(2, n, 2)]
        *back, mixed = kernel_call(
            functools.partial(backward_kernel, (n, rows, pool)),
            (sds((2 * quarter + pool, wide), BF16),) * half + (sds((live_cap, head_dim), BF16),),
            [SMEM] + [VMEM] * 10,
            [pltpu.VMEM((live_cap + rows, head_dim), F32)],
        )(meta, compact, weights, att, d_mixed, paired, *far, pick_out, live)

        def group_sums():
            sums = kernel_call(sums_kernel, sds((negs + 8, head_dim), F32), [VMEM] * 3)(coef_c, mixed, most)
            sums = [sums] + [swap(sums, "dp", d) for d in range(1, groups)]
            total, most_of_all = kernel_call(
                total_kernel, (sds((negs, head_dim), F32), sds((8, 128), F32)), [VMEM] * groups
            )(*sums)
            return total, most_of_all[0, 0] > 0.0

        returned, (total, overflow) = exchange(back, group_sums)
        return overflow, (even, odd, w_out, negatives, total, *returned)

    def finish(*parts):
        return kernel_call(
            functools.partial(finish_kernel, (n, rows, groups)),
            (sds((rows, PARTS * width), BF16), sds((rows, width), BF16), sds((head_dim, width // groups), F32)),
            [SMEM] + [VMEM] * (5 + n),
        )(meta, *parts)

    overflow, parts = passes(SLOTS, POOL)
    d_home, layer_out, d_w_out = lax.cond(overflow, lambda *_: finish(*passes(rows, 2 * rows)[1]), finish, *parts)
    return (layer_out, d_home, d_w_out)


def solution(mesh):
    placed = (
        P(("dp", "seq"), None),
        P(),
        P(("dp", "seq"), None),
        P("seq", None),
        P("seq"),
        P(("dp", "seq"), None),
        P(("dp", "seq"), None),
        P("dp", None),
    )
    return jax.shard_map(
        head_plan if mesh.shape["seq"] == HEADS else tile_plan,
        mesh=mesh,
        in_specs=placed,
        out_specs=(P(("dp", "seq"), None), P(("dp", "seq"), None), P("seq", "dp")),
        check_vma=False,
    )
```

```python
import functools
import math

import jax
import jax.numpy as jnp
from jax import lax
from jax.experimental import pallas as pl
from jax.experimental.pallas import tpu as pltpu
from jax.sharding import PartitionSpec as P

HEADS = 8
SPAN = 3
PARTS = 4
SLOTS = 60
POOL = 104
LENS = 2


eps = 1e-05

VMEM = pl.BlockSpec(memory_space=pltpu.VMEM)
SMEM = pl.BlockSpec(memory_space=pltpu.SMEM)
ANY = pl.BlockSpec(memory_space=pl.ANY)
F32 = jnp.float32
BF16 = jnp.bfloat16


def shifted(block, axis, distance):
    devices = range(lax.axis_size(axis))
    route = [(i - distance, i) for i in devices if i - distance in devices]
    return lax.ppermute(block, axis, route)


def silu_grad(values):
    sigmoid_val = jax.nn.sigmoid(values)
    return sigmoid_val * (1.0 + values * (1.0 - sigmoid_val))


def pair_mask(count, len_p, len_q, allowed, causal):
    positions = jnp.arange(count, dtype=jnp.int32)
    live = (positions[:, None] < len_p) & (positions[None, :] < len_q) & allowed
    if causal:
        live = live & (positions[None, :] <= positions[:, None])
    return jnp.where(live, 1.0, 0.0).astype(jnp.float32)


def head_major(flat, count, head_dim):
    return flat.reshape(count, HEADS, head_dim).transpose(1, 0, 2)


def row_major(heads_first, count, width):
    return heads_first.transpose(1, 0, 2).reshape(count, width)


def tile_plan(qkvu, w_out, head_coef, item_table, neg_ids, send_order, recv_order, tile_len):
    row_count = qkvu.shape[0]
    model_width = w_out.shape[0]
    head_dim = model_width // HEADS
    score_scale = 1.0 / math.sqrt(head_dim)
    send_list = send_order[0]
    recv_list = recv_order[0]
    own_index = lax.axis_index("seq")
    lengths_row = tile_len[0]
    own_len = jnp.take(lengths_row, own_index)
    outgoing = jnp.take(qkvu, send_list, axis=0)
    received = lax.all_to_all(outgoing, "seq", split_axis=0, concat_axis=0, tiled=True)
    balanced = jnp.take(received, recv_list, axis=0)
    neg_all = lax.all_gather(jnp.take(item_table, neg_ids, axis=0), "seq", axis=0, tiled=True)
    u_part = balanced[:, :model_width].astype(jnp.float32)
    value_heads = head_major(balanced[:, model_width : 2 * model_width], row_count, head_dim)
    query_heads = head_major(balanced[:, 2 * model_width : 3 * model_width], row_count, head_dim)
    key_heads = head_major(balanced[:, 3 * model_width :], row_count, head_dim)
    lagged = []
    carried = (value_heads, key_heads)
    for lag in range(1, SPAN):
        carried = shifted((carried[0], carried[1]), "seq", 1)
        lagged.append(carried)
    value_list = [value_heads]
    key_list = [key_heads]
    mask_list = [pair_mask(row_count, own_len, own_len, True, True)]
    for lag in range(1, SPAN):
        earlier_len = jnp.take(lengths_row, jnp.maximum(own_index - lag, 0))
        value_list.append(lagged[lag - 1][0])
        key_list.append(lagged[lag - 1][1])
        mask_list.append(pair_mask(row_count, own_len, earlier_len, own_index >= lag, False))
    values_all = jnp.concatenate(value_list, axis=1)
    keys_all = jnp.concatenate(key_list, axis=1)
    mask_all = jnp.concatenate(mask_list, axis=1)
    scores = (
        jnp.einsum("hpd,hqd->hpq", query_heads, keys_all, preferred_element_type=jnp.float32)
        * score_scale
    )
    weights = (jax.nn.silu(scores) * mask_all[None] / row_count).astype(jnp.bfloat16)
    attended_heads = jnp.einsum(
        "hpq,hqd->hpd", weights, values_all, preferred_element_type=jnp.float32
    )
    attended = row_major(attended_heads, row_count, model_width)
    row_mean = jnp.mean(attended, axis=1, keepdims=True)
    centered = attended - row_mean
    variance = jnp.mean(centered * centered, axis=1, keepdims=True)
    inv_std = lax.rsqrt(variance + eps)
    normed = centered * inv_std
    mixed_rows = (normed * u_part).astype(jnp.bfloat16)
    layer_out = jnp.dot(mixed_rows, w_out, preferred_element_type=jnp.float32).astype(jnp.bfloat16)
    positions = jnp.arange(row_count, dtype=jnp.int32)
    live_col = jnp.where(positions < own_len, 1.0, 0.0).astype(jnp.float32)[:, None]
    coef_live = (head_coef * live_col).astype(jnp.bfloat16)
    head_grad = jnp.dot(coef_live, neg_all, preferred_element_type=jnp.float32).astype(jnp.bfloat16)
    d_mixed = lax.dot_general(
        head_grad, w_out, (((1,), (1,)), ((), ())), preferred_element_type=jnp.float32
    )
    d_u_part = d_mixed * normed
    d_normed = d_mixed * u_part
    d_att = (
        d_normed
        - jnp.mean(d_normed, axis=1, keepdims=True)
        - normed * jnp.mean(d_normed * normed, axis=1, keepdims=True)
    ) * inv_std
    d_att_heads = head_major(d_att.astype(jnp.bfloat16), row_count, head_dim)
    d_weights = jnp.einsum(
        "hpd,hqd->hpq", d_att_heads, values_all, preferred_element_type=jnp.float32
    )
    d_scores = (d_weights * mask_all[None] / row_count * silu_grad(scores) * score_scale).astype(
        jnp.bfloat16
    )
    d_query = jnp.einsum("hpq,hqd->hpd", d_scores, keys_all, preferred_element_type=jnp.float32)
    part_keys = jnp.einsum(
        "hpq,hpd->hqd", d_scores, query_heads, preferred_element_type=jnp.float32
    )
    part_values = jnp.einsum(
        "hpq,hpd->hqd", weights, d_att_heads, preferred_element_type=jnp.float32
    )
    key_grad = part_keys[:, :row_count]
    value_grad = part_values[:, :row_count]
    for lag in range(1, SPAN):
        block_keys = part_keys[:, lag * row_count : (lag + 1) * row_count].astype(jnp.bfloat16)
        block_values = part_values[:, lag * row_count : (lag + 1) * row_count].astype(jnp.bfloat16)
        back_values, back_keys = shifted((block_values, block_keys), "seq", -lag)
        key_grad = key_grad + back_keys.astype(jnp.float32)
        value_grad = value_grad + back_values.astype(jnp.float32)
    tile_grads = jnp.concatenate(
        [
            d_u_part,
            row_major(value_grad, row_count, model_width),
            row_major(d_query, row_count, model_width),
            row_major(key_grad, row_count, model_width),
        ],
        axis=1,
    ).astype(jnp.bfloat16)
    slot_grads = jnp.zeros_like(tile_grads).at[recv_list].set(tile_grads)
    returned = lax.all_to_all(slot_grads, "seq", split_axis=0, concat_axis=0, tiled=True)
    d_home = jnp.zeros_like(returned).at[send_list].set(returned)
    coef_sums = lax.psum_scatter(
        lax.dot_general(
            mixed_rows, coef_live, (((0,), (0,)), ((), ())), preferred_element_type=jnp.float32
        ),
        "seq",
        scatter_dimension=0,
        tiled=True,
    )
    row_grad = jnp.dot(coef_sums, neg_all.astype(jnp.float32), precision=lax.Precision.HIGHEST)
    d_w_out = lax.psum_scatter(
        row_grad.astype(jnp.bfloat16), "dp", scatter_dimension=1, tiled=True
    ).astype(jnp.float32)
    return (layer_out, d_home, d_w_out)


def dot(a, b, dims=((1,), (0,))):
    return lax.dot_general(a, b, (dims, ((), ())), preferred_element_type=F32)


def iota(shape, dim):
    return lax.broadcasted_iota(jnp.int32, shape, dim)


def starts_of(meta, count):
    starts = [jnp.int32(0)]
    for t in range(count):
        starts.append(starts[-1] + meta[LENS + t])
    return starts


def tile_of(position, starts):
    tile = jnp.zeros(position.shape, jnp.int32)
    for start in starts[1:-1]:
        tile = tile + jnp.where(position >= start, 1, 0)
    return tile


def one_hot(condition):
    return jnp.where(condition, 1.0, 0.0).astype(BF16)


def slot_table(meta, blocks, order_ref):
    n, _, rows = order_ref.shape
    cell = rows // n
    for b in range(n):
        order_ref[meta[0] ^ b] = blocks[b // (n // 2)][b % (n // 2)].astype(F32)
    starts = starts_of(meta, n)
    pos = iota((cell, rows), 1)
    filled = [jnp.broadcast_to(order_ref[t], (cell, rows)) for t in range(n)]
    value = [jnp.where(pos < meta[LENS + t], pos + starts[t] + 1, 0).astype(F32) for t in range(n)]
    return jnp.concatenate(filled, axis=0), jnp.concatenate(value, axis=0)


def slot_places(filled, value, source, cell):
    slot = (iota(filled.shape, 0) % cell + source * cell).astype(F32)
    return jnp.sum(jnp.where(filled == slot, value, 0.0), axis=1, keepdims=True)


def slot_ranks(places):
    rows = places.shape[0]
    live = places > 0.5
    before = dot(one_hot(iota((rows, rows), 1) < iota((rows, rows), 0)), one_hot(live))
    return jnp.where(live, before, -1.0)


def put_rows(me, head_dim, picked, outs):
    width = picked.shape[1] // PARTS
    for x in range(2 * len(outs)):
        first = pl.multiple_of((me ^ x) * head_dim, head_dim)
        outs[x // 2][x % 2] = jnp.concatenate([picked[:, pl.ds(i * width + first, head_dim)] for i in range(PARTS)], axis=1)


def prep_kernel(ids, send, coef_t, table, qkvu, held, below, home, send_row, coef_rows, items, neg_rows, sems):
    per, chunk, width = items.shape
    rows = send_row.shape[1]
    wide = below.shape[1]
    copies = [
        pltpu.make_async_copy(source, target, sems.at[i])
        for i, (source, target) in enumerate(((send, send_row), (coef_t, coef_rows), (qkvu, held)))
    ]
    for j in range(per):
        start = pl.multiple_of((ids[j] // chunk) * chunk, chunk)
        copies.append(pltpu.make_async_copy(table.at[pl.ds(start, chunk)], items.at[j], sems.at[3 + j]))
    for copy in copies:
        copy.start()
    lane = iota((rows, rows), 1)
    copies[0].wait()
    own = jnp.where(lane == iota((rows, rows), 0), send_row[...].astype(F32), 0.0)
    home[...] = one_hot(jnp.sum(own, axis=1, keepdims=True) == lane.astype(F32))
    copies[1].wait()
    for j in range(per):
        copies[3 + j].wait()
        own = iota((chunk, width), 0) == ids[j] % chunk
        neg_rows[j : j + 1] = jnp.sum(jnp.where(own, items[j].astype(F32), 0.0), axis=0, keepdims=True)
    step = coef_rows.shape[0] * rows // wide
    coefs = jnp.concatenate([coef_rows[b * step : (b + 1) * step].astype(F32) for b in range(wide // rows)], axis=1)
    negs = jnp.concatenate([neg_rows[0:per, b * wide : (b + 1) * wide] for b in range(width // wide)], axis=0)
    below[...] = jnp.concatenate([coefs, negs], axis=0).astype(BF16)
    copies[2].wait()


def pack_kernel(sizes, meta, b0, b1, held, below, home, *refs):
    n, rows, slots = sizes
    pairs = n // 2
    outs = refs[:pairs]
    pick, order_ref = refs[pairs:]
    head_dim = outs[0].shape[1] // PARTS
    width = head_dim * n
    cell = rows // n
    me = meta[0]
    filled, value = slot_table(meta, (b0, b1), order_ref)
    places = jnp.broadcast_to(slot_places(filled, value, me, cell), (rows, rows))
    by_rank = one_hot(slot_ranks(places) == iota((rows, rows), 1).astype(F32))
    chosen = dot(by_rank, home[...], ((0,), (0,)))
    pick[...] = chosen.astype(BF16)
    none = jnp.zeros((slots, rows), F32)
    both = jnp.concatenate(
        [jnp.concatenate([chosen[0:slots], none], axis=1), jnp.concatenate([none, chosen[0:slots]], axis=1)], axis=0
    ).astype(BF16)
    for d in range(pairs):
        columns = []
        for x in (2 * d, 2 * d + 1):
            first = pl.multiple_of((me ^ x) * head_dim, head_dim)
            columns.append(jnp.concatenate([held[:, pl.ds(i * width + first, head_dim)] for i in range(PARTS)], axis=1))
        outs[d][0 : 2 * slots] = dot(both, jnp.concatenate(columns, axis=0)).astype(BF16)
        outs[d][2 * slots :] = below[...]


def index_kernel(sizes, meta, b0, b1, pick, w_out, pick_in, pick_out, home_even, home_odd, live, most, w_cols, order_ref, w_rows, sem):
    n, rows, slots, pool = sizes
    cell = rows // n
    live_cap = live.shape[0]
    head_dim = w_rows.shape[0]
    copy = pltpu.make_async_copy(w_out.at[pl.ds(pl.multiple_of(meta[0] * head_dim, head_dim), head_dim)], w_rows, sem)
    copy.start()
    span = pick_in.shape[1] // n
    me = meta[0]
    filled, value = slot_table(meta, (b0, b1), order_ref)
    lane = iota((rows, rows), 1)
    columns = [slot_places(filled, value, me ^ x, cell) for x in range(n)]
    places = jnp.zeros((rows, rows), F32)
    for x in range(n):
        places = jnp.where(lane == x, columns[x], places)
    ranks = slot_ranks(places)
    count = jnp.sum(jnp.where(places > 0.5, 1.0, 0.0), axis=0, keepdims=True)
    counts = [count[:, x : x + 1] for x in range(n)]
    excess = [c - slots for c in counts] + [counts[2 * d] + counts[2 * d + 1] - pool for d in range(n // 2)]
    most[...] = jnp.broadcast_to(functools.reduce(jnp.maximum, excess), most.shape)

    def placed(x, first, width):
        at = ranks[:, x : x + 1] + first
        hit = jnp.where(at == iota((rows, width), 1).astype(F32), columns[x], 0.0)
        return jnp.sum(hit, axis=0, keepdims=True)

    lines = []
    for x in range(n):
        first = span - slots if x % 2 else 0
        line = placed(x, first, max(span, rows))[:, :span]
        at = iota((1, span), 1)
        lines.append(jnp.where((at >= first) & (at < first + slots), line, 0.0))
    line = jnp.concatenate(lines, axis=1) - 1.0
    pick_in[...] = one_hot(iota((live_cap, line.shape[1]), 0).astype(F32) == line)
    reach = -(-pool // rows) * rows
    for d in range(n // 2):
        line = placed(2 * d, 0.0, reach) + placed(2 * d + 1, counts[2 * d], reach) - 1.0
        hit = one_hot(iota((live_cap, reach), 0).astype(F32) == line)
        pick_out[d * pool : (d + 1) * pool] = jnp.transpose(hit.astype(F32))[:pool].astype(BF16)
    slot = iota((reach, rows), 0).astype(F32)
    for home, first in ((home_even, jnp.zeros((1, 1), F32)), (home_odd, counts[1])):
        moved = dot(one_hot(slot == lane[0:1].astype(F32) + first), pick[...])
        home[...] = moved[:pool].astype(BF16)
    copy.wait()
    w_cols[...] = jnp.transpose(w_rows[...].astype(F32)).astype(BF16)
    live[...] = jnp.where(pair_live(live_cap, starts_of(meta, n)), 1.0 / rows, 0.0)


def pair_live(live_cap, starts):
    row = iota((live_cap, 1), 0)
    col = iota((1, live_cap), 1)
    return (col <= row) & (tile_of(col, starts) > tile_of(row, starts) - SPAN) & (row < starts[-1])


def forward_kernel(sizes, meta, pick, live, w_cols, *refs):
    n, rows, slots, per = sizes
    blocks = refs[:n]
    compact, weights, att, stats, coef_c, d_mixed, negatives, neg_rows = refs[n:]
    live_cap, head_dim = att.shape
    negs = coef_c.shape[0]
    wide = blocks[0].shape[1]
    span = pick.shape[1] // n
    me = meta[0]
    received = [block[2 * slots - span : 2 * slots] if x % 2 else block[0:span] for x, block in enumerate(blocks)]
    both = dot(pick[...], jnp.concatenate(received, axis=0)).astype(BF16)
    compact[...] = both
    total = jnp.zeros((negs, live_cap), F32)
    lane = iota((negs, live_cap), 1)
    step = negs * rows // wide
    for x in range(n):
        t = me ^ x
        start = start_of(meta, n, t)
        below = blocks[x][2 * slots :].astype(F32)
        coefs = jnp.concatenate([below[0:step, b * rows : (b + 1) * rows] for b in range(wide // rows)], axis=0)
        coefs = jnp.concatenate([coefs, jnp.zeros((negs, live_cap - rows), F32)], axis=1)
        total = jnp.where((lane >= start) & (lane < start + meta[LENS + t]), pltpu.roll(coefs, start, 1), total)
        for b in range(n * head_dim // wide):
            neg_rows[t, 0:per, b * wide : (b + 1) * wide] = below[step + b * per : step + (b + 1) * per]
    coef_t = total.astype(BF16)
    coef_c[...] = coef_t
    neg = jnp.concatenate([neg_rows[s, 0:per] for s in range(n)], axis=0).astype(BF16)
    negatives[...] = neg
    head_grad = dot(coef_t, neg, ((0,), (0,))).astype(BF16)
    dm = dot(head_grad, w_cols[...])
    d_mixed[...] = dm
    u, v, q, k = (both[:, i * head_dim : (i + 1) * head_dim] for i in range(PARTS))
    scores = dot(q, k, ((1,), (1,))) * (1.0 / math.sqrt(head_dim))
    sig = jax.nn.sigmoid(scores)
    w = (scores * sig * live[...]).astype(BF16)
    weights[...] = w
    a = dot(w, v)
    att[...] = a
    dn = dm * u.astype(F32)
    mean = jnp.sum(a, axis=1, keepdims=True) * (1.0 / head_dim)
    cen = a - mean
    lane = iota((live_cap, 128), 1)
    cols = jnp.where(lane == 0, mean, 0.0)
    cols = jnp.where(lane == 1, jnp.sum(cen * cen, axis=1, keepdims=True), cols)
    cols = jnp.where(lane == 2, jnp.sum(dn, axis=1, keepdims=True), cols)
    cols = jnp.where(lane == 3, jnp.sum(dn * cen, axis=1, keepdims=True), cols)
    stats[...] = jnp.transpose(cols)[0:8]


def merge_stats(a, b, count):
    gap = b[0] - a[0]
    return (
        (a[0] + b[0]) * 0.5,
        a[1] + b[1] + gap * gap * (0.5 * count),
        a[2] + b[2],
        a[3] + b[3] + (b[2] - a[2]) * gap * 0.5,
    )


def start_of(meta, n, tile):
    start = jnp.int32(0)
    for t in range(n):
        start = start + jnp.where(t < tile, meta[LENS + t], 0)
    return start


def backward_kernel(sizes, meta, compact, weights, att, d_mixed, st0, st1, st2, st3, pick, live, *refs):
    n, rows, pool = sizes
    outs = refs[: n // 2]
    mixed_ref, mixed_rows = refs[n // 2 :]
    live_cap, head_dim = att.shape
    width = head_dim * n
    me = meta[0]
    quad = [[st[i : i + 1] for i in range(4)] for st in (st0, st1, st2, st3)]
    ab = merge_stats(quad[0], quad[1], 2 * head_dim)
    cd = merge_stats(quad[2], quad[3], 2 * head_dim)
    mean, m2, s_dn, s_dna = merge_stats(ab, cd, 4 * head_dim)
    inv = lax.rsqrt(m2 * (1.0 / width) + eps)
    table = jnp.concatenate([mean, inv, s_dn * (1.0 / width), s_dna * inv * (1.0 / width), jnp.zeros((124, live_cap), F32)], axis=0)
    table = jnp.transpose(table)
    mean, inv, mean_dn, mean_dnn = (table[:, i : i + 1] for i in range(4))
    both = compact[...]
    u, v, q, k = (both[:, i * head_dim : (i + 1) * head_dim] for i in range(PARTS))
    u = u.astype(F32)
    dm = d_mixed[...]
    normed = (att[...] - mean) * inv
    mixed = (normed * u).astype(BF16)
    dn = dm * u
    d_att = ((dn - mean_dn - normed * mean_dnn) * inv).astype(BF16)
    scale = 1.0 / math.sqrt(head_dim)
    scores = dot(q, k, ((1,), (1,))) * scale
    sig = jax.nn.sigmoid(scores)
    slope = sig * (1.0 + scores * (1.0 - sig)) * scale * live[...]
    ds = (dot(d_att, v, ((1,), (1,))) * slope).astype(BF16)
    grad = jnp.concatenate(
        [dm * normed, dot(weights[...], d_att, ((0,), (0,))), dot(ds, k), dot(ds, q, ((0,), (0,)))], axis=1
    ).astype(BF16)
    mixed_ref[...] = mixed
    sent = dot(pick[...], grad).astype(BF16)
    mixed_rows[0:live_cap] = mixed.astype(F32)
    mixed_rows[live_cap:] = jnp.zeros((rows, head_dim), F32)
    quarter = rows // PARTS
    row = iota((rows, head_dim), 0)
    for x in range(n):
        t = me ^ x
        tile = mixed_rows[pl.ds(start_of(meta, n, t), rows), :]
        tile = jnp.where(row < meta[LENS + t], tile, 0.0)
        first = quarter * (x % 2)
        outs[x // 2][first : first + quarter] = jnp.concatenate(
            [tile[b * quarter : (b + 1) * quarter] for b in range(PARTS)], axis=1
        ).astype(BF16)
    for d in range(n // 2):
        outs[d][2 * quarter :] = sent[d * pool : (d + 1) * pool]


def sums_kernel(coef_c, mixed, most, sums):
    negs = coef_c.shape[0]
    sums[0:negs] = dot(coef_c[...], mixed[...])
    sums[negs:] = most[...]


def total_kernel(meta, even, odd, negatives, w_out, *refs):
    sums, (d_w_out, most, kit, sem) = refs[:-4], refs[-4:]
    width = w_out.shape[0]
    copy = pltpu.make_async_copy(w_out, kit.at[pl.ds(0, width)], sem)
    copy.start()
    pool, rows = even.shape
    kit[width : width + pool, 0:rows] = even[...]
    kit[width : width + pool, rows : 2 * rows] = odd[...]
    negs, groups = negatives.shape[0], len(sums)
    most[...] = functools.reduce(jnp.maximum, [part[negs:] for part in sums])
    rest = functools.reduce(jnp.add, [part[0:negs] for part in sums])
    columns = width // groups
    neg = negatives[:, pl.ds(pl.multiple_of(meta[1] * columns, columns), columns)]
    grad = jnp.zeros((rest.shape[1], columns), F32)
    for _ in range(3):
        piece = rest.astype(BF16)
        grad = grad + dot(piece, neg, ((0,), (0,)))
        rest = rest - piece.astype(F32)
    d_w_out[...] = grad
    copy.wait()


def finish_kernel(sizes, meta, kit, *refs):
    n, rows = sizes
    blocks, (d_home, layer_out) = refs[:n], refs[n:]
    width = kit.shape[1]
    head_dim = width // n
    quarter = rows // PARTS
    layer = jnp.zeros((rows, width), F32)
    for d in range(0, n, 2):
        mixed, weights = [], []
        for x in (d, d + 1):
            head = pl.multiple_of((meta[0] ^ x) * head_dim, head_dim)
            block = blocks[x]
            pick = kit[width : width + block.shape[0] - 2 * quarter, rows * (x % 2) : rows * (x % 2 + 1)]
            part = dot(pick, block[2 * quarter :], ((0,), (0,))).astype(BF16)
            for i in range(PARTS):
                d_home[:, pl.ds(i * width + head, head_dim)] = part[:, i * head_dim : (i + 1) * head_dim]
            lines = block[quarter * (x % 2) : quarter * (x % 2 + 1)]
            mixed.append(jnp.concatenate([lines[:, b * head_dim : (b + 1) * head_dim] for b in range(PARTS)], axis=0))
            weights.append(kit[pl.ds(head, head_dim), :])
        layer = layer + dot(jnp.concatenate(mixed, axis=1), jnp.concatenate(weights, axis=0))
    layer_out[...] = layer.astype(BF16)


def kernel_call(body, shapes, specs, scratch=(), limit=40):
    return pl.pallas_call(
        body,
        out_shape=shapes,
        in_specs=specs,
        out_specs=jax.tree.map(lambda _: VMEM, shapes),
        scratch_shapes=scratch,
        compiler_params=pltpu.CompilerParams(vmem_limit_bytes=limit * 1024 * 1024),
    )


def swap(block, axis, distance):
    return lax.ppermute(block, axis, [(i, i ^ distance) for i in range(lax.axis_size(axis))])


def exchange(message, between):
    far = [swap(own, "seq", 2 * d) for d, own in enumerate(message) if d > 0]
    made = between()
    blocks = [message[0], swap(message[0], "seq", 1)]
    for d, own in enumerate(far):
        if d == len(far) - 1:
            own, made = lax.optimization_barrier((own, made))
        blocks += [own, swap(own, "seq", 1)]
    return blocks, made


def gather_small(block, between):
    n = lax.axis_size("seq")
    known, distance = block[None], 1
    while distance < n // 2:
        known = jnp.concatenate([known, swap(known, "seq", distance)], axis=0)
        distance *= 2
    known, made = lax.optimization_barrier((known, between()))
    return [known, swap(known, "seq", distance)], made


def head_plan(qkvu, w_out, head_coef, item_table, neg_ids, send_order, recv_order, tile_len):
    n = lax.axis_size("seq")
    groups = lax.axis_size("dp")
    rows = qkvu.shape[0]
    width = w_out.shape[0]
    head_dim = width // HEADS
    negs = head_coef.shape[1]
    per = neg_ids.shape[0]
    wide = PARTS * head_dim
    live_cap = -(-(n * rows // 3) // 128) * 128
    sds = jax.ShapeDtypeStruct
    me = lax.axis_index("seq")
    meta = jnp.concatenate([jnp.stack([me, lax.axis_index("dp")]).astype(jnp.int32), tile_len[0]])
    head_coef_t = head_coef.T

    half = n // 2
    quarter = rows // PARTS
    below = (negs * rows + per * width) // wide

    def passes(slots, pool):
        span = -(-slots // 8) * 8
        def prep():
            return kernel_call(
                prep_kernel,
                (sds(qkvu.shape, BF16), sds((below, wide), BF16), sds((rows, rows), BF16)),
                [SMEM] + [ANY] * 4,
                [
                    pltpu.VMEM((1, rows), jnp.int32),
                    pltpu.VMEM((negs, rows), BF16),
                    pltpu.VMEM((per, 16, width), BF16),
                    pltpu.VMEM((8, width), F32),
                    pltpu.SemaphoreType.DMA((3 + per,)),
                ],
            )(neg_ids, send_order, head_coef_t, item_table, qkvu)

        orders, prepared = gather_small(recv_order, prep)
        *message, pick = kernel_call(
            functools.partial(pack_kernel, (n, rows, slots)),
            (sds((2 * slots + below, wide), BF16),) * half + (sds((rows, rows), BF16),),
            [SMEM] + [VMEM] * 5,
            [pltpu.VMEM((n, 1, rows), F32)],
        )(meta, *orders, *prepared)

        def index():
            return kernel_call(
                functools.partial(index_kernel, (n, rows, slots, pool)),
                (
                    sds((live_cap, n * span), BF16),
                    sds((half * pool, live_cap), BF16),
                    sds((pool, rows), BF16),
                    sds((pool, rows), BF16),
                    sds((live_cap, live_cap), F32),
                    sds((8, 128), F32),
                    sds((width, head_dim), BF16),
                ),
                [SMEM] + [VMEM] * 3 + [ANY],
                [pltpu.VMEM((n, 1, rows), F32), pltpu.VMEM((head_dim, width), BF16), pltpu.SemaphoreType.DMA],
            )(meta, *orders, pick, w_out)

        received, (pick_in, pick_out, even, odd, live, most, w_cols) = exchange(message, index)
        compact, weights, att, stats, coef_c, d_mixed, negatives = kernel_call(
            functools.partial(forward_kernel, (n, rows, slots, per)),
            (
                sds((live_cap, wide), BF16),
                sds((live_cap, live_cap), BF16),
                sds((live_cap, head_dim), F32),
                sds((8, live_cap), F32),
                sds((negs, live_cap), BF16),
                sds((live_cap, head_dim), F32),
                sds((negs, width), BF16),
            ),
            [SMEM] + [VMEM] * (3 + n),
            [pltpu.VMEM((n, 8, width), F32)],
        )(meta, pick_in, live, w_cols, *received)
        paired = merge_stats(stats, swap(stats, "seq", 1), head_dim)
        paired = jnp.stack(list(paired) + [jnp.zeros_like(stats[0])] * 4)
        far = [swap(paired, "seq", d) for d in range(2, n, 2)]
        *back, mixed = kernel_call(
            functools.partial(backward_kernel, (n, rows, pool)),
            (sds((2 * quarter + pool, wide), BF16),) * half + (sds((live_cap, head_dim), BF16),),
            [SMEM] + [VMEM] * 10,
            [pltpu.VMEM((live_cap + rows, head_dim), F32)],
        )(meta, compact, weights, att, d_mixed, paired, *far, pick_out, live)

        def group_sums():
            sums = kernel_call(sums_kernel, sds((negs + 8, head_dim), F32), [VMEM] * 3)(coef_c, mixed, most)
            sums = [sums] + [swap(sums, "dp", d) for d in range(1, groups)]
            d_w, most_of_all, kit = kernel_call(
                total_kernel,
                (sds((head_dim, width // groups), F32), sds((8, 128), F32), sds((width + -(-pool // 16) * 16, width), BF16)),
                [SMEM] + [VMEM] * 3 + [ANY] + [VMEM] * groups,
                [pltpu.SemaphoreType.DMA],
            )(meta, even, odd, negatives, w_out, *sums)
            return d_w, kit, most_of_all

        returned, (d_w, kit, most_of_all) = exchange(back, group_sums)
        return most_of_all[0, 0] > 0.0, (d_w, kit, *returned)

    def finish(d_w, *parts):
        outs = kernel_call(
            functools.partial(finish_kernel, (n, rows)),
            (sds((rows, PARTS * width), BF16), sds((rows, width), BF16)),
            [SMEM] + [VMEM] * (1 + n),
        )(meta, *parts)
        return (*outs, d_w)

    overflow, parts = passes(SLOTS, POOL)
    d_home, layer_out, d_w_out = lax.cond(
        overflow, lambda *_: finish(*passes(rows, 2 * rows)[1]), lambda *outs: outs, *finish(*parts)
    )
    return (layer_out, d_home, d_w_out)


def solution(mesh):
    placed = (
        P(("dp", "seq"), None),
        P(),
        P(("dp", "seq"), None),
        P("seq", None),
        P("seq"),
        P(("dp", "seq"), None),
        P(("dp", "seq"), None),
        P("dp", None),
    )
    return jax.shard_map(
        head_plan if mesh.shape["seq"] == HEADS else tile_plan,
        mesh=mesh,
        in_specs=placed,
        out_specs=(P(("dp", "seq"), None), P(("dp", "seq"), None), P("seq", "dp")),
        check_vma=False,
    )
```

```python
import functools
import math

import jax
import jax.numpy as jnp
from jax import lax
from jax.experimental import pallas as pl
from jax.experimental.pallas import tpu as pltpu
from jax.sharding import PartitionSpec as P

HEADS = 8
SPAN = 3
PARTS = 4
SLOTS = 60
POOL = 104
LENS = 2


eps = 1e-05

VMEM = pl.BlockSpec(memory_space=pltpu.VMEM)
SMEM = pl.BlockSpec(memory_space=pltpu.SMEM)
ANY = pl.BlockSpec(memory_space=pl.ANY)
F32 = jnp.float32
BF16 = jnp.bfloat16


def shifted(block, axis, distance):
    devices = range(lax.axis_size(axis))
    route = [(i - distance, i) for i in devices if i - distance in devices]
    return lax.ppermute(block, axis, route)


def silu_grad(values):
    sigmoid_val = jax.nn.sigmoid(values)
    return sigmoid_val * (1.0 + values * (1.0 - sigmoid_val))


def pair_mask(count, len_p, len_q, allowed, causal):
    positions = jnp.arange(count, dtype=jnp.int32)
    live = (positions[:, None] < len_p) & (positions[None, :] < len_q) & allowed
    if causal:
        live = live & (positions[None, :] <= positions[:, None])
    return jnp.where(live, 1.0, 0.0).astype(jnp.float32)


def head_major(flat, count, head_dim):
    return flat.reshape(count, HEADS, head_dim).transpose(1, 0, 2)


def row_major(heads_first, count, width):
    return heads_first.transpose(1, 0, 2).reshape(count, width)


def tile_plan(qkvu, w_out, head_coef, item_table, neg_ids, send_order, recv_order, tile_len):
    row_count = qkvu.shape[0]
    model_width = w_out.shape[0]
    head_dim = model_width // HEADS
    score_scale = 1.0 / math.sqrt(head_dim)
    send_list = send_order[0]
    recv_list = recv_order[0]
    own_index = lax.axis_index("seq")
    lengths_row = tile_len[0]
    own_len = jnp.take(lengths_row, own_index)
    outgoing = jnp.take(qkvu, send_list, axis=0)
    received = lax.all_to_all(outgoing, "seq", split_axis=0, concat_axis=0, tiled=True)
    balanced = jnp.take(received, recv_list, axis=0)
    neg_all = lax.all_gather(jnp.take(item_table, neg_ids, axis=0), "seq", axis=0, tiled=True)
    u_part = balanced[:, :model_width].astype(jnp.float32)
    value_heads = head_major(balanced[:, model_width : 2 * model_width], row_count, head_dim)
    query_heads = head_major(balanced[:, 2 * model_width : 3 * model_width], row_count, head_dim)
    key_heads = head_major(balanced[:, 3 * model_width :], row_count, head_dim)
    lagged = []
    carried = (value_heads, key_heads)
    for lag in range(1, SPAN):
        carried = shifted((carried[0], carried[1]), "seq", 1)
        lagged.append(carried)
    value_list = [value_heads]
    key_list = [key_heads]
    mask_list = [pair_mask(row_count, own_len, own_len, True, True)]
    for lag in range(1, SPAN):
        earlier_len = jnp.take(lengths_row, jnp.maximum(own_index - lag, 0))
        value_list.append(lagged[lag - 1][0])
        key_list.append(lagged[lag - 1][1])
        mask_list.append(pair_mask(row_count, own_len, earlier_len, own_index >= lag, False))
    values_all = jnp.concatenate(value_list, axis=1)
    keys_all = jnp.concatenate(key_list, axis=1)
    mask_all = jnp.concatenate(mask_list, axis=1)
    scores = (
        jnp.einsum("hpd,hqd->hpq", query_heads, keys_all, preferred_element_type=jnp.float32)
        * score_scale
    )
    weights = (jax.nn.silu(scores) * mask_all[None] / row_count).astype(jnp.bfloat16)
    attended_heads = jnp.einsum(
        "hpq,hqd->hpd", weights, values_all, preferred_element_type=jnp.float32
    )
    attended = row_major(attended_heads, row_count, model_width)
    row_mean = jnp.mean(attended, axis=1, keepdims=True)
    centered = attended - row_mean
    variance = jnp.mean(centered * centered, axis=1, keepdims=True)
    inv_std = lax.rsqrt(variance + eps)
    normed = centered * inv_std
    mixed_rows = (normed * u_part).astype(jnp.bfloat16)
    layer_out = jnp.dot(mixed_rows, w_out, preferred_element_type=jnp.float32).astype(jnp.bfloat16)
    positions = jnp.arange(row_count, dtype=jnp.int32)
    live_col = jnp.where(positions < own_len, 1.0, 0.0).astype(jnp.float32)[:, None]
    coef_live = (head_coef * live_col).astype(jnp.bfloat16)
    head_grad = jnp.dot(coef_live, neg_all, preferred_element_type=jnp.float32).astype(jnp.bfloat16)
    d_mixed = lax.dot_general(
        head_grad, w_out, (((1,), (1,)), ((), ())), preferred_element_type=jnp.float32
    )
    d_u_part = d_mixed * normed
    d_normed = d_mixed * u_part
    d_att = (
        d_normed
        - jnp.mean(d_normed, axis=1, keepdims=True)
        - normed * jnp.mean(d_normed * normed, axis=1, keepdims=True)
    ) * inv_std
    d_att_heads = head_major(d_att.astype(jnp.bfloat16), row_count, head_dim)
    d_weights = jnp.einsum(
        "hpd,hqd->hpq", d_att_heads, values_all, preferred_element_type=jnp.float32
    )
    d_scores = (d_weights * mask_all[None] / row_count * silu_grad(scores) * score_scale).astype(
        jnp.bfloat16
    )
    d_query = jnp.einsum("hpq,hqd->hpd", d_scores, keys_all, preferred_element_type=jnp.float32)
    part_keys = jnp.einsum(
        "hpq,hpd->hqd", d_scores, query_heads, preferred_element_type=jnp.float32
    )
    part_values = jnp.einsum(
        "hpq,hpd->hqd", weights, d_att_heads, preferred_element_type=jnp.float32
    )
    key_grad = part_keys[:, :row_count]
    value_grad = part_values[:, :row_count]
    for lag in range(1, SPAN):
        block_keys = part_keys[:, lag * row_count : (lag + 1) * row_count].astype(jnp.bfloat16)
        block_values = part_values[:, lag * row_count : (lag + 1) * row_count].astype(jnp.bfloat16)
        back_values, back_keys = shifted((block_values, block_keys), "seq", -lag)
        key_grad = key_grad + back_keys.astype(jnp.float32)
        value_grad = value_grad + back_values.astype(jnp.float32)
    tile_grads = jnp.concatenate(
        [
            d_u_part,
            row_major(value_grad, row_count, model_width),
            row_major(d_query, row_count, model_width),
            row_major(key_grad, row_count, model_width),
        ],
        axis=1,
    ).astype(jnp.bfloat16)
    slot_grads = jnp.zeros_like(tile_grads).at[recv_list].set(tile_grads)
    returned = lax.all_to_all(slot_grads, "seq", split_axis=0, concat_axis=0, tiled=True)
    d_home = jnp.zeros_like(returned).at[send_list].set(returned)
    coef_sums = lax.psum_scatter(
        lax.dot_general(
            mixed_rows, coef_live, (((0,), (0,)), ((), ())), preferred_element_type=jnp.float32
        ),
        "seq",
        scatter_dimension=0,
        tiled=True,
    )
    row_grad = jnp.dot(coef_sums, neg_all.astype(jnp.float32), precision=lax.Precision.HIGHEST)
    d_w_out = lax.psum_scatter(
        row_grad.astype(jnp.bfloat16), "dp", scatter_dimension=1, tiled=True
    ).astype(jnp.float32)
    return (layer_out, d_home, d_w_out)


def dot(a, b, dims=((1,), (0,))):
    return lax.dot_general(a, b, (dims, ((), ())), preferred_element_type=F32)


def iota(shape, dim):
    return lax.broadcasted_iota(jnp.int32, shape, dim)


def starts_of(meta, count):
    starts = [jnp.int32(0)]
    for t in range(count):
        starts.append(starts[-1] + meta[LENS + t])
    return starts


def tile_of(position, starts):
    tile = jnp.zeros(position.shape, jnp.int32)
    for start in starts[1:-1]:
        tile = tile + jnp.where(position >= start, 1, 0)
    return tile


def one_hot(condition):
    return jnp.where(condition, 1.0, 0.0).astype(BF16)


def slot_table(meta, blocks, order_ref):
    n, _, rows = order_ref.shape
    cell = rows // n
    for b in range(n):
        order_ref[meta[0] ^ b] = blocks[b // (n // 2)][b % (n // 2) : b % (n // 2) + 1].astype(F32)
    starts = starts_of(meta, n)
    pos = iota((cell, rows), 1)
    filled = [jnp.broadcast_to(order_ref[t], (cell, rows)) for t in range(n)]
    value = [jnp.where(pos < meta[LENS + t], pos + starts[t] + 1, 0).astype(F32) for t in range(n)]
    return jnp.concatenate(filled, axis=0), jnp.concatenate(value, axis=0)


def slot_places(filled, value, source, cell):
    slot = (iota(filled.shape, 0) % cell + source * cell).astype(F32)
    return jnp.sum(jnp.where(filled == slot, value, 0.0), axis=1, keepdims=True)


def slot_ranks(places):
    rows = places.shape[0]
    live = places > 0.5
    before = dot(one_hot(iota((rows, rows), 1) < iota((rows, rows), 0)), one_hot(live))
    return jnp.where(live, before, -1.0)


def put_rows(me, head_dim, picked, outs):
    width = picked.shape[1] // PARTS
    for x in range(2 * len(outs)):
        first = pl.multiple_of((me ^ x) * head_dim, head_dim)
        outs[x // 2][x % 2] = jnp.concatenate([picked[:, pl.ds(i * width + first, head_dim)] for i in range(PARTS)], axis=1)


def prep_kernel(ids, send, coef_t, table, qkvu, held, below, home, send_row, coef_rows, items, neg_rows, sems):
    per, chunk, width = items.shape
    rows = send_row.shape[1]
    wide = below.shape[1]
    copies = [
        pltpu.make_async_copy(source, target, sems.at[i])
        for i, (source, target) in enumerate(((send, send_row), (coef_t, coef_rows), (qkvu, held)))
    ]
    for j in range(per):
        start = pl.multiple_of((ids[j] // chunk) * chunk, chunk)
        copies.append(pltpu.make_async_copy(table.at[pl.ds(start, chunk)], items.at[j], sems.at[3 + j]))
    for copy in copies:
        copy.start()
    lane = iota((rows, rows), 1)
    copies[0].wait()
    own = jnp.where(lane == iota((rows, rows), 0), send_row[...].astype(F32), 0.0)
    home[...] = one_hot(jnp.sum(own, axis=1, keepdims=True) == lane.astype(F32))
    copies[1].wait()
    for j in range(per):
        copies[3 + j].wait()
        own = iota((chunk, width), 0) == ids[j] % chunk
        neg_rows[j : j + 1] = jnp.sum(jnp.where(own, items[j].astype(F32), 0.0), axis=0, keepdims=True)
    step = coef_rows.shape[0] * rows // wide
    coefs = jnp.concatenate([coef_rows[b * step : (b + 1) * step].astype(F32) for b in range(wide // rows)], axis=1)
    negs = jnp.concatenate([neg_rows[0:per, b * wide : (b + 1) * wide] for b in range(width // wide)], axis=0)
    below[...] = jnp.concatenate([coefs, negs], axis=0).astype(BF16)
    copies[2].wait()


def pack_kernel(sizes, meta, b0, b1, held, below, home, *refs):
    n, rows, slots = sizes
    pairs = n // 2
    outs = refs[:pairs]
    pick, order_ref = refs[pairs:]
    head_dim = outs[0].shape[1] // PARTS
    width = head_dim * n
    cell = rows // n
    me = meta[0]
    filled, value = slot_table(meta, (b0, b1), order_ref)
    places = jnp.broadcast_to(slot_places(filled, value, me, cell), (rows, rows))
    by_rank = one_hot(slot_ranks(places) == iota((rows, rows), 1).astype(F32))
    chosen = dot(by_rank, home[...], ((0,), (0,)))
    pick[...] = chosen.astype(BF16)
    none = jnp.zeros((slots, rows), F32)
    both = jnp.concatenate(
        [jnp.concatenate([chosen[0:slots], none], axis=1), jnp.concatenate([none, chosen[0:slots]], axis=1)], axis=0
    ).astype(BF16)
    for d in range(pairs):
        columns = []
        for x in (2 * d, 2 * d + 1):
            first = pl.multiple_of((me ^ x) * head_dim, head_dim)
            columns.append(jnp.concatenate([held[:, pl.ds(i * width + first, head_dim)] for i in range(PARTS)], axis=1))
        outs[d][0 : 2 * slots] = dot(both, jnp.concatenate(columns, axis=0)).astype(BF16)
        outs[d][2 * slots :] = below[...]


def index_kernel(sizes, meta, b0, b1, pick, w_out, pick_in, pick_out, home_even, home_odd, live, most, w_cols, order_ref, w_rows, sem):
    n, rows, slots, pool = sizes
    cell = rows // n
    live_cap = live.shape[0]
    head_dim = w_rows.shape[0]
    copy = pltpu.make_async_copy(w_out.at[pl.ds(pl.multiple_of(meta[0] * head_dim, head_dim), head_dim)], w_rows, sem)
    copy.start()
    span = pick_in.shape[1] // n
    me = meta[0]
    filled, value = slot_table(meta, (b0, b1), order_ref)
    lane = iota((rows, rows), 1)
    columns = [slot_places(filled, value, me ^ x, cell) for x in range(n)]
    places = jnp.zeros((rows, rows), F32)
    for x in range(n):
        places = jnp.where(lane == x, columns[x], places)
    ranks = slot_ranks(places)
    count = jnp.sum(jnp.where(places > 0.5, 1.0, 0.0), axis=0, keepdims=True)
    counts = [count[:, x : x + 1] for x in range(n)]
    excess = [c - slots for c in counts] + [counts[2 * d] + counts[2 * d + 1] - pool for d in range(n // 2)]
    most[...] = jnp.broadcast_to(functools.reduce(jnp.maximum, excess), most.shape)

    def placed(x, first, width):
        at = ranks[:, x : x + 1] + first
        hit = jnp.where(at == iota((rows, width), 1).astype(F32), columns[x], 0.0)
        return jnp.sum(hit, axis=0, keepdims=True)

    lines = []
    for x in range(n):
        first = span - slots if x % 2 else 0
        line = placed(x, first, max(span, rows))[:, :span]
        at = iota((1, span), 1)
        lines.append(jnp.where((at >= first) & (at < first + slots), line, 0.0))
    line = jnp.concatenate(lines, axis=1) - 1.0
    pick_in[...] = one_hot(iota((live_cap, line.shape[1]), 0).astype(F32) == line)
    reach = -(-pool // rows) * rows
    for d in range(n // 2):
        line = placed(2 * d, 0.0, reach) + placed(2 * d + 1, counts[2 * d], reach) - 1.0
        hit = one_hot(iota((live_cap, reach), 0).astype(F32) == line)
        pick_out[d * pool : (d + 1) * pool] = jnp.transpose(hit.astype(F32))[:pool].astype(BF16)
    slot = iota((reach, rows), 0).astype(F32)
    for home, first in ((home_even, jnp.zeros((1, 1), F32)), (home_odd, counts[1])):
        moved = dot(one_hot(slot == lane[0:1].astype(F32) + first), pick[...])
        home[...] = moved[:pool].astype(BF16)
    copy.wait()
    w_cols[...] = jnp.transpose(w_rows[...].astype(F32)).astype(BF16)
    live[...] = jnp.where(pair_live(live_cap, starts_of(meta, n)), 1.0 / rows, 0.0)


def pair_live(live_cap, starts):
    row = iota((live_cap, 1), 0)
    col = iota((1, live_cap), 1)
    return (col <= row) & (tile_of(col, starts) > tile_of(row, starts) - SPAN) & (row < starts[-1])


def forward_kernel(sizes, meta, pick, live, w_cols, *refs):
    n, rows, slots, per = sizes
    blocks = refs[:n]
    compact, weights, att, stats, coef_c, d_mixed, negatives, neg_rows = refs[n:]
    live_cap, head_dim = att.shape
    negs = coef_c.shape[0]
    wide = blocks[0].shape[1]
    span = pick.shape[1] // n
    me = meta[0]
    received = [block[2 * slots - span : 2 * slots] if x % 2 else block[0:span] for x, block in enumerate(blocks)]
    both = dot(pick[...], jnp.concatenate(received, axis=0)).astype(BF16)
    compact[...] = both
    total = jnp.zeros((negs, live_cap), F32)
    lane = iota((negs, live_cap), 1)
    step = negs * rows // wide
    for x in range(n):
        t = me ^ x
        start = start_of(meta, n, t)
        below = blocks[x][2 * slots :].astype(F32)
        coefs = jnp.concatenate([below[0:step, b * rows : (b + 1) * rows] for b in range(wide // rows)], axis=0)
        coefs = jnp.concatenate([coefs, jnp.zeros((negs, live_cap - rows), F32)], axis=1)
        total = jnp.where((lane >= start) & (lane < start + meta[LENS + t]), pltpu.roll(coefs, start, 1), total)
        for b in range(n * head_dim // wide):
            neg_rows[t, 0:per, b * wide : (b + 1) * wide] = below[step + b * per : step + (b + 1) * per]
    coef_t = total.astype(BF16)
    coef_c[...] = coef_t
    neg = jnp.concatenate([neg_rows[s, 0:per] for s in range(n)], axis=0).astype(BF16)
    negatives[...] = neg
    head_grad = dot(coef_t, neg, ((0,), (0,))).astype(BF16)
    dm = dot(head_grad, w_cols[...])
    d_mixed[...] = dm
    u, v, q, k = (both[:, i * head_dim : (i + 1) * head_dim] for i in range(PARTS))
    scores = dot(q, k, ((1,), (1,))) * (1.0 / math.sqrt(head_dim))
    sig = jax.nn.sigmoid(scores)
    w = (scores * sig * live[...]).astype(BF16)
    weights[...] = w
    a = dot(w, v)
    att[...] = a
    dn = dm * u.astype(F32)
    mean = jnp.sum(a, axis=1, keepdims=True) * (1.0 / head_dim)
    cen = a - mean
    lane = iota((live_cap, 128), 1)
    cols = jnp.where(lane == 0, mean, 0.0)
    cols = jnp.where(lane == 1, jnp.sum(cen * cen, axis=1, keepdims=True), cols)
    cols = jnp.where(lane == 2, jnp.sum(dn, axis=1, keepdims=True), cols)
    cols = jnp.where(lane == 3, jnp.sum(dn * cen, axis=1, keepdims=True), cols)
    stats[...] = jnp.transpose(cols)[0:8]


def merge_stats(a, b, count):
    gap = b[0] - a[0]
    return (
        (a[0] + b[0]) * 0.5,
        a[1] + b[1] + gap * gap * (0.5 * count),
        a[2] + b[2],
        a[3] + b[3] + (b[2] - a[2]) * gap * 0.5,
    )


def start_of(meta, n, tile):
    start = jnp.int32(0)
    for t in range(n):
        start = start + jnp.where(t < tile, meta[LENS + t], 0)
    return start


def backward_kernel(sizes, meta, compact, weights, att, d_mixed, st0, st1, st2, st3, pick, live, *refs):
    n, rows, pool = sizes
    outs = refs[: n // 2]
    mixed_ref, mixed_rows = refs[n // 2 :]
    live_cap, head_dim = att.shape
    width = head_dim * n
    me = meta[0]
    quad = [[st[i : i + 1] for i in range(4)] for st in (st0, st1, st2, st3)]
    ab = merge_stats(quad[0], quad[1], 2 * head_dim)
    cd = merge_stats(quad[2], quad[3], 2 * head_dim)
    mean, m2, s_dn, s_dna = merge_stats(ab, cd, 4 * head_dim)
    inv = lax.rsqrt(m2 * (1.0 / width) + eps)
    table = jnp.concatenate([mean, inv, s_dn * (1.0 / width), s_dna * inv * (1.0 / width), jnp.zeros((124, live_cap), F32)], axis=0)
    table = jnp.transpose(table)
    mean, inv, mean_dn, mean_dnn = (table[:, i : i + 1] for i in range(4))
    both = compact[...]
    u, v, q, k = (both[:, i * head_dim : (i + 1) * head_dim] for i in range(PARTS))
    u = u.astype(F32)
    dm = d_mixed[...]
    normed = (att[...] - mean) * inv
    mixed = (normed * u).astype(BF16)
    dn = dm * u
    d_att = ((dn - mean_dn - normed * mean_dnn) * inv).astype(BF16)
    scale = 1.0 / math.sqrt(head_dim)
    scores = dot(q, k, ((1,), (1,))) * scale
    sig = jax.nn.sigmoid(scores)
    slope = sig * (1.0 + scores * (1.0 - sig)) * scale * live[...]
    ds = (dot(d_att, v, ((1,), (1,))) * slope).astype(BF16)
    grad = jnp.concatenate(
        [dm * normed, dot(weights[...], d_att, ((0,), (0,))), dot(ds, k), dot(ds, q, ((0,), (0,)))], axis=1
    ).astype(BF16)
    mixed_ref[...] = mixed
    sent = dot(pick[...], grad).astype(BF16)
    mixed_rows[0:live_cap] = mixed.astype(F32)
    mixed_rows[live_cap:] = jnp.zeros((rows, head_dim), F32)
    quarter = rows // PARTS
    row = iota((rows, head_dim), 0)
    for x in range(n):
        t = me ^ x
        tile = mixed_rows[pl.ds(start_of(meta, n, t), rows), :]
        tile = jnp.where(row < meta[LENS + t], tile, 0.0)
        first = quarter * (x % 2)
        outs[x // 2][first : first + quarter] = jnp.concatenate(
            [tile[b * quarter : (b + 1) * quarter] for b in range(PARTS)], axis=1
        ).astype(BF16)
    for d in range(n // 2):
        outs[d][2 * quarter :] = sent[d * pool : (d + 1) * pool]


def sums_kernel(coef_c, mixed, most, sums):
    negs = coef_c.shape[0]
    sums[0:negs] = dot(coef_c[...], mixed[...])
    sums[negs:] = most[...]


def total_kernel(meta, even, odd, negatives, w_out, *refs):
    sums, (d_w_out, most, kit, sem) = refs[:-4], refs[-4:]
    width = w_out.shape[0]
    copy = pltpu.make_async_copy(w_out, kit.at[pl.ds(0, width)], sem)
    copy.start()
    pool, rows = even.shape
    kit[width : width + pool, 0:rows] = even[...]
    kit[width : width + pool, rows : 2 * rows] = odd[...]
    negs, groups = negatives.shape[0], len(sums)
    most[...] = functools.reduce(jnp.maximum, [part[negs:] for part in sums])
    rest = functools.reduce(jnp.add, [part[0:negs] for part in sums])
    columns = width // groups
    neg = negatives[:, pl.ds(pl.multiple_of(meta[1] * columns, columns), columns)]
    grad = jnp.zeros((rest.shape[1], columns), F32)
    for _ in range(3):
        piece = rest.astype(BF16)
        grad = grad + dot(piece, neg, ((0,), (0,)))
        rest = rest - piece.astype(F32)
    d_w_out[...] = grad
    copy.wait()


def finish_kernel(sizes, meta, kit, *refs):
    n, rows = sizes
    blocks, (d_home, layer_out) = refs[:n], refs[n:]
    width = kit.shape[1]
    head_dim = width // n
    quarter = rows // PARTS
    layer = jnp.zeros((rows, width), F32)
    for d in range(0, n, 2):
        mixed, weights = [], []
        for x in (d, d + 1):
            head = pl.multiple_of((meta[0] ^ x) * head_dim, head_dim)
            block = blocks[x]
            pick = kit[width : width + block.shape[0] - 2 * quarter, rows * (x % 2) : rows * (x % 2 + 1)]
            part = dot(pick, block[2 * quarter :], ((0,), (0,))).astype(BF16)
            for i in range(PARTS):
                d_home[:, pl.ds(i * width + head, head_dim)] = part[:, i * head_dim : (i + 1) * head_dim]
            lines = block[quarter * (x % 2) : quarter * (x % 2 + 1)]
            mixed.append(jnp.concatenate([lines[:, b * head_dim : (b + 1) * head_dim] for b in range(PARTS)], axis=0))
            weights.append(kit[pl.ds(head, head_dim), :])
        layer = layer + dot(jnp.concatenate(mixed, axis=1), jnp.concatenate(weights, axis=0))
    layer_out[...] = layer.astype(BF16)


def kernel_call(body, shapes, specs, scratch=(), limit=40):
    return pl.pallas_call(
        body,
        out_shape=shapes,
        in_specs=specs,
        out_specs=jax.tree.map(lambda _: VMEM, shapes),
        scratch_shapes=scratch,
        compiler_params=pltpu.CompilerParams(vmem_limit_bytes=limit * 1024 * 1024),
    )


def swap(block, axis, distance):
    return lax.ppermute(block, axis, [(i, i ^ distance) for i in range(lax.axis_size(axis))])


def exchange(message, between):
    far = [swap(own, "seq", 2 * d) for d, own in enumerate(message) if d > 0]
    made = between()
    blocks = [message[0], swap(message[0], "seq", 1)]
    for d, own in enumerate(far):
        if d == len(far) - 1:
            own, made = lax.optimization_barrier((own, made))
        blocks += [own, swap(own, "seq", 1)]
    return blocks, made


def load_kernel(block, out):
    out[...] = block[...]


def join_kernel(first, second, out):
    out[0 : first.shape[0]] = first[...]
    out[first.shape[0] :] = second[...]


def gather_small(block, between):
    n = lax.axis_size("seq")
    known, distance = kernel_call(load_kernel, jax.ShapeDtypeStruct(block.shape, block.dtype), [VMEM])(block), 1
    while distance < n // 2:
        shape = jax.ShapeDtypeStruct((2 * known.shape[0], known.shape[1]), known.dtype)
        known = kernel_call(join_kernel, shape, [VMEM] * 2)(known, swap(block if distance == 1 else known, "seq", distance))
        distance *= 2
    known, made = lax.optimization_barrier((known, between()))
    return [known, swap(known, "seq", distance)], made


def head_plan(qkvu, w_out, head_coef, item_table, neg_ids, send_order, recv_order, tile_len):
    n = lax.axis_size("seq")
    groups = lax.axis_size("dp")
    rows = qkvu.shape[0]
    width = w_out.shape[0]
    head_dim = width // HEADS
    negs = head_coef.shape[1]
    per = neg_ids.shape[0]
    wide = PARTS * head_dim
    live_cap = -(-(n * rows // 3) // 128) * 128
    sds = jax.ShapeDtypeStruct
    me = lax.axis_index("seq")
    meta = jnp.concatenate([jnp.stack([me, lax.axis_index("dp")]).astype(jnp.int32), tile_len[0]])
    head_coef_t = head_coef.T

    half = n // 2
    quarter = rows // PARTS
    below = (negs * rows + per * width) // wide

    def passes(slots, pool):
        span = -(-slots // 8) * 8
        def prep():
            return kernel_call(
                prep_kernel,
                (sds(qkvu.shape, BF16), sds((below, wide), BF16), sds((rows, rows), BF16)),
                [SMEM] + [ANY] * 4,
                [
                    pltpu.VMEM((1, rows), jnp.int32),
                    pltpu.VMEM((negs, rows), BF16),
                    pltpu.VMEM((per, 16, width), BF16),
                    pltpu.VMEM((8, width), F32),
                    pltpu.SemaphoreType.DMA((3 + per,)),
                ],
            )(neg_ids, send_order, head_coef_t, item_table, qkvu)

        orders, prepared = gather_small(recv_order, prep)
        *message, pick = kernel_call(
            functools.partial(pack_kernel, (n, rows, slots)),
            (sds((2 * slots + below, wide), BF16),) * half + (sds((rows, rows), BF16),),
            [SMEM] + [VMEM] * 5,
            [pltpu.VMEM((n, 1, rows), F32)],
        )(meta, *orders, *prepared)

        def index():
            return kernel_call(
                functools.partial(index_kernel, (n, rows, slots, pool)),
                (
                    sds((live_cap, n * span), BF16),
                    sds((half * pool, live_cap), BF16),
                    sds((pool, rows), BF16),
                    sds((pool, rows), BF16),
                    sds((live_cap, live_cap), F32),
                    sds((8, 128), F32),
                    sds((width, head_dim), BF16),
                ),
                [SMEM] + [VMEM] * 3 + [ANY],
                [pltpu.VMEM((n, 1, rows), F32), pltpu.VMEM((head_dim, width), BF16), pltpu.SemaphoreType.DMA],
            )(meta, *orders, pick, w_out)

        received, (pick_in, pick_out, even, odd, live, most, w_cols) = exchange(message, index)
        compact, weights, att, stats, coef_c, d_mixed, negatives = kernel_call(
            functools.partial(forward_kernel, (n, rows, slots, per)),
            (
                sds((live_cap, wide), BF16),
                sds((live_cap, live_cap), BF16),
                sds((live_cap, head_dim), F32),
                sds((8, live_cap), F32),
                sds((negs, live_cap), BF16),
                sds((live_cap, head_dim), F32),
                sds((negs, width), BF16),
            ),
            [SMEM] + [VMEM] * (3 + n),
            [pltpu.VMEM((n, 8, width), F32)],
        )(meta, pick_in, live, w_cols, *received)
        paired = merge_stats(stats, swap(stats, "seq", 1), head_dim)
        paired = jnp.stack(list(paired) + [jnp.zeros_like(stats[0])] * 4)
        far = [swap(paired, "seq", d) for d in range(2, n, 2)]
        *back, mixed = kernel_call(
            functools.partial(backward_kernel, (n, rows, pool)),
            (sds((2 * quarter + pool, wide), BF16),) * half + (sds((live_cap, head_dim), BF16),),
            [SMEM] + [VMEM] * 10,
            [pltpu.VMEM((live_cap + rows, head_dim), F32)],
        )(meta, compact, weights, att, d_mixed, paired, *far, pick_out, live)

        def group_sums():
            sums = kernel_call(sums_kernel, sds((negs + 8, head_dim), F32), [VMEM] * 3)(coef_c, mixed, most)
            sums = [sums] + [swap(sums, "dp", d) for d in range(1, groups)]
            d_w, most_of_all, kit = kernel_call(
                total_kernel,
                (sds((head_dim, width // groups), F32), sds((8, 128), F32), sds((width + -(-pool // 16) * 16, width), BF16)),
                [SMEM] + [VMEM] * 3 + [ANY] + [VMEM] * groups,
                [pltpu.SemaphoreType.DMA],
            )(meta, even, odd, negatives, w_out, *sums)
            return d_w, kit, most_of_all

        returned, (d_w, kit, most_of_all) = exchange(back, group_sums)
        return most_of_all[0, 0] > 0.0, (d_w, kit, *returned)

    def finish(d_w, *parts):
        outs = kernel_call(
            functools.partial(finish_kernel, (n, rows)),
            (sds((rows, PARTS * width), BF16), sds((rows, width), BF16)),
            [SMEM] + [VMEM] * (1 + n),
        )(meta, *parts)
        return (*outs, d_w)

    overflow, parts = passes(SLOTS, POOL)
    d_home, layer_out, d_w_out = lax.cond(
        overflow, lambda *_: finish(*passes(rows, 2 * rows)[1]), lambda *outs: outs, *finish(*parts)
    )
    return (layer_out, d_home, d_w_out)


def solution(mesh):
    placed = (
        P(("dp", "seq"), None),
        P(),
        P(("dp", "seq"), None),
        P("seq", None),
        P("seq"),
        P(("dp", "seq"), None),
        P(("dp", "seq"), None),
        P("dp", None),
    )
    return jax.shard_map(
        head_plan if mesh.shape["seq"] == HEADS else tile_plan,
        mesh=mesh,
        in_specs=placed,
        out_specs=(P(("dp", "seq"), None), P(("dp", "seq"), None), P("seq", "dp")),
        check_vma=False,
    )
```

```python
import functools
import math

import jax
import jax.numpy as jnp
from jax import lax
from jax.experimental import pallas as pl
from jax.experimental.pallas import tpu as pltpu
from jax.sharding import PartitionSpec as P

HEADS = 8
SPAN = 3
PARTS = 4
SLOTS = 60
POOL = 152
LENS = 2


eps = 1e-05

VMEM = pl.BlockSpec(memory_space=pltpu.VMEM)
SMEM = pl.BlockSpec(memory_space=pltpu.SMEM)
ANY = pl.BlockSpec(memory_space=pl.ANY)
F32 = jnp.float32
BF16 = jnp.bfloat16


def shifted(block, axis, distance):
    devices = range(lax.axis_size(axis))
    route = [(i - distance, i) for i in devices if i - distance in devices]
    return lax.ppermute(block, axis, route)


def silu_grad(values):
    sigmoid_val = jax.nn.sigmoid(values)
    return sigmoid_val * (1.0 + values * (1.0 - sigmoid_val))


def pair_mask(count, len_p, len_q, allowed, causal):
    positions = jnp.arange(count, dtype=jnp.int32)
    live = (positions[:, None] < len_p) & (positions[None, :] < len_q) & allowed
    if causal:
        live = live & (positions[None, :] <= positions[:, None])
    return jnp.where(live, 1.0, 0.0).astype(jnp.float32)


def head_major(flat, count, head_dim):
    return flat.reshape(count, HEADS, head_dim).transpose(1, 0, 2)


def row_major(heads_first, count, width):
    return heads_first.transpose(1, 0, 2).reshape(count, width)


def tile_plan(qkvu, w_out, head_coef, item_table, neg_ids, send_order, recv_order, tile_len):
    row_count = qkvu.shape[0]
    model_width = w_out.shape[0]
    head_dim = model_width // HEADS
    score_scale = 1.0 / math.sqrt(head_dim)
    send_list = send_order[0]
    recv_list = recv_order[0]
    own_index = lax.axis_index("seq")
    lengths_row = tile_len[0]
    own_len = jnp.take(lengths_row, own_index)
    outgoing = jnp.take(qkvu, send_list, axis=0)
    received = lax.all_to_all(outgoing, "seq", split_axis=0, concat_axis=0, tiled=True)
    balanced = jnp.take(received, recv_list, axis=0)
    neg_all = lax.all_gather(jnp.take(item_table, neg_ids, axis=0), "seq", axis=0, tiled=True)
    u_part = balanced[:, :model_width].astype(jnp.float32)
    value_heads = head_major(balanced[:, model_width : 2 * model_width], row_count, head_dim)
    query_heads = head_major(balanced[:, 2 * model_width : 3 * model_width], row_count, head_dim)
    key_heads = head_major(balanced[:, 3 * model_width :], row_count, head_dim)
    lagged = []
    carried = (value_heads, key_heads)
    for lag in range(1, SPAN):
        carried = shifted((carried[0], carried[1]), "seq", 1)
        lagged.append(carried)
    value_list = [value_heads]
    key_list = [key_heads]
    mask_list = [pair_mask(row_count, own_len, own_len, True, True)]
    for lag in range(1, SPAN):
        earlier_len = jnp.take(lengths_row, jnp.maximum(own_index - lag, 0))
        value_list.append(lagged[lag - 1][0])
        key_list.append(lagged[lag - 1][1])
        mask_list.append(pair_mask(row_count, own_len, earlier_len, own_index >= lag, False))
    values_all = jnp.concatenate(value_list, axis=1)
    keys_all = jnp.concatenate(key_list, axis=1)
    mask_all = jnp.concatenate(mask_list, axis=1)
    scores = (
        jnp.einsum("hpd,hqd->hpq", query_heads, keys_all, preferred_element_type=jnp.float32)
        * score_scale
    )
    weights = (jax.nn.silu(scores) * mask_all[None] / row_count).astype(jnp.bfloat16)
    attended_heads = jnp.einsum(
        "hpq,hqd->hpd", weights, values_all, preferred_element_type=jnp.float32
    )
    attended = row_major(attended_heads, row_count, model_width)
    row_mean = jnp.mean(attended, axis=1, keepdims=True)
    centered = attended - row_mean
    variance = jnp.mean(centered * centered, axis=1, keepdims=True)
    inv_std = lax.rsqrt(variance + eps)
    normed = centered * inv_std
    mixed_rows = (normed * u_part).astype(jnp.bfloat16)
    layer_out = jnp.dot(mixed_rows, w_out, preferred_element_type=jnp.float32).astype(jnp.bfloat16)
    positions = jnp.arange(row_count, dtype=jnp.int32)
    live_col = jnp.where(positions < own_len, 1.0, 0.0).astype(jnp.float32)[:, None]
    coef_live = (head_coef * live_col).astype(jnp.bfloat16)
    head_grad = jnp.dot(coef_live, neg_all, preferred_element_type=jnp.float32).astype(jnp.bfloat16)
    d_mixed = lax.dot_general(
        head_grad, w_out, (((1,), (1,)), ((), ())), preferred_element_type=jnp.float32
    )
    d_u_part = d_mixed * normed
    d_normed = d_mixed * u_part
    d_att = (
        d_normed
        - jnp.mean(d_normed, axis=1, keepdims=True)
        - normed * jnp.mean(d_normed * normed, axis=1, keepdims=True)
    ) * inv_std
    d_att_heads = head_major(d_att.astype(jnp.bfloat16), row_count, head_dim)
    d_weights = jnp.einsum(
        "hpd,hqd->hpq", d_att_heads, values_all, preferred_element_type=jnp.float32
    )
    d_scores = (d_weights * mask_all[None] / row_count * silu_grad(scores) * score_scale).astype(
        jnp.bfloat16
    )
    d_query = jnp.einsum("hpq,hqd->hpd", d_scores, keys_all, preferred_element_type=jnp.float32)
    part_keys = jnp.einsum(
        "hpq,hpd->hqd", d_scores, query_heads, preferred_element_type=jnp.float32
    )
    part_values = jnp.einsum(
        "hpq,hpd->hqd", weights, d_att_heads, preferred_element_type=jnp.float32
    )
    key_grad = part_keys[:, :row_count]
    value_grad = part_values[:, :row_count]
    for lag in range(1, SPAN):
        block_keys = part_keys[:, lag * row_count : (lag + 1) * row_count].astype(jnp.bfloat16)
        block_values = part_values[:, lag * row_count : (lag + 1) * row_count].astype(jnp.bfloat16)
        back_values, back_keys = shifted((block_values, block_keys), "seq", -lag)
        key_grad = key_grad + back_keys.astype(jnp.float32)
        value_grad = value_grad + back_values.astype(jnp.float32)
    tile_grads = jnp.concatenate(
        [
            d_u_part,
            row_major(value_grad, row_count, model_width),
            row_major(d_query, row_count, model_width),
            row_major(key_grad, row_count, model_width),
        ],
        axis=1,
    ).astype(jnp.bfloat16)
    slot_grads = jnp.zeros_like(tile_grads).at[recv_list].set(tile_grads)
    returned = lax.all_to_all(slot_grads, "seq", split_axis=0, concat_axis=0, tiled=True)
    d_home = jnp.zeros_like(returned).at[send_list].set(returned)
    coef_sums = lax.psum_scatter(
        lax.dot_general(
            mixed_rows, coef_live, (((0,), (0,)), ((), ())), preferred_element_type=jnp.float32
        ),
        "seq",
        scatter_dimension=0,
        tiled=True,
    )
    row_grad = jnp.dot(coef_sums, neg_all.astype(jnp.float32), precision=lax.Precision.HIGHEST)
    d_w_out = lax.psum_scatter(
        row_grad.astype(jnp.bfloat16), "dp", scatter_dimension=1, tiled=True
    ).astype(jnp.float32)
    return (layer_out, d_home, d_w_out)


def dot(a, b, dims=((1,), (0,))):
    return lax.dot_general(a, b, (dims, ((), ())), preferred_element_type=F32)


def iota(shape, dim):
    return lax.broadcasted_iota(jnp.int32, shape, dim)


def starts_of(meta, count):
    starts = [jnp.int32(0)]
    for t in range(count):
        starts.append(starts[-1] + meta[LENS + t])
    return starts


def tile_of(position, starts):
    tile = jnp.zeros(position.shape, jnp.int32)
    for start in starts[1:-1]:
        tile = tile + jnp.where(position >= start, 1, 0)
    return tile


def one_hot(condition):
    return jnp.where(condition, 1.0, 0.0).astype(BF16)


def slot_table(meta, blocks, order_ref):
    n, _, rows = order_ref.shape
    cell = rows // n
    for b in range(n):
        order_ref[meta[0] ^ b] = blocks[b // (n // 2)][b % (n // 2) : b % (n // 2) + 1].astype(F32)
    starts = starts_of(meta, n)
    pos = iota((cell, rows), 1)
    filled = [jnp.broadcast_to(order_ref[t], (cell, rows)) for t in range(n)]
    value = [jnp.where(pos < meta[LENS + t], pos + starts[t] + 1, 0).astype(F32) for t in range(n)]
    return jnp.concatenate(filled, axis=0), jnp.concatenate(value, axis=0)


def slot_places(filled, value, source, cell):
    slot = (iota(filled.shape, 0) % cell + source * cell).astype(F32)
    return jnp.sum(jnp.where(filled == slot, value, 0.0), axis=1, keepdims=True)


def slot_ranks(places):
    rows = places.shape[0]
    live = places > 0.5
    before = dot(one_hot(iota((rows, rows), 1) < iota((rows, rows), 0)), one_hot(live))
    return jnp.where(live, before, -1.0)


def put_rows(me, head_dim, picked, outs):
    width = picked.shape[1] // PARTS
    for x in range(2 * len(outs)):
        first = pl.multiple_of((me ^ x) * head_dim, head_dim)
        outs[x // 2][x % 2] = jnp.concatenate([picked[:, pl.ds(i * width + first, head_dim)] for i in range(PARTS)], axis=1)


def prep_kernel(ids, send, coef_t, table, qkvu, held, below, home, send_row, coef_rows, items, neg_rows, sems):
    per, chunk, width = items.shape
    rows = send_row.shape[1]
    wide = below.shape[1]
    copies = [
        pltpu.make_async_copy(source, target, sems.at[i])
        for i, (source, target) in enumerate(((send, send_row), (coef_t, coef_rows), (qkvu, held)))
    ]
    for j in range(per):
        start = pl.multiple_of((ids[j] // chunk) * chunk, chunk)
        copies.append(pltpu.make_async_copy(table.at[pl.ds(start, chunk)], items.at[j], sems.at[3 + j]))
    for copy in copies:
        copy.start()
    lane = iota((rows, rows), 1)
    copies[0].wait()
    own = jnp.where(lane == iota((rows, rows), 0), send_row[...].astype(F32), 0.0)
    home[...] = one_hot(jnp.sum(own, axis=1, keepdims=True) == lane.astype(F32))
    copies[1].wait()
    for j in range(per):
        copies[3 + j].wait()
        own = iota((chunk, width), 0) == ids[j] % chunk
        neg_rows[j : j + 1] = jnp.sum(jnp.where(own, items[j].astype(F32), 0.0), axis=0, keepdims=True)
    step = coef_rows.shape[0] * rows // wide
    coefs = jnp.concatenate([coef_rows[b * step : (b + 1) * step].astype(F32) for b in range(wide // rows)], axis=1)
    negs = jnp.concatenate([neg_rows[0:per, b * wide : (b + 1) * wide] for b in range(width // wide)], axis=0)
    below[...] = jnp.concatenate([coefs, negs], axis=0).astype(BF16)
    copies[2].wait()


def pack_kernel(sizes, meta, b0, b1, held, below, home, *refs):
    n, rows, slots = sizes
    pairs = n // 2
    outs = refs[:pairs]
    pick, order_ref = refs[pairs:]
    head_dim = outs[0].shape[1] // PARTS
    width = head_dim * n
    cell = rows // n
    me = meta[0]
    filled, value = slot_table(meta, (b0, b1), order_ref)
    places = jnp.broadcast_to(slot_places(filled, value, me, cell), (rows, rows))
    by_rank = one_hot(slot_ranks(places) == iota((rows, rows), 1).astype(F32))
    chosen = dot(by_rank, home[...], ((0,), (0,)))
    pick[...] = chosen.astype(BF16)
    none = jnp.zeros((slots, rows), F32)
    both = jnp.concatenate(
        [jnp.concatenate([chosen[0:slots], none], axis=1), jnp.concatenate([none, chosen[0:slots]], axis=1)], axis=0
    ).astype(BF16)
    for d in range(pairs):
        columns = []
        for x in (2 * d, 2 * d + 1):
            first = pl.multiple_of((me ^ x) * head_dim, head_dim)
            columns.append(jnp.concatenate([held[:, pl.ds(i * width + first, head_dim)] for i in range(PARTS)], axis=1))
        outs[d][0 : 2 * slots] = dot(both, jnp.concatenate(columns, axis=0)).astype(BF16)
        outs[d][2 * slots :] = below[...]


def index_kernel(sizes, meta, b0, b1, pick, w_out, pick_in, pick_out, home_even, home_odd, tile, live, most, w_cols, order_ref, w_rows, sem):
    n, rows, slots, pool = sizes
    cell = rows // n
    live_cap = live.shape[0]
    head_dim = w_rows.shape[0]
    copy = pltpu.make_async_copy(w_out.at[pl.ds(pl.multiple_of(meta[0] * head_dim, head_dim), head_dim)], w_rows, sem)
    copy.start()
    span = pick_in.shape[1] // n
    me = meta[0]
    filled, value = slot_table(meta, (b0, b1), order_ref)
    lane = iota((rows, rows), 1)
    columns = [slot_places(filled, value, me ^ x, cell) for x in range(n)]
    places = jnp.zeros((rows, rows), F32)
    for x in range(n):
        places = jnp.where(lane == x, columns[x], places)
    ranks = slot_ranks(places)
    count = jnp.sum(jnp.where(places > 0.5, 1.0, 0.0), axis=0, keepdims=True)
    counts = [count[:, x : x + 1] for x in range(n)]
    lines_of = [pair_lines(meta, (me >> 1) ^ d) for d in range(n // 2)]
    excess = [c - slots for c in counts] + [counts[2 * d] + counts[2 * d + 1] + (lines_of[d] - pool).astype(F32) for d in range(n // 2)]
    most[...] = jnp.broadcast_to(functools.reduce(jnp.maximum, excess), most.shape)

    def placed(x, first, width):
        at = ranks[:, x : x + 1] + first
        hit = jnp.where(at == iota((rows, width), 1).astype(F32), columns[x], 0.0)
        return jnp.sum(hit, axis=0, keepdims=True)

    lines = []
    for x in range(n):
        first = span - slots if x % 2 else 0
        line = placed(x, first, max(span, rows))[:, :span]
        at = iota((1, span), 1)
        lines.append(jnp.where((at >= first) & (at < first + slots), line, 0.0))
    line = jnp.concatenate(lines, axis=1) - 1.0
    pick_in[...] = one_hot(iota((live_cap, line.shape[1]), 0).astype(F32) == line)
    reach = -(-pool // rows) * rows
    for d in range(n // 2):
        first = lines_of[d].astype(F32)
        line = placed(2 * d, first, reach) + placed(2 * d + 1, counts[2 * d] + first, reach) - 1.0
        hit = one_hot(iota((live_cap, reach), 0).astype(F32) == line)
        pick_out[d * pool : (d + 1) * pool] = jnp.transpose(hit.astype(F32))[:pool].astype(BF16)
    slot = iota((reach, rows), 0).astype(F32)
    for home, first in ((home_even, jnp.zeros((1, 1), F32)), (home_odd, counts[1])):
        first = first + lines_of[0].astype(F32)
        moved = dot(one_hot(slot == lane[0:1].astype(F32) + first), pick[...])
        home[...] = jnp.transpose(moved).astype(BF16)
    quarter = tile.shape[1] // PARTS
    line = iota((rows, quarter), 1)
    row = iota((rows, quarter), 0)
    before = jnp.where(me % 2 == 1, meta[LENS + (me ^ 1)], 0)
    for b in range(PARTS):
        hit = (line + b * lines_of[0] == row + before) & (line < lines_of[0]) & (row < meta[LENS + me])
        tile[:, b * quarter : (b + 1) * quarter] = one_hot(hit)
    copy.wait()
    w_cols[...] = jnp.transpose(w_rows[...].astype(F32)).astype(BF16)
    live[...] = jnp.where(pair_live(live_cap, starts_of(meta, n)), 1.0 / rows, 0.0)


def pair_live(live_cap, starts):
    row = iota((live_cap, 1), 0)
    col = iota((1, live_cap), 1)
    return (col <= row) & (tile_of(col, starts) > tile_of(row, starts) - SPAN) & (row < starts[-1])


def forward_kernel(sizes, meta, pick, live, w_cols, *refs):
    n, rows, slots, per = sizes
    blocks = refs[:n]
    compact, weights, att, stats, coef_c, d_mixed, negatives, neg_rows = refs[n:]
    live_cap, head_dim = att.shape
    negs = coef_c.shape[0]
    wide = blocks[0].shape[1]
    span = pick.shape[1] // n
    me = meta[0]
    received = [block[2 * slots - span : 2 * slots] if x % 2 else block[0:span] for x, block in enumerate(blocks)]
    both = dot(pick[...], jnp.concatenate(received, axis=0)).astype(BF16)
    compact[...] = both
    total = jnp.zeros((negs, live_cap), F32)
    lane = iota((negs, live_cap), 1)
    step = negs * rows // wide
    for x in range(n):
        t = me ^ x
        start = start_of(meta, n, t)
        below = blocks[x][2 * slots :].astype(F32)
        coefs = jnp.concatenate([below[0:step, b * rows : (b + 1) * rows] for b in range(wide // rows)], axis=0)
        coefs = jnp.concatenate([coefs, jnp.zeros((negs, live_cap - rows), F32)], axis=1)
        total = jnp.where((lane >= start) & (lane < start + meta[LENS + t]), pltpu.roll(coefs, start, 1), total)
        for b in range(n * head_dim // wide):
            neg_rows[t, 0:per, b * wide : (b + 1) * wide] = below[step + b * per : step + (b + 1) * per]
    coef_t = total.astype(BF16)
    coef_c[...] = coef_t
    neg = jnp.concatenate([neg_rows[s, 0:per] for s in range(n)], axis=0).astype(BF16)
    negatives[...] = neg
    head_grad = dot(coef_t, neg, ((0,), (0,))).astype(BF16)
    dm = dot(head_grad, w_cols[...])
    d_mixed[...] = dm
    u, v, q, k = (both[:, i * head_dim : (i + 1) * head_dim] for i in range(PARTS))
    scores = dot(q, k, ((1,), (1,))) * (1.0 / math.sqrt(head_dim))
    sig = jax.nn.sigmoid(scores)
    w = (scores * sig * live[...]).astype(BF16)
    weights[...] = w
    a = dot(w, v)
    att[...] = a
    dn = dm * u.astype(F32)
    mean = jnp.sum(a, axis=1, keepdims=True) * (1.0 / head_dim)
    cen = a - mean
    lane = iota((live_cap, 128), 1)
    cols = jnp.where(lane == 0, mean, 0.0)
    cols = jnp.where(lane == 1, jnp.sum(cen * cen, axis=1, keepdims=True), cols)
    cols = jnp.where(lane == 2, jnp.sum(dn, axis=1, keepdims=True), cols)
    cols = jnp.where(lane == 3, jnp.sum(dn * cen, axis=1, keepdims=True), cols)
    stats[...] = jnp.transpose(cols)[0:8]


def merge_stats(a, b, count):
    gap = b[0] - a[0]
    return (
        (a[0] + b[0]) * 0.5,
        a[1] + b[1] + gap * gap * (0.5 * count),
        a[2] + b[2],
        a[3] + b[3] + (b[2] - a[2]) * gap * 0.5,
    )


def pair_lines(meta, chip):
    return (meta[LENS + 2 * chip] + meta[LENS + 2 * chip + 1] + PARTS - 1) // PARTS


def start_of(meta, n, tile):
    start = jnp.int32(0)
    for t in range(n):
        start = start + jnp.where(t < tile, meta[LENS + t], 0)
    return start


def backward_kernel(sizes, meta, compact, weights, att, d_mixed, st0, st1, st2, st3, pick, live, *refs):
    n, rows, pool = sizes
    outs = refs[: n // 2]
    mixed_ref, mixed_rows = refs[n // 2 :]
    live_cap, head_dim = att.shape
    width = head_dim * n
    me = meta[0]
    quad = [[st[i : i + 1] for i in range(4)] for st in (st0, st1, st2, st3)]
    ab = merge_stats(quad[0], quad[1], 2 * head_dim)
    cd = merge_stats(quad[2], quad[3], 2 * head_dim)
    mean, m2, s_dn, s_dna = merge_stats(ab, cd, 4 * head_dim)
    inv = lax.rsqrt(m2 * (1.0 / width) + eps)
    table = jnp.concatenate([mean, inv, s_dn * (1.0 / width), s_dna * inv * (1.0 / width), jnp.zeros((124, live_cap), F32)], axis=0)
    table = jnp.transpose(table)
    mean, inv, mean_dn, mean_dnn = (table[:, i : i + 1] for i in range(4))
    both = compact[...]
    u, v, q, k = (both[:, i * head_dim : (i + 1) * head_dim] for i in range(PARTS))
    u = u.astype(F32)
    dm = d_mixed[...]
    normed = (att[...] - mean) * inv
    mixed = (normed * u).astype(BF16)
    dn = dm * u
    d_att = ((dn - mean_dn - normed * mean_dnn) * inv).astype(BF16)
    scale = 1.0 / math.sqrt(head_dim)
    scores = dot(q, k, ((1,), (1,))) * scale
    sig = jax.nn.sigmoid(scores)
    slope = sig * (1.0 + scores * (1.0 - sig)) * scale * live[...]
    ds = (dot(d_att, v, ((1,), (1,))) * slope).astype(BF16)
    grad = jnp.concatenate(
        [dm * normed, dot(weights[...], d_att, ((0,), (0,))), dot(ds, k), dot(ds, q, ((0,), (0,)))], axis=1
    ).astype(BF16)
    mixed_ref[...] = mixed
    sent = dot(pick[...], grad)
    mixed_rows[0:live_cap] = mixed.astype(F32)
    mixed_rows[live_cap:] = jnp.zeros((2 * rows, head_dim), F32)
    half = 2 * rows // PARTS
    row = iota((half, head_dim), 0)
    for d in range(n // 2):
        chip = (me >> 1) ^ d
        lines = pair_lines(meta, chip)
        count = meta[LENS + 2 * chip] + meta[LENS + 2 * chip + 1]
        parts = []
        for b in range(PARTS):
            part = mixed_rows[pl.ds(start_of(meta, n, 2 * chip) + b * lines, half), :]
            parts.append(jnp.where((row < lines) & (row + b * lines < count), part, 0.0))
        rows_out = sent[d * pool : (d + 1) * pool]
        outs[d][0:half] = (rows_out[0:half] + jnp.concatenate(parts, axis=1)).astype(BF16)
        outs[d][half:] = rows_out[half:].astype(BF16)


def sums_kernel(coef_c, mixed, most, sums):
    negs = coef_c.shape[0]
    sums[0:negs] = dot(coef_c[...], mixed[...])
    sums[negs:] = most[...]


def total_kernel(meta, even, odd, tile, negatives, w_out, *refs):
    sums, (d_w_out, most, kit, sem) = refs[:-4], refs[-4:]
    width = w_out.shape[0]
    copy = pltpu.make_async_copy(w_out, kit.at[pl.ds(0, width)], sem)
    copy.start()
    rows, reach = even.shape
    kit[width:, 0:reach] = even[...]
    kit[width:, reach : 2 * reach] = odd[...]
    kit[width:, 2 * reach : 2 * reach + 2 * rows] = tile[...]
    negs, groups = negatives.shape[0], len(sums)
    most[...] = functools.reduce(jnp.maximum, [part[negs:] for part in sums])
    rest = functools.reduce(jnp.add, [part[0:negs] for part in sums])
    columns = width // groups
    neg = negatives[:, pl.ds(pl.multiple_of(meta[1] * columns, columns), columns)]
    grad = jnp.zeros((rest.shape[1], columns), F32)
    for _ in range(3):
        piece = rest.astype(BF16)
        grad = grad + dot(piece, neg, ((0,), (0,)))
        rest = rest - piece.astype(F32)
    d_w_out[...] = grad
    copy.wait()


def finish_kernel(sizes, meta, kit, *refs):
    n, rows = sizes
    blocks, (d_home, layer_out) = refs[:n], refs[n:]
    width = kit.shape[1]
    head_dim = width // n
    quarter = rows // PARTS
    reach = -(-blocks[0].shape[0] // rows) * rows
    for x in range(n):
        head = pl.multiple_of((meta[0] ^ x) * head_dim, head_dim)
        block = blocks[x][...]
        pick = kit[width:, reach * (x % 2) : reach * (x % 2) + block.shape[0]]
        part = dot(pick, block).astype(BF16)
        for i in range(PARTS):
            d_home[:, pl.ds(i * width + head, head_dim)] = part[:, i * head_dim : (i + 1) * head_dim]
        lines = jnp.concatenate([block[0 : 2 * quarter, b * head_dim : (b + 1) * head_dim] for b in range(PARTS)], axis=0)
        layer_out[:, pl.ds(head, head_dim)] = dot(kit[width:, 2 * reach : 2 * reach + 2 * rows], lines).astype(BF16)
    layer = dot(layer_out[...], kit[0:width])
    layer_out[...] = layer.astype(BF16)


def kernel_call(body, shapes, specs, scratch=(), limit=40):
    return pl.pallas_call(
        body,
        out_shape=shapes,
        in_specs=specs,
        out_specs=jax.tree.map(lambda _: VMEM, shapes),
        scratch_shapes=scratch,
        compiler_params=pltpu.CompilerParams(vmem_limit_bytes=limit * 1024 * 1024),
    )


def swap(block, axis, distance):
    return lax.ppermute(block, axis, [(i, i ^ distance) for i in range(lax.axis_size(axis))])


def exchange(message, between):
    far = [swap(own, "seq", 2 * d) for d, own in enumerate(message) if d > 0]
    made = between()
    blocks = [message[0], swap(message[0], "seq", 1)]
    for d, own in enumerate(far):
        if d == len(far) - 1:
            own, made = lax.optimization_barrier((own, made))
        blocks += [own, swap(own, "seq", 1)]
    return blocks, made


def load_kernel(block, out):
    out[...] = block[...]


def join_kernel(first, second, out):
    out[0 : first.shape[0]] = first[...]
    out[first.shape[0] :] = second[...]


def gather_small(block, between):
    n = lax.axis_size("seq")
    known, distance = kernel_call(load_kernel, jax.ShapeDtypeStruct(block.shape, block.dtype), [VMEM])(block), 1
    while distance < n // 2:
        shape = jax.ShapeDtypeStruct((2 * known.shape[0], known.shape[1]), known.dtype)
        known = kernel_call(join_kernel, shape, [VMEM] * 2)(known, swap(block if distance == 1 else known, "seq", distance))
        distance *= 2
    known, made = lax.optimization_barrier((known, between()))
    return [known, swap(known, "seq", distance)], made


def head_plan(qkvu, w_out, head_coef, item_table, neg_ids, send_order, recv_order, tile_len):
    n = lax.axis_size("seq")
    groups = lax.axis_size("dp")
    rows = qkvu.shape[0]
    width = w_out.shape[0]
    head_dim = width // HEADS
    negs = head_coef.shape[1]
    per = neg_ids.shape[0]
    wide = PARTS * head_dim
    live_cap = -(-(n * rows // 3) // 128) * 128
    sds = jax.ShapeDtypeStruct
    me = lax.axis_index("seq")
    meta = jnp.concatenate([jnp.stack([me, lax.axis_index("dp")]).astype(jnp.int32), tile_len[0]])
    head_coef_t = head_coef.T

    half = n // 2
    quarter = rows // PARTS
    below = (negs * rows + per * width) // wide

    def passes(slots, pool):
        span = -(-slots // 8) * 8
        reach = -(-pool // rows) * rows
        def prep():
            return kernel_call(
                prep_kernel,
                (sds(qkvu.shape, BF16), sds((below, wide), BF16), sds((rows, rows), BF16)),
                [SMEM] + [ANY] * 4,
                [
                    pltpu.VMEM((1, rows), jnp.int32),
                    pltpu.VMEM((negs, rows), BF16),
                    pltpu.VMEM((per, 16, width), BF16),
                    pltpu.VMEM((8, width), F32),
                    pltpu.SemaphoreType.DMA((3 + per,)),
                ],
            )(neg_ids, send_order, head_coef_t, item_table, qkvu)

        orders, prepared = gather_small(recv_order, prep)
        *message, pick = kernel_call(
            functools.partial(pack_kernel, (n, rows, slots)),
            (sds((2 * slots + below, wide), BF16),) * half + (sds((rows, rows), BF16),),
            [SMEM] + [VMEM] * 5,
            [pltpu.VMEM((n, 1, rows), F32)],
        )(meta, *orders, *prepared)

        def index():
            return kernel_call(
                functools.partial(index_kernel, (n, rows, slots, pool)),
                (
                    sds((live_cap, n * span), BF16),
                    sds((half * pool, live_cap), BF16),
                    sds((rows, reach), BF16),
                    sds((rows, reach), BF16),
                    sds((rows, 2 * rows), BF16),
                    sds((live_cap, live_cap), F32),
                    sds((8, 128), F32),
                    sds((width, head_dim), BF16),
                ),
                [SMEM] + [VMEM] * 3 + [ANY],
                [pltpu.VMEM((n, 1, rows), F32), pltpu.VMEM((head_dim, width), BF16), pltpu.SemaphoreType.DMA],
            )(meta, *orders, pick, w_out)

        received, (pick_in, pick_out, even, odd, tile, live, most, w_cols) = exchange(message, index)
        compact, weights, att, stats, coef_c, d_mixed, negatives = kernel_call(
            functools.partial(forward_kernel, (n, rows, slots, per)),
            (
                sds((live_cap, wide), BF16),
                sds((live_cap, live_cap), BF16),
                sds((live_cap, head_dim), F32),
                sds((8, live_cap), F32),
                sds((negs, live_cap), BF16),
                sds((live_cap, head_dim), F32),
                sds((negs, width), BF16),
            ),
            [SMEM] + [VMEM] * (3 + n),
            [pltpu.VMEM((n, 8, width), F32)],
        )(meta, pick_in, live, w_cols, *received)
        paired = merge_stats(stats, swap(stats, "seq", 1), head_dim)
        paired = jnp.stack(list(paired) + [jnp.zeros_like(stats[0])] * 4)
        far = [swap(paired, "seq", d) for d in range(n - 2, 0, -2)]
        *back, mixed = kernel_call(
            functools.partial(backward_kernel, (n, rows, pool)),
            (sds((pool, wide), BF16),) * half + (sds((live_cap, head_dim), BF16),),
            [SMEM] + [VMEM] * 10,
            [pltpu.VMEM((live_cap + 2 * rows, head_dim), F32)],
        )(meta, compact, weights, att, d_mixed, paired, *far, pick_out, live)

        def group_sums():
            sums = kernel_call(sums_kernel, sds((negs + 8, head_dim), F32), [VMEM] * 3)(coef_c, mixed, most)
            sums = [sums] + [swap(sums, "dp", d) for d in range(1, groups)]
            d_w, most_of_all, kit = kernel_call(
                total_kernel,
                (sds((head_dim, width // groups), F32), sds((8, 128), F32), sds((width + rows, width), BF16)),
                [SMEM] + [VMEM] * 4 + [ANY] + [VMEM] * groups,
                [pltpu.SemaphoreType.DMA],
            )(meta, even, odd, tile, negatives, w_out, *sums)
            return d_w, kit, most_of_all

        returned, (d_w, kit, most_of_all) = exchange(back, group_sums)
        return most_of_all[0, 0] > 0.0, (d_w, kit, *returned)

    def finish(d_w, *parts):
        outs = kernel_call(
            functools.partial(finish_kernel, (n, rows)),
            (sds((rows, PARTS * width), BF16), sds((rows, width), BF16)),
            [SMEM] + [VMEM] * (1 + n),
        )(meta, *parts)
        return (*outs, d_w)

    overflow, parts = passes(SLOTS, POOL)
    d_home, layer_out, d_w_out = lax.cond(
        overflow, lambda *_: finish(*passes(rows, 2 * rows + 2 * quarter)[1]), lambda *outs: outs, *finish(*parts)
    )
    return (layer_out, d_home, d_w_out)


def solution(mesh):
    placed = (
        P(("dp", "seq"), None),
        P(),
        P(("dp", "seq"), None),
        P("seq", None),
        P("seq"),
        P(("dp", "seq"), None),
        P(("dp", "seq"), None),
        P("dp", None),
    )
    return jax.shard_map(
        head_plan if mesh.shape["seq"] == HEADS else tile_plan,
        mesh=mesh,
        in_specs=placed,
        out_specs=(P(("dp", "seq"), None), P(("dp", "seq"), None), P("seq", "dp")),
        check_vma=False,
    )
```

```python
import functools
import math

import jax
import jax.numpy as jnp
from jax import lax
from jax.experimental import pallas as pl
from jax.experimental.pallas import tpu as pltpu
from jax.sharding import PartitionSpec as P

HEADS = 8
SPAN = 3
PARTS = 4
SLOTS = 60
POOL = 152
LENS = 2


eps = 1e-05

VMEM = pl.BlockSpec(memory_space=pltpu.VMEM)
SMEM = pl.BlockSpec(memory_space=pltpu.SMEM)
ANY = pl.BlockSpec(memory_space=pl.ANY)
F32 = jnp.float32
BF16 = jnp.bfloat16


def shifted(block, axis, distance):
    devices = range(lax.axis_size(axis))
    route = [(i - distance, i) for i in devices if i - distance in devices]
    return lax.ppermute(block, axis, route)


def silu_grad(values):
    sigmoid_val = jax.nn.sigmoid(values)
    return sigmoid_val * (1.0 + values * (1.0 - sigmoid_val))


def pair_mask(count, len_p, len_q, allowed, causal):
    positions = jnp.arange(count, dtype=jnp.int32)
    live = (positions[:, None] < len_p) & (positions[None, :] < len_q) & allowed
    if causal:
        live = live & (positions[None, :] <= positions[:, None])
    return jnp.where(live, 1.0, 0.0).astype(jnp.float32)


def head_major(flat, count, head_dim):
    return flat.reshape(count, HEADS, head_dim).transpose(1, 0, 2)


def row_major(heads_first, count, width):
    return heads_first.transpose(1, 0, 2).reshape(count, width)


def tile_plan(qkvu, w_out, head_coef, item_table, neg_ids, send_order, recv_order, tile_len):
    row_count = qkvu.shape[0]
    model_width = w_out.shape[0]
    head_dim = model_width // HEADS
    score_scale = 1.0 / math.sqrt(head_dim)
    send_list = send_order[0]
    recv_list = recv_order[0]
    own_index = lax.axis_index("seq")
    lengths_row = tile_len[0]
    own_len = jnp.take(lengths_row, own_index)
    outgoing = jnp.take(qkvu, send_list, axis=0)
    received = lax.all_to_all(outgoing, "seq", split_axis=0, concat_axis=0, tiled=True)
    balanced = jnp.take(received, recv_list, axis=0)
    neg_all = lax.all_gather(jnp.take(item_table, neg_ids, axis=0), "seq", axis=0, tiled=True)
    u_part = balanced[:, :model_width].astype(jnp.float32)
    value_heads = head_major(balanced[:, model_width : 2 * model_width], row_count, head_dim)
    query_heads = head_major(balanced[:, 2 * model_width : 3 * model_width], row_count, head_dim)
    key_heads = head_major(balanced[:, 3 * model_width :], row_count, head_dim)
    lagged = []
    carried = (value_heads, key_heads)
    for lag in range(1, SPAN):
        carried = shifted((carried[0], carried[1]), "seq", 1)
        lagged.append(carried)
    value_list = [value_heads]
    key_list = [key_heads]
    mask_list = [pair_mask(row_count, own_len, own_len, True, True)]
    for lag in range(1, SPAN):
        earlier_len = jnp.take(lengths_row, jnp.maximum(own_index - lag, 0))
        value_list.append(lagged[lag - 1][0])
        key_list.append(lagged[lag - 1][1])
        mask_list.append(pair_mask(row_count, own_len, earlier_len, own_index >= lag, False))
    values_all = jnp.concatenate(value_list, axis=1)
    keys_all = jnp.concatenate(key_list, axis=1)
    mask_all = jnp.concatenate(mask_list, axis=1)
    scores = (
        jnp.einsum("hpd,hqd->hpq", query_heads, keys_all, preferred_element_type=jnp.float32)
        * score_scale
    )
    weights = (jax.nn.silu(scores) * mask_all[None] / row_count).astype(jnp.bfloat16)
    attended_heads = jnp.einsum(
        "hpq,hqd->hpd", weights, values_all, preferred_element_type=jnp.float32
    )
    attended = row_major(attended_heads, row_count, model_width)
    row_mean = jnp.mean(attended, axis=1, keepdims=True)
    centered = attended - row_mean
    variance = jnp.mean(centered * centered, axis=1, keepdims=True)
    inv_std = lax.rsqrt(variance + eps)
    normed = centered * inv_std
    mixed_rows = (normed * u_part).astype(jnp.bfloat16)
    layer_out = jnp.dot(mixed_rows, w_out, preferred_element_type=jnp.float32).astype(jnp.bfloat16)
    positions = jnp.arange(row_count, dtype=jnp.int32)
    live_col = jnp.where(positions < own_len, 1.0, 0.0).astype(jnp.float32)[:, None]
    coef_live = (head_coef * live_col).astype(jnp.bfloat16)
    head_grad = jnp.dot(coef_live, neg_all, preferred_element_type=jnp.float32).astype(jnp.bfloat16)
    d_mixed = lax.dot_general(
        head_grad, w_out, (((1,), (1,)), ((), ())), preferred_element_type=jnp.float32
    )
    d_u_part = d_mixed * normed
    d_normed = d_mixed * u_part
    d_att = (
        d_normed
        - jnp.mean(d_normed, axis=1, keepdims=True)
        - normed * jnp.mean(d_normed * normed, axis=1, keepdims=True)
    ) * inv_std
    d_att_heads = head_major(d_att.astype(jnp.bfloat16), row_count, head_dim)
    d_weights = jnp.einsum(
        "hpd,hqd->hpq", d_att_heads, values_all, preferred_element_type=jnp.float32
    )
    d_scores = (d_weights * mask_all[None] / row_count * silu_grad(scores) * score_scale).astype(
        jnp.bfloat16
    )
    d_query = jnp.einsum("hpq,hqd->hpd", d_scores, keys_all, preferred_element_type=jnp.float32)
    part_keys = jnp.einsum(
        "hpq,hpd->hqd", d_scores, query_heads, preferred_element_type=jnp.float32
    )
    part_values = jnp.einsum(
        "hpq,hpd->hqd", weights, d_att_heads, preferred_element_type=jnp.float32
    )
    key_grad = part_keys[:, :row_count]
    value_grad = part_values[:, :row_count]
    for lag in range(1, SPAN):
        block_keys = part_keys[:, lag * row_count : (lag + 1) * row_count].astype(jnp.bfloat16)
        block_values = part_values[:, lag * row_count : (lag + 1) * row_count].astype(jnp.bfloat16)
        back_values, back_keys = shifted((block_values, block_keys), "seq", -lag)
        key_grad = key_grad + back_keys.astype(jnp.float32)
        value_grad = value_grad + back_values.astype(jnp.float32)
    tile_grads = jnp.concatenate(
        [
            d_u_part,
            row_major(value_grad, row_count, model_width),
            row_major(d_query, row_count, model_width),
            row_major(key_grad, row_count, model_width),
        ],
        axis=1,
    ).astype(jnp.bfloat16)
    slot_grads = jnp.zeros_like(tile_grads).at[recv_list].set(tile_grads)
    returned = lax.all_to_all(slot_grads, "seq", split_axis=0, concat_axis=0, tiled=True)
    d_home = jnp.zeros_like(returned).at[send_list].set(returned)
    coef_sums = lax.psum_scatter(
        lax.dot_general(
            mixed_rows, coef_live, (((0,), (0,)), ((), ())), preferred_element_type=jnp.float32
        ),
        "seq",
        scatter_dimension=0,
        tiled=True,
    )
    row_grad = jnp.dot(coef_sums, neg_all.astype(jnp.float32), precision=lax.Precision.HIGHEST)
    d_w_out = lax.psum_scatter(
        row_grad.astype(jnp.bfloat16), "dp", scatter_dimension=1, tiled=True
    ).astype(jnp.float32)
    return (layer_out, d_home, d_w_out)


def dot(a, b, dims=((1,), (0,))):
    return lax.dot_general(a, b, (dims, ((), ())), preferred_element_type=F32)


def iota(shape, dim):
    return lax.broadcasted_iota(jnp.int32, shape, dim)


def starts_of(meta, count):
    starts = [jnp.int32(0)]
    for t in range(count):
        starts.append(starts[-1] + meta[LENS + t])
    return starts


def tile_of(position, starts):
    tile = jnp.zeros(position.shape, jnp.int32)
    for start in starts[1:-1]:
        tile = tile + jnp.where(position >= start, 1, 0)
    return tile


def one_hot(condition):
    return jnp.where(condition, 1.0, 0.0).astype(BF16)


def slot_table(meta, blocks, order_ref):
    n, _, rows = order_ref.shape
    cell = rows // n
    for b in range(n):
        order_ref[meta[0] ^ b] = blocks[b // (n // 2)][b % (n // 2) : b % (n // 2) + 1].astype(F32)
    starts = starts_of(meta, n)
    pos = iota((cell, rows), 1)
    filled = [jnp.broadcast_to(order_ref[t], (cell, rows)) for t in range(n)]
    value = [jnp.where(pos < meta[LENS + t], pos + starts[t] + 1, 0).astype(F32) for t in range(n)]
    return jnp.concatenate(filled, axis=0), jnp.concatenate(value, axis=0)


def slot_places(filled, value, source, cell):
    slot = (iota(filled.shape, 0) % cell + source * cell).astype(F32)
    return jnp.sum(jnp.where(filled == slot, value, 0.0), axis=1, keepdims=True)


def slot_ranks(places):
    rows = places.shape[0]
    live = places > 0.5
    before = dot(one_hot(iota((rows, rows), 1) < iota((rows, rows), 0)), one_hot(live))
    return jnp.where(live, before, -1.0)


def put_rows(me, head_dim, picked, outs):
    width = picked.shape[1] // PARTS
    for x in range(2 * len(outs)):
        first = pl.multiple_of((me ^ x) * head_dim, head_dim)
        outs[x // 2][x % 2] = jnp.concatenate([picked[:, pl.ds(i * width + first, head_dim)] for i in range(PARTS)], axis=1)


def prep_kernel(ids, send, coef_t, table, qkvu, held, below, home, send_row, coef_rows, items, neg_rows, sems):
    per, chunk, width = items.shape
    rows = send_row.shape[1]
    wide = below.shape[1]
    copies = [
        pltpu.make_async_copy(source, target, sems.at[i])
        for i, (source, target) in enumerate(((send, send_row), (coef_t, coef_rows), (qkvu, held)))
    ]
    for j in range(per):
        start = pl.multiple_of((ids[j] // chunk) * chunk, chunk)
        copies.append(pltpu.make_async_copy(table.at[pl.ds(start, chunk)], items.at[j], sems.at[3 + j]))
    for copy in copies:
        copy.start()
    lane = iota((rows, rows), 1)
    copies[0].wait()
    own = jnp.where(lane == iota((rows, rows), 0), send_row[...].astype(F32), 0.0)
    home[...] = one_hot(jnp.sum(own, axis=1, keepdims=True) == lane.astype(F32))
    copies[1].wait()
    for j in range(per):
        copies[3 + j].wait()
        own = iota((chunk, width), 0) == ids[j] % chunk
        neg_rows[j : j + 1] = jnp.sum(jnp.where(own, items[j].astype(F32), 0.0), axis=0, keepdims=True)
    step = coef_rows.shape[0] * rows // wide
    coefs = jnp.concatenate([coef_rows[b * step : (b + 1) * step].astype(F32) for b in range(wide // rows)], axis=1)
    negs = jnp.concatenate([neg_rows[0:per, b * wide : (b + 1) * wide] for b in range(width // wide)], axis=0)
    below[...] = jnp.concatenate([coefs, negs], axis=0).astype(BF16)
    copies[2].wait()


def pack_kernel(sizes, meta, b0, b1, held, below, home, *refs):
    n, rows, slots = sizes
    pairs = n // 2
    outs = refs[:pairs]
    pick, order_ref = refs[pairs:]
    head_dim = outs[0].shape[1] // PARTS
    width = head_dim * n
    cell = rows // n
    me = meta[0]
    filled, value = slot_table(meta, (b0, b1), order_ref)
    places = jnp.broadcast_to(slot_places(filled, value, me, cell), (rows, rows))
    by_rank = one_hot(slot_ranks(places) == iota((rows, rows), 1).astype(F32))
    chosen = dot(by_rank, home[...], ((0,), (0,)))
    pick[...] = chosen.astype(BF16)
    none = jnp.zeros((slots, rows), F32)
    both = jnp.concatenate(
        [jnp.concatenate([chosen[0:slots], none], axis=1), jnp.concatenate([none, chosen[0:slots]], axis=1)], axis=0
    ).astype(BF16)
    for d in range(pairs):
        columns = []
        for x in (2 * d, 2 * d + 1):
            first = pl.multiple_of((me ^ x) * head_dim, head_dim)
            columns.append(jnp.concatenate([held[:, pl.ds(i * width + first, head_dim)] for i in range(PARTS)], axis=1))
        outs[d][0 : 2 * slots] = dot(both, jnp.concatenate(columns, axis=0)).astype(BF16)
        outs[d][2 * slots :] = below[...]


def index_kernel(sizes, meta, b0, b1, pick, w_out, pick_in, pick_out, home_even, home_odd, tile, live, most, w_cols, order_ref, w_rows, sem):
    n, rows, slots, pool = sizes
    cell = rows // n
    live_cap = live.shape[0]
    head_dim = w_rows.shape[0]
    copy = pltpu.make_async_copy(w_out.at[pl.ds(pl.multiple_of(meta[0] * head_dim, head_dim), head_dim)], w_rows, sem)
    copy.start()
    span = pick_in.shape[1] // n
    me = meta[0]
    filled, value = slot_table(meta, (b0, b1), order_ref)
    lane = iota((rows, rows), 1)
    columns = [slot_places(filled, value, me ^ x, cell) for x in range(n)]
    places = jnp.zeros((rows, rows), F32)
    for x in range(n):
        places = jnp.where(lane == x, columns[x], places)
    ranks = slot_ranks(places)
    count = jnp.sum(jnp.where(places > 0.5, 1.0, 0.0), axis=0, keepdims=True)
    counts = [count[:, x : x + 1] for x in range(n)]
    lines_of = [pair_lines(meta, (me >> 1) ^ d) for d in range(n // 2)]
    excess = [c - slots for c in counts] + [counts[2 * d] + counts[2 * d + 1] + (lines_of[d] - pool).astype(F32) for d in range(n // 2)]
    most[...] = jnp.broadcast_to(functools.reduce(jnp.maximum, excess), most.shape)

    def placed(x, first, width):
        at = ranks[:, x : x + 1] + first
        hit = jnp.where(at == iota((rows, width), 1).astype(F32), columns[x], 0.0)
        return jnp.sum(hit, axis=0, keepdims=True)

    lines = []
    for x in range(n):
        first = span - slots if x % 2 else 0
        line = placed(x, first, max(span, rows))[:, :span]
        at = iota((1, span), 1)
        lines.append(jnp.where((at >= first) & (at < first + slots), line, 0.0))
    line = jnp.concatenate(lines, axis=1) - 1.0
    pick_in[...] = one_hot(iota((live_cap, line.shape[1]), 0).astype(F32) == line)
    reach = -(-pool // rows) * rows
    for d in range(n // 2):
        first = lines_of[d].astype(F32)
        line = placed(2 * d, first, reach) + placed(2 * d + 1, counts[2 * d] + first, reach) - 1.0
        hit = one_hot(iota((live_cap, reach), 0).astype(F32) == line)
        pick_out[d * pool : (d + 1) * pool] = jnp.transpose(hit.astype(F32))[:pool].astype(BF16)
    slot = iota((reach, rows), 0).astype(F32)
    for home, first in ((home_even, jnp.zeros((1, 1), F32)), (home_odd, counts[1])):
        first = first + lines_of[0].astype(F32)
        moved = dot(one_hot(slot == lane[0:1].astype(F32) + first), pick[...])
        home[...] = jnp.transpose(moved).astype(BF16)
    quarter = tile.shape[1] // PARTS
    line = iota((rows, quarter), 1)
    row = iota((rows, quarter), 0)
    before = jnp.where(me % 2 == 1, meta[LENS + (me ^ 1)], 0)
    for b in range(PARTS):
        hit = (line + b * lines_of[0] == row + before) & (line < lines_of[0]) & (row < meta[LENS + me])
        tile[:, b * quarter : (b + 1) * quarter] = one_hot(hit)
    copy.wait()
    w_cols[...] = jnp.transpose(w_rows[...].astype(F32)).astype(BF16)
    live[...] = jnp.where(pair_live(live_cap, starts_of(meta, n)), 1.0 / rows, 0.0)


def pair_live(live_cap, starts):
    row = iota((live_cap, 1), 0)
    col = iota((1, live_cap), 1)
    return (col <= row) & (tile_of(col, starts) > tile_of(row, starts) - SPAN) & (row < starts[-1])


def forward_kernel(sizes, meta, pick, live, w_cols, *refs):
    n, rows, slots, per = sizes
    blocks = refs[:n]
    compact, weights, att, stats, coef_c, d_mixed, negatives, neg_rows = refs[n:]
    live_cap, head_dim = att.shape
    negs = coef_c.shape[0]
    wide = blocks[0].shape[1]
    span = pick.shape[1] // n
    me = meta[0]
    received = [block[2 * slots - span : 2 * slots] if x % 2 else block[0:span] for x, block in enumerate(blocks)]
    both = dot(pick[...], jnp.concatenate(received, axis=0)).astype(BF16)
    compact[...] = both
    total = jnp.zeros((negs, live_cap), F32)
    lane = iota((negs, live_cap), 1)
    step = negs * rows // wide
    for x in range(n):
        t = me ^ x
        start = start_of(meta, n, t)
        below = blocks[x][2 * slots :].astype(F32)
        coefs = jnp.concatenate([below[0:step, b * rows : (b + 1) * rows] for b in range(wide // rows)], axis=0)
        coefs = jnp.concatenate([coefs, jnp.zeros((negs, live_cap - rows), F32)], axis=1)
        total = jnp.where((lane >= start) & (lane < start + meta[LENS + t]), pltpu.roll(coefs, start, 1), total)
        for b in range(n * head_dim // wide):
            neg_rows[t, 0:per, b * wide : (b + 1) * wide] = below[step + b * per : step + (b + 1) * per]
    coef_t = total.astype(BF16)
    coef_c[...] = coef_t
    neg = jnp.concatenate([neg_rows[s, 0:per] for s in range(n)], axis=0).astype(BF16)
    negatives[...] = neg
    head_grad = dot(coef_t, neg, ((0,), (0,))).astype(BF16)
    dm = dot(head_grad, w_cols[...])
    d_mixed[...] = dm
    u, v, q, k = (both[:, i * head_dim : (i + 1) * head_dim] for i in range(PARTS))
    scores = dot(q, k, ((1,), (1,))) * (1.0 / math.sqrt(head_dim))
    sig = jax.nn.sigmoid(scores)
    w = (scores * sig * live[...]).astype(BF16)
    weights[...] = w
    a = dot(w, v)
    att[...] = a
    dn = dm * u.astype(F32)
    mean = jnp.sum(a, axis=1, keepdims=True) * (1.0 / head_dim)
    cen = a - mean
    lane = iota((live_cap, 128), 1)
    cols = jnp.where(lane == 0, mean, 0.0)
    cols = jnp.where(lane == 1, jnp.sum(cen * cen, axis=1, keepdims=True), cols)
    cols = jnp.where(lane == 2, jnp.sum(dn, axis=1, keepdims=True), cols)
    cols = jnp.where(lane == 3, jnp.sum(dn * cen, axis=1, keepdims=True), cols)
    stats[...] = jnp.transpose(cols)[0:8]


def merge_stats(a, b, count):
    gap = b[0] - a[0]
    return (
        (a[0] + b[0]) * 0.5,
        a[1] + b[1] + gap * gap * (0.5 * count),
        a[2] + b[2],
        a[3] + b[3] + (b[2] - a[2]) * gap * 0.5,
    )


def pair_lines(meta, chip):
    return (meta[LENS + 2 * chip] + meta[LENS + 2 * chip + 1] + PARTS - 1) // PARTS


def start_of(meta, n, tile):
    start = jnp.int32(0)
    for t in range(n):
        start = start + jnp.where(t < tile, meta[LENS + t], 0)
    return start


def backward_kernel(sizes, meta, compact, weights, att, d_mixed, st0, st1, st2, st3, pick, live, *refs):
    n, rows, pool = sizes
    outs = refs[: n // 2]
    mixed_ref, mixed_rows = refs[n // 2 :]
    live_cap, head_dim = att.shape
    width = head_dim * n
    me = meta[0]
    quad = [[st[i : i + 1] for i in range(4)] for st in (st0, st1, st2, st3)]
    ab = merge_stats(quad[0], quad[1], 2 * head_dim)
    cd = merge_stats(quad[2], quad[3], 2 * head_dim)
    mean, m2, s_dn, s_dna = merge_stats(ab, cd, 4 * head_dim)
    inv = lax.rsqrt(m2 * (1.0 / width) + eps)
    table = jnp.concatenate([mean, inv, s_dn * (1.0 / width), s_dna * inv * (1.0 / width), jnp.zeros((124, live_cap), F32)], axis=0)
    table = jnp.transpose(table)
    mean, inv, mean_dn, mean_dnn = (table[:, i : i + 1] for i in range(4))
    both = compact[...]
    u, v, q, k = (both[:, i * head_dim : (i + 1) * head_dim] for i in range(PARTS))
    u = u.astype(F32)
    dm = d_mixed[...]
    normed = (att[...] - mean) * inv
    mixed = (normed * u).astype(BF16)
    dn = dm * u
    d_att = ((dn - mean_dn - normed * mean_dnn) * inv).astype(BF16)
    scale = 1.0 / math.sqrt(head_dim)
    scores = dot(q, k, ((1,), (1,))) * scale
    sig = jax.nn.sigmoid(scores)
    slope = sig * (1.0 + scores * (1.0 - sig)) * scale * live[...]
    ds = (dot(d_att, v, ((1,), (1,))) * slope).astype(BF16)
    grad = jnp.concatenate(
        [dm * normed, dot(weights[...], d_att, ((0,), (0,))), dot(ds, k), dot(ds, q, ((0,), (0,)))], axis=1
    ).astype(BF16)
    mixed_ref[...] = mixed
    sent = dot(pick[...], grad)
    mixed_rows[0:live_cap] = mixed.astype(F32)
    mixed_rows[live_cap:] = jnp.zeros((2 * rows, head_dim), F32)
    half = 2 * rows // PARTS
    row = iota((half, head_dim), 0)
    for d in range(n // 2):
        chip = (me >> 1) ^ d
        lines = pair_lines(meta, chip)
        count = meta[LENS + 2 * chip] + meta[LENS + 2 * chip + 1]
        parts = []
        for b in range(PARTS):
            part = mixed_rows[pl.ds(start_of(meta, n, 2 * chip) + b * lines, half), :]
            parts.append(jnp.where((row < lines) & (row + b * lines < count), part, 0.0))
        rows_out = sent[d * pool : (d + 1) * pool]
        outs[d][0:half] = (rows_out[0:half] + jnp.concatenate(parts, axis=1)).astype(BF16)
        outs[d][half:] = rows_out[half:].astype(BF16)


def sums_kernel(coef_c, mixed, most, sums):
    negs = coef_c.shape[0]
    sums[0:negs] = dot(coef_c[...], mixed[...])
    sums[negs:] = most[...]


def total_kernel(meta, even, odd, tile, negatives, w_out, *refs):
    sums, (d_w_out, most, kit, sem) = refs[:-4], refs[-4:]
    width = w_out.shape[0]
    copy = pltpu.make_async_copy(w_out, kit.at[pl.ds(0, width)], sem)
    copy.start()
    rows, reach = even.shape
    kit[width:, 0:reach] = even[...]
    kit[width:, reach : 2 * reach] = odd[...]
    kit[width:, 2 * reach : 2 * reach + 2 * rows] = tile[...]
    negs, groups = negatives.shape[0], len(sums)
    most[...] = functools.reduce(jnp.maximum, [part[negs:] for part in sums])
    rest = functools.reduce(jnp.add, [part[0:negs] for part in sums])
    columns = width // groups
    neg = negatives[:, pl.ds(pl.multiple_of(meta[1] * columns, columns), columns)]
    grad = jnp.zeros((rest.shape[1], columns), F32)
    for _ in range(3):
        piece = rest.astype(BF16)
        grad = grad + dot(piece, neg, ((0,), (0,)))
        rest = rest - piece.astype(F32)
    d_w_out[...] = grad
    copy.wait()


def finish_kernel(sizes, meta, kit, *refs):
    n, rows = sizes
    blocks, (d_home, layer_out) = refs[:n], refs[n:]
    width = kit.shape[1]
    head_dim = width // n
    quarter = rows // PARTS
    reach = -(-blocks[0].shape[0] // rows) * rows
    for x in range(n):
        head = pl.multiple_of((meta[0] ^ x) * head_dim, head_dim)
        block = blocks[x][...]
        pick = kit[width:, reach * (x % 2) : reach * (x % 2) + block.shape[0]]
        part = dot(pick, block).astype(BF16)
        for i in range(PARTS):
            d_home[:, pl.ds(i * width + head, head_dim)] = part[:, i * head_dim : (i + 1) * head_dim]
        lines = jnp.concatenate([block[0 : 2 * quarter, b * head_dim : (b + 1) * head_dim] for b in range(PARTS)], axis=0)
        layer_out[:, pl.ds(head, head_dim)] = dot(kit[width:, 2 * reach : 2 * reach + 2 * rows], lines).astype(BF16)
    layer = dot(layer_out[...], kit[0:width])
    layer_out[...] = layer.astype(BF16)


def kernel_call(body, shapes, specs, scratch=(), limit=40):
    return pl.pallas_call(
        body,
        out_shape=shapes,
        in_specs=specs,
        out_specs=jax.tree.map(lambda _: VMEM, shapes),
        scratch_shapes=scratch,
        compiler_params=pltpu.CompilerParams(vmem_limit_bytes=limit * 1024 * 1024),
    )


def swap(block, axis, distance):
    return lax.ppermute(block, axis, [(i, i ^ distance) for i in range(lax.axis_size(axis))])


def exchange(message, between):
    order = (1, 3, 2)
    far = {d: swap(message[d], "seq", 2 * d) for d in order}
    made = between()
    far[0] = message[0]
    far[order[-1]], made = lax.optimization_barrier((far[order[-1]], made))
    near = {d: swap(far[d], "seq", 1) for d in (0, *order)}
    blocks = [block for d in range(len(message)) for block in (far[d], near[d])]
    return blocks, made


def load_kernel(block, out):
    out[...] = block[...]


def join_kernel(first, second, out):
    out[0 : first.shape[0]] = first[...]
    out[first.shape[0] :] = second[...]


def gather_small(block, between):
    n = lax.axis_size("seq")
    known, distance = kernel_call(load_kernel, jax.ShapeDtypeStruct(block.shape, block.dtype), [VMEM])(block), 1
    while distance < n // 2:
        shape = jax.ShapeDtypeStruct((2 * known.shape[0], known.shape[1]), known.dtype)
        known = kernel_call(join_kernel, shape, [VMEM] * 2)(known, swap(block if distance == 1 else known, "seq", distance))
        distance *= 2
    known, made = lax.optimization_barrier((known, between()))
    return [known, swap(known, "seq", distance)], made


def head_plan(qkvu, w_out, head_coef, item_table, neg_ids, send_order, recv_order, tile_len):
    n = lax.axis_size("seq")
    groups = lax.axis_size("dp")
    rows = qkvu.shape[0]
    width = w_out.shape[0]
    head_dim = width // HEADS
    negs = head_coef.shape[1]
    per = neg_ids.shape[0]
    wide = PARTS * head_dim
    live_cap = -(-(n * rows // 3) // 128) * 128
    sds = jax.ShapeDtypeStruct
    me = lax.axis_index("seq")
    meta = jnp.concatenate([jnp.stack([me, lax.axis_index("dp")]).astype(jnp.int32), tile_len[0]])
    head_coef_t = head_coef.T

    half = n // 2
    quarter = rows // PARTS
    below = (negs * rows + per * width) // wide

    def passes(slots, pool):
        span = -(-slots // 8) * 8
        reach = -(-pool // rows) * rows
        def prep():
            return kernel_call(
                prep_kernel,
                (sds(qkvu.shape, BF16), sds((below, wide), BF16), sds((rows, rows), BF16)),
                [SMEM] + [ANY] * 4,
                [
                    pltpu.VMEM((1, rows), jnp.int32),
                    pltpu.VMEM((negs, rows), BF16),
                    pltpu.VMEM((per, 16, width), BF16),
                    pltpu.VMEM((8, width), F32),
                    pltpu.SemaphoreType.DMA((3 + per,)),
                ],
            )(neg_ids, send_order, head_coef_t, item_table, qkvu)

        orders, prepared = gather_small(recv_order, prep)
        *message, pick = kernel_call(
            functools.partial(pack_kernel, (n, rows, slots)),
            (sds((2 * slots + below, wide), BF16),) * half + (sds((rows, rows), BF16),),
            [SMEM] + [VMEM] * 5,
            [pltpu.VMEM((n, 1, rows), F32)],
        )(meta, *orders, *prepared)

        def index():
            return kernel_call(
                functools.partial(index_kernel, (n, rows, slots, pool)),
                (
                    sds((live_cap, n * span), BF16),
                    sds((half * pool, live_cap), BF16),
                    sds((rows, reach), BF16),
                    sds((rows, reach), BF16),
                    sds((rows, 2 * rows), BF16),
                    sds((live_cap, live_cap), F32),
                    sds((8, 128), F32),
                    sds((width, head_dim), BF16),
                ),
                [SMEM] + [VMEM] * 3 + [ANY],
                [pltpu.VMEM((n, 1, rows), F32), pltpu.VMEM((head_dim, width), BF16), pltpu.SemaphoreType.DMA],
            )(meta, *orders, pick, w_out)

        received, (pick_in, pick_out, even, odd, tile, live, most, w_cols) = exchange(message, index)
        compact, weights, att, stats, coef_c, d_mixed, negatives = kernel_call(
            functools.partial(forward_kernel, (n, rows, slots, per)),
            (
                sds((live_cap, wide), BF16),
                sds((live_cap, live_cap), BF16),
                sds((live_cap, head_dim), F32),
                sds((8, live_cap), F32),
                sds((negs, live_cap), BF16),
                sds((live_cap, head_dim), F32),
                sds((negs, width), BF16),
            ),
            [SMEM] + [VMEM] * (3 + n),
            [pltpu.VMEM((n, 8, width), F32)],
        )(meta, pick_in, live, w_cols, *received)
        paired = merge_stats(stats, swap(stats, "seq", 1), head_dim)
        paired = jnp.stack(list(paired) + [jnp.zeros_like(stats[0])] * 4)
        far = [swap(paired, "seq", d) for d in range(n - 2, 0, -2)]
        *back, mixed = kernel_call(
            functools.partial(backward_kernel, (n, rows, pool)),
            (sds((pool, wide), BF16),) * half + (sds((live_cap, head_dim), BF16),),
            [SMEM] + [VMEM] * 10,
            [pltpu.VMEM((live_cap + 2 * rows, head_dim), F32)],
        )(meta, compact, weights, att, d_mixed, paired, *far, pick_out, live)

        def group_sums():
            sums = kernel_call(sums_kernel, sds((negs + 8, head_dim), F32), [VMEM] * 3)(coef_c, mixed, most)
            sums = [sums] + [swap(sums, "dp", d) for d in range(1, groups)]
            d_w, most_of_all, kit = kernel_call(
                total_kernel,
                (sds((head_dim, width // groups), F32), sds((8, 128), F32), sds((width + rows, width), BF16)),
                [SMEM] + [VMEM] * 4 + [ANY] + [VMEM] * groups,
                [pltpu.SemaphoreType.DMA],
            )(meta, even, odd, tile, negatives, w_out, *sums)
            return d_w, kit, most_of_all

        returned, (d_w, kit, most_of_all) = exchange(back, group_sums)
        return most_of_all[0, 0] > 0.0, (d_w, kit, *returned)

    def finish(d_w, *parts):
        outs = kernel_call(
            functools.partial(finish_kernel, (n, rows)),
            (sds((rows, PARTS * width), BF16), sds((rows, width), BF16)),
            [SMEM] + [VMEM] * (1 + n),
        )(meta, *parts)
        return (*outs, d_w)

    overflow, parts = passes(SLOTS, POOL)
    d_home, layer_out, d_w_out = lax.cond(
        overflow, lambda *_: finish(*passes(rows, 2 * rows + 2 * quarter)[1]), lambda *outs: outs, *finish(*parts)
    )
    return (layer_out, d_home, d_w_out)


def solution(mesh):
    placed = (
        P(("dp", "seq"), None),
        P(),
        P(("dp", "seq"), None),
        P("seq", None),
        P("seq"),
        P(("dp", "seq"), None),
        P(("dp", "seq"), None),
        P("dp", None),
    )
    return jax.shard_map(
        head_plan if mesh.shape["seq"] == HEADS else tile_plan,
        mesh=mesh,
        in_specs=placed,
        out_specs=(P(("dp", "seq"), None), P(("dp", "seq"), None), P("seq", "dp")),
        check_vma=False,
    )
```

```python
import functools
import math

import jax
import jax.numpy as jnp
from jax import lax
from jax.experimental import pallas as pl
from jax.experimental.pallas import tpu as pltpu
from jax.sharding import PartitionSpec as P

HEADS = 8
SPAN = 3
PARTS = 4
SLOTS = 60
POOL = 152
LENS = 2


eps = 1e-05

VMEM = pl.BlockSpec(memory_space=pltpu.VMEM)
SMEM = pl.BlockSpec(memory_space=pltpu.SMEM)
ANY = pl.BlockSpec(memory_space=pl.ANY)
F32 = jnp.float32
BF16 = jnp.bfloat16


def shifted(block, axis, distance):
    devices = range(lax.axis_size(axis))
    route = [(i - distance, i) for i in devices if i - distance in devices]
    return lax.ppermute(block, axis, route)


def silu_grad(values):
    sigmoid_val = jax.nn.sigmoid(values)
    return sigmoid_val * (1.0 + values * (1.0 - sigmoid_val))


def pair_mask(count, len_p, len_q, allowed, causal):
    positions = jnp.arange(count, dtype=jnp.int32)
    live = (positions[:, None] < len_p) & (positions[None, :] < len_q) & allowed
    if causal:
        live = live & (positions[None, :] <= positions[:, None])
    return jnp.where(live, 1.0, 0.0).astype(jnp.float32)


def head_major(flat, count, head_dim):
    return flat.reshape(count, HEADS, head_dim).transpose(1, 0, 2)


def row_major(heads_first, count, width):
    return heads_first.transpose(1, 0, 2).reshape(count, width)


def tile_plan(qkvu, w_out, head_coef, item_table, neg_ids, send_order, recv_order, tile_len):
    row_count = qkvu.shape[0]
    model_width = w_out.shape[0]
    head_dim = model_width // HEADS
    score_scale = 1.0 / math.sqrt(head_dim)
    send_list = send_order[0]
    recv_list = recv_order[0]
    own_index = lax.axis_index("seq")
    lengths_row = tile_len[0]
    own_len = jnp.take(lengths_row, own_index)
    outgoing = jnp.take(qkvu, send_list, axis=0)
    received = lax.all_to_all(outgoing, "seq", split_axis=0, concat_axis=0, tiled=True)
    balanced = jnp.take(received, recv_list, axis=0)
    neg_all = lax.all_gather(jnp.take(item_table, neg_ids, axis=0), "seq", axis=0, tiled=True)
    u_part = balanced[:, :model_width].astype(jnp.float32)
    value_heads = head_major(balanced[:, model_width : 2 * model_width], row_count, head_dim)
    query_heads = head_major(balanced[:, 2 * model_width : 3 * model_width], row_count, head_dim)
    key_heads = head_major(balanced[:, 3 * model_width :], row_count, head_dim)
    lagged = []
    carried = (value_heads, key_heads)
    for lag in range(1, SPAN):
        carried = shifted((carried[0], carried[1]), "seq", 1)
        lagged.append(carried)
    value_list = [value_heads]
    key_list = [key_heads]
    mask_list = [pair_mask(row_count, own_len, own_len, True, True)]
    for lag in range(1, SPAN):
        earlier_len = jnp.take(lengths_row, jnp.maximum(own_index - lag, 0))
        value_list.append(lagged[lag - 1][0])
        key_list.append(lagged[lag - 1][1])
        mask_list.append(pair_mask(row_count, own_len, earlier_len, own_index >= lag, False))
    values_all = jnp.concatenate(value_list, axis=1)
    keys_all = jnp.concatenate(key_list, axis=1)
    mask_all = jnp.concatenate(mask_list, axis=1)
    scores = (
        jnp.einsum("hpd,hqd->hpq", query_heads, keys_all, preferred_element_type=jnp.float32)
        * score_scale
    )
    weights = (jax.nn.silu(scores) * mask_all[None] / row_count).astype(jnp.bfloat16)
    attended_heads = jnp.einsum(
        "hpq,hqd->hpd", weights, values_all, preferred_element_type=jnp.float32
    )
    attended = row_major(attended_heads, row_count, model_width)
    row_mean = jnp.mean(attended, axis=1, keepdims=True)
    centered = attended - row_mean
    variance = jnp.mean(centered * centered, axis=1, keepdims=True)
    inv_std = lax.rsqrt(variance + eps)
    normed = centered * inv_std
    mixed_rows = (normed * u_part).astype(jnp.bfloat16)
    layer_out = jnp.dot(mixed_rows, w_out, preferred_element_type=jnp.float32).astype(jnp.bfloat16)
    positions = jnp.arange(row_count, dtype=jnp.int32)
    live_col = jnp.where(positions < own_len, 1.0, 0.0).astype(jnp.float32)[:, None]
    coef_live = (head_coef * live_col).astype(jnp.bfloat16)
    head_grad = jnp.dot(coef_live, neg_all, preferred_element_type=jnp.float32).astype(jnp.bfloat16)
    d_mixed = lax.dot_general(
        head_grad, w_out, (((1,), (1,)), ((), ())), preferred_element_type=jnp.float32
    )
    d_u_part = d_mixed * normed
    d_normed = d_mixed * u_part
    d_att = (
        d_normed
        - jnp.mean(d_normed, axis=1, keepdims=True)
        - normed * jnp.mean(d_normed * normed, axis=1, keepdims=True)
    ) * inv_std
    d_att_heads = head_major(d_att.astype(jnp.bfloat16), row_count, head_dim)
    d_weights = jnp.einsum(
        "hpd,hqd->hpq", d_att_heads, values_all, preferred_element_type=jnp.float32
    )
    d_scores = (d_weights * mask_all[None] / row_count * silu_grad(scores) * score_scale).astype(
        jnp.bfloat16
    )
    d_query = jnp.einsum("hpq,hqd->hpd", d_scores, keys_all, preferred_element_type=jnp.float32)
    part_keys = jnp.einsum(
        "hpq,hpd->hqd", d_scores, query_heads, preferred_element_type=jnp.float32
    )
    part_values = jnp.einsum(
        "hpq,hpd->hqd", weights, d_att_heads, preferred_element_type=jnp.float32
    )
    key_grad = part_keys[:, :row_count]
    value_grad = part_values[:, :row_count]
    for lag in range(1, SPAN):
        block_keys = part_keys[:, lag * row_count : (lag + 1) * row_count].astype(jnp.bfloat16)
        block_values = part_values[:, lag * row_count : (lag + 1) * row_count].astype(jnp.bfloat16)
        back_values, back_keys = shifted((block_values, block_keys), "seq", -lag)
        key_grad = key_grad + back_keys.astype(jnp.float32)
        value_grad = value_grad + back_values.astype(jnp.float32)
    tile_grads = jnp.concatenate(
        [
            d_u_part,
            row_major(value_grad, row_count, model_width),
            row_major(d_query, row_count, model_width),
            row_major(key_grad, row_count, model_width),
        ],
        axis=1,
    ).astype(jnp.bfloat16)
    slot_grads = jnp.zeros_like(tile_grads).at[recv_list].set(tile_grads)
    returned = lax.all_to_all(slot_grads, "seq", split_axis=0, concat_axis=0, tiled=True)
    d_home = jnp.zeros_like(returned).at[send_list].set(returned)
    coef_sums = lax.psum_scatter(
        lax.dot_general(
            mixed_rows, coef_live, (((0,), (0,)), ((), ())), preferred_element_type=jnp.float32
        ),
        "seq",
        scatter_dimension=0,
        tiled=True,
    )
    row_grad = jnp.dot(coef_sums, neg_all.astype(jnp.float32), precision=lax.Precision.HIGHEST)
    d_w_out = lax.psum_scatter(
        row_grad.astype(jnp.bfloat16), "dp", scatter_dimension=1, tiled=True
    ).astype(jnp.float32)
    return (layer_out, d_home, d_w_out)


def dot(a, b, dims=((1,), (0,))):
    return lax.dot_general(a, b, (dims, ((), ())), preferred_element_type=F32)


def iota(shape, dim):
    return lax.broadcasted_iota(jnp.int32, shape, dim)


def starts_of(meta, count):
    starts = [jnp.int32(0)]
    for t in range(count):
        starts.append(starts[-1] + meta[LENS + t])
    return starts


def tile_of(position, starts):
    tile = jnp.zeros(position.shape, jnp.int32)
    for start in starts[1:-1]:
        tile = tile + jnp.where(position >= start, 1, 0)
    return tile


def one_hot(condition):
    return jnp.where(condition, 1.0, 0.0).astype(BF16)


def slot_table(meta, blocks, order_ref):
    n, _, rows = order_ref.shape
    cell = rows // n
    for b in range(n):
        order_ref[meta[0] ^ b] = blocks[b // (n // 2)][b % (n // 2) : b % (n // 2) + 1].astype(F32)
    starts = starts_of(meta, n)
    pos = iota((cell, rows), 1)
    filled = [jnp.broadcast_to(order_ref[t], (cell, rows)) for t in range(n)]
    value = [jnp.where(pos < meta[LENS + t], pos + starts[t] + 1, 0).astype(F32) for t in range(n)]
    return jnp.concatenate(filled, axis=0), jnp.concatenate(value, axis=0)


def slot_places(filled, value, source, cell):
    slot = (iota(filled.shape, 0) % cell + source * cell).astype(F32)
    return jnp.sum(jnp.where(filled == slot, value, 0.0), axis=1, keepdims=True)


def slot_ranks(places):
    rows = places.shape[0]
    live = places > 0.5
    before = dot(one_hot(iota((rows, rows), 1) < iota((rows, rows), 0)), one_hot(live))
    return jnp.where(live, before, -1.0)


def put_rows(me, head_dim, picked, outs):
    width = picked.shape[1] // PARTS
    for x in range(2 * len(outs)):
        first = pl.multiple_of((me ^ x) * head_dim, head_dim)
        outs[x // 2][x % 2] = jnp.concatenate([picked[:, pl.ds(i * width + first, head_dim)] for i in range(PARTS)], axis=1)


def prep_kernel(ids, send, coef_t, table, qkvu, held, below, home, send_row, coef_rows, items, neg_rows, sems):
    per, chunk, width = items.shape
    rows = send_row.shape[1]
    wide = below.shape[1]
    copies = [
        pltpu.make_async_copy(source, target, sems.at[i])
        for i, (source, target) in enumerate(((send, send_row), (coef_t, coef_rows), (qkvu, held)))
    ]
    for j in range(per):
        start = pl.multiple_of((ids[j] // chunk) * chunk, chunk)
        copies.append(pltpu.make_async_copy(table.at[pl.ds(start, chunk)], items.at[j], sems.at[3 + j]))
    for copy in copies:
        copy.start()
    lane = iota((rows, rows), 1)
    copies[0].wait()
    own = jnp.where(lane == iota((rows, rows), 0), send_row[...].astype(F32), 0.0)
    home[...] = one_hot(jnp.sum(own, axis=1, keepdims=True) == lane.astype(F32))
    copies[1].wait()
    for j in range(per):
        copies[3 + j].wait()
        own = iota((chunk, width), 0) == ids[j] % chunk
        neg_rows[j : j + 1] = jnp.sum(jnp.where(own, items[j].astype(F32), 0.0), axis=0, keepdims=True)
    step = coef_rows.shape[0] * rows // wide
    coefs = jnp.concatenate([coef_rows[b * step : (b + 1) * step].astype(F32) for b in range(wide // rows)], axis=1)
    negs = jnp.concatenate([neg_rows[0:per, b * wide : (b + 1) * wide] for b in range(width // wide)], axis=0)
    below[...] = jnp.concatenate([coefs, negs], axis=0).astype(BF16)
    copies[2].wait()


def pack_kernel(sizes, meta, b0, b1, held, below, home, *refs):
    n, rows, slots = sizes
    pairs = n // 2
    outs = refs[:pairs]
    pick, order_ref = refs[pairs:]
    head_dim = outs[0].shape[1] // PARTS
    width = head_dim * n
    cell = rows // n
    me = meta[0]
    filled, value = slot_table(meta, (b0, b1), order_ref)
    places = jnp.broadcast_to(slot_places(filled, value, me, cell), (rows, rows))
    by_rank = one_hot(slot_ranks(places) == iota((rows, rows), 1).astype(F32))
    chosen = dot(by_rank, home[...], ((0,), (0,)))
    pick[...] = chosen.astype(BF16)
    none = jnp.zeros((slots, rows), F32)
    both = jnp.concatenate(
        [jnp.concatenate([chosen[0:slots], none], axis=1), jnp.concatenate([none, chosen[0:slots]], axis=1)], axis=0
    ).astype(BF16)
    for d in range(pairs):
        columns = []
        for x in (2 * d, 2 * d + 1):
            first = pl.multiple_of((me ^ x) * head_dim, head_dim)
            columns.append(jnp.concatenate([held[:, pl.ds(i * width + first, head_dim)] for i in range(PARTS)], axis=1))
        outs[d][0 : 2 * slots] = dot(both, jnp.concatenate(columns, axis=0)).astype(BF16)
        outs[d][2 * slots :] = below[...]


def index_kernel(sizes, meta, b0, b1, pick, w_out, pick_in, pick_out, home_even, home_odd, tile, live, most, w_cols, order_ref, w_rows, sem):
    n, rows, slots, pool = sizes
    cell = rows // n
    live_cap = live.shape[0]
    head_dim = w_rows.shape[0]
    copy = pltpu.make_async_copy(w_out.at[pl.ds(pl.multiple_of(meta[0] * head_dim, head_dim), head_dim)], w_rows, sem)
    copy.start()
    span = pick_in.shape[1] // n
    me = meta[0]
    filled, value = slot_table(meta, (b0, b1), order_ref)
    lane = iota((rows, rows), 1)
    columns = [slot_places(filled, value, me ^ x, cell) for x in range(n)]
    places = jnp.zeros((rows, rows), F32)
    for x in range(n):
        places = jnp.where(lane == x, columns[x], places)
    ranks = slot_ranks(places)
    count = jnp.sum(jnp.where(places > 0.5, 1.0, 0.0), axis=0, keepdims=True)
    counts = [count[:, x : x + 1] for x in range(n)]
    lines_of = [pair_lines(meta, (me >> 1) ^ d) for d in range(n // 2)]
    excess = [c - slots for c in counts] + [counts[2 * d] + counts[2 * d + 1] + (lines_of[d] - pool).astype(F32) for d in range(n // 2)]
    most[...] = jnp.broadcast_to(functools.reduce(jnp.maximum, excess), most.shape)

    def placed(x, first, width):
        at = ranks[:, x : x + 1] + first
        hit = jnp.where(at == iota((rows, width), 1).astype(F32), columns[x], 0.0)
        return jnp.sum(hit, axis=0, keepdims=True)

    lines = []
    for x in range(n):
        first = span - slots if x % 2 else 0
        line = placed(x, first, max(span, rows))[:, :span]
        at = iota((1, span), 1)
        lines.append(jnp.where((at >= first) & (at < first + slots), line, 0.0))
    line = jnp.concatenate(lines, axis=1) - 1.0
    pick_in[...] = one_hot(iota((live_cap, line.shape[1]), 0).astype(F32) == line)
    reach = -(-pool // rows) * rows
    for d in range(n // 2):
        first = lines_of[d].astype(F32)
        line = placed(2 * d, first, reach) + placed(2 * d + 1, counts[2 * d] + first, reach) - 1.0
        hit = one_hot(iota((live_cap, reach), 0).astype(F32) == line)
        pick_out[d * pool : (d + 1) * pool] = jnp.transpose(hit.astype(F32))[:pool].astype(BF16)
    slot = iota((reach, rows), 0).astype(F32)
    for home, first in ((home_even, jnp.zeros((1, 1), F32)), (home_odd, counts[1])):
        first = first + lines_of[0].astype(F32)
        moved = dot(one_hot(slot == lane[0:1].astype(F32) + first), pick[...])
        home[...] = jnp.transpose(moved).astype(BF16)
    quarter = tile.shape[1] // PARTS
    line = iota((rows, quarter), 1)
    row = iota((rows, quarter), 0)
    before = jnp.where(me % 2 == 1, meta[LENS + (me ^ 1)], 0)
    for b in range(PARTS):
        hit = (line + b * lines_of[0] == row + before) & (line < lines_of[0]) & (row < meta[LENS + me])
        tile[:, b * quarter : (b + 1) * quarter] = one_hot(hit)
    copy.wait()
    w_cols[...] = jnp.transpose(w_rows[...].astype(F32)).astype(BF16)
    live[...] = jnp.where(pair_live(live_cap, starts_of(meta, n)), 1.0 / rows, 0.0)


def pair_live(live_cap, starts):
    row = iota((live_cap, 1), 0)
    col = iota((1, live_cap), 1)
    return (col <= row) & (tile_of(col, starts) > tile_of(row, starts) - SPAN) & (row < starts[-1])


def forward_kernel(sizes, meta, pick, live, w_cols, *refs):
    n, rows, slots, per = sizes
    blocks = refs[:n]
    compact, weights, att, stats, coef_c, d_mixed, negatives, neg_rows = refs[n:]
    live_cap, head_dim = att.shape
    negs = coef_c.shape[0]
    wide = blocks[0].shape[1]
    span = pick.shape[1] // n
    me = meta[0]
    received = [block[2 * slots - span : 2 * slots] if x % 2 else block[0:span] for x, block in enumerate(blocks)]
    both = dot(pick[...], jnp.concatenate(received, axis=0)).astype(BF16)
    compact[...] = both
    total = jnp.zeros((negs, live_cap), F32)
    lane = iota((negs, live_cap), 1)
    step = negs * rows // wide
    for x in range(n):
        t = me ^ x
        start = start_of(meta, n, t)
        below = blocks[x][2 * slots :].astype(F32)
        coefs = jnp.concatenate([below[0:step, b * rows : (b + 1) * rows] for b in range(wide // rows)], axis=0)
        coefs = jnp.concatenate([coefs, jnp.zeros((negs, live_cap - rows), F32)], axis=1)
        total = jnp.where((lane >= start) & (lane < start + meta[LENS + t]), pltpu.roll(coefs, start, 1), total)
        for b in range(n * head_dim // wide):
            neg_rows[t, 0:per, b * wide : (b + 1) * wide] = below[step + b * per : step + (b + 1) * per]
    coef_t = total.astype(BF16)
    coef_c[...] = coef_t
    neg = jnp.concatenate([neg_rows[s, 0:per] for s in range(n)], axis=0).astype(BF16)
    negatives[...] = neg
    head_grad = dot(coef_t, neg, ((0,), (0,))).astype(BF16)
    dm = dot(head_grad, w_cols[...])
    d_mixed[...] = dm
    u, v, q, k = (both[:, i * head_dim : (i + 1) * head_dim] for i in range(PARTS))
    scores = dot(q, k, ((1,), (1,))) * (1.0 / math.sqrt(head_dim))
    sig = jax.nn.sigmoid(scores)
    w = (scores * sig * live[...]).astype(BF16)
    weights[...] = w
    a = dot(w, v)
    att[...] = a
    dn = dm * u.astype(F32)
    mean = jnp.sum(a, axis=1, keepdims=True) * (1.0 / head_dim)
    cen = a - mean
    lane = iota((live_cap, 128), 1)
    cols = jnp.where(lane == 0, mean, 0.0)
    cols = jnp.where(lane == 1, jnp.sum(cen * cen, axis=1, keepdims=True), cols)
    cols = jnp.where(lane == 2, jnp.sum(dn, axis=1, keepdims=True), cols)
    cols = jnp.where(lane == 3, jnp.sum(dn * cen, axis=1, keepdims=True), cols)
    stats[...] = jnp.transpose(cols)[0:8]


def merge_stats(a, b, count):
    gap = b[0] - a[0]
    return (
        (a[0] + b[0]) * 0.5,
        a[1] + b[1] + gap * gap * (0.5 * count),
        a[2] + b[2],
        a[3] + b[3] + (b[2] - a[2]) * gap * 0.5,
    )


def pair_lines(meta, chip):
    return (meta[LENS + 2 * chip] + meta[LENS + 2 * chip + 1] + PARTS - 1) // PARTS


def start_of(meta, n, tile):
    start = jnp.int32(0)
    for t in range(n):
        start = start + jnp.where(t < tile, meta[LENS + t], 0)
    return start


def backward_kernel(sizes, meta, compact, weights, att, d_mixed, st0, st1, st2, st3, pick, live, *refs):
    n, rows, pool = sizes
    outs = refs[: n // 2]
    mixed_ref, mixed_rows = refs[n // 2 :]
    live_cap, head_dim = att.shape
    width = head_dim * n
    me = meta[0]
    quad = [[st[i : i + 1] for i in range(4)] for st in (st0, st1, st2, st3)]
    ab = merge_stats(quad[0], quad[1], 2 * head_dim)
    cd = merge_stats(quad[2], quad[3], 2 * head_dim)
    mean, m2, s_dn, s_dna = merge_stats(ab, cd, 4 * head_dim)
    inv = lax.rsqrt(m2 * (1.0 / width) + eps)
    table = jnp.concatenate([mean, inv, s_dn * (1.0 / width), s_dna * inv * (1.0 / width), jnp.zeros((124, live_cap), F32)], axis=0)
    table = jnp.transpose(table)
    mean, inv, mean_dn, mean_dnn = (table[:, i : i + 1] for i in range(4))
    both = compact[...]
    u, v, q, k = (both[:, i * head_dim : (i + 1) * head_dim] for i in range(PARTS))
    u = u.astype(F32)
    dm = d_mixed[...]
    normed = (att[...] - mean) * inv
    mixed = (normed * u).astype(BF16)
    dn = dm * u
    d_att = ((dn - mean_dn - normed * mean_dnn) * inv).astype(BF16)
    scale = 1.0 / math.sqrt(head_dim)
    scores = dot(q, k, ((1,), (1,))) * scale
    sig = jax.nn.sigmoid(scores)
    slope = sig * (1.0 + scores * (1.0 - sig)) * scale * live[...]
    ds = (dot(d_att, v, ((1,), (1,))) * slope).astype(BF16)
    grad = jnp.concatenate(
        [dm * normed, dot(weights[...], d_att, ((0,), (0,))), dot(ds, k), dot(ds, q, ((0,), (0,)))], axis=1
    ).astype(BF16)
    mixed_ref[...] = mixed
    sent = dot(pick[...], grad)
    mixed_rows[0:live_cap] = mixed.astype(F32)
    mixed_rows[live_cap:] = jnp.zeros((2 * rows, head_dim), F32)
    half = 2 * rows // PARTS
    row = iota((half, head_dim), 0)
    for d in range(n // 2):
        chip = (me >> 1) ^ d
        lines = pair_lines(meta, chip)
        count = meta[LENS + 2 * chip] + meta[LENS + 2 * chip + 1]
        parts = []
        for b in range(PARTS):
            part = mixed_rows[pl.ds(start_of(meta, n, 2 * chip) + b * lines, half), :]
            parts.append(jnp.where((row < lines) & (row + b * lines < count), part, 0.0))
        rows_out = sent[d * pool : (d + 1) * pool]
        outs[d][0:half] = (rows_out[0:half] + jnp.concatenate(parts, axis=1)).astype(BF16)
        outs[d][half:] = rows_out[half:].astype(BF16)


def sums_kernel(coef_c, mixed, most, sums):
    negs = coef_c.shape[0]
    sums[0:negs] = dot(coef_c[...], mixed[...])
    sums[negs:] = most[...]


def total_kernel(meta, even, odd, tile, negatives, w_out, *refs):
    sums, (d_w_out, most, kit, sem) = refs[:-4], refs[-4:]
    width = w_out.shape[0]
    copy = pltpu.make_async_copy(w_out, kit.at[pl.ds(0, width)], sem)
    copy.start()
    rows, reach = even.shape
    kit[width:, 0:reach] = even[...]
    kit[width:, reach : 2 * reach] = odd[...]
    kit[width:, 2 * reach : 2 * reach + 2 * rows] = tile[...]
    negs, groups = negatives.shape[0], len(sums)
    most[...] = functools.reduce(jnp.maximum, [part[negs:] for part in sums])
    rest = functools.reduce(jnp.add, [part[0:negs] for part in sums])
    columns = width // groups
    neg = negatives[:, pl.ds(pl.multiple_of(meta[1] * columns, columns), columns)]
    grad = jnp.zeros((rest.shape[1], columns), F32)
    for _ in range(3):
        piece = rest.astype(BF16)
        grad = grad + dot(piece, neg, ((0,), (0,)))
        rest = rest - piece.astype(F32)
    d_w_out[...] = grad
    copy.wait()


def finish_kernel(sizes, meta, kit, *refs):
    n, rows = sizes
    blocks, (d_home, layer_out) = refs[:n], refs[n:]
    width = kit.shape[1]
    head_dim = width // n
    quarter = rows // PARTS
    reach = -(-blocks[0].shape[0] // rows) * rows
    for x in range(n):
        head = pl.multiple_of((meta[0] ^ x) * head_dim, head_dim)
        block = blocks[x][...]
        pick = kit[width:, reach * (x % 2) : reach * (x % 2) + block.shape[0]]
        part = dot(pick, block).astype(BF16)
        for i in range(PARTS):
            d_home[:, pl.ds(i * width + head, head_dim)] = part[:, i * head_dim : (i + 1) * head_dim]
        lines = jnp.concatenate([block[0 : 2 * quarter, b * head_dim : (b + 1) * head_dim] for b in range(PARTS)], axis=0)
        layer_out[:, pl.ds(head, head_dim)] = dot(kit[width:, 2 * reach : 2 * reach + 2 * rows], lines).astype(BF16)
    layer = dot(layer_out[...], kit[0:width])
    layer_out[...] = layer.astype(BF16)


def kernel_call(body, shapes, specs, scratch=(), limit=40):
    return pl.pallas_call(
        body,
        out_shape=shapes,
        in_specs=specs,
        out_specs=jax.tree.map(lambda _: VMEM, shapes),
        scratch_shapes=scratch,
        compiler_params=pltpu.CompilerParams(vmem_limit_bytes=limit * 1024 * 1024),
    )


def swap(block, axis, distance):
    return lax.ppermute(block, axis, [(i, i ^ distance) for i in range(lax.axis_size(axis))])


def exchange(message, between):
    order = (1, 3, 2)
    far = {d: swap(message[d], "seq", 2 * d) for d in order}
    made = between()
    far[0] = message[0]
    far[order[-1]], made = lax.optimization_barrier((far[order[-1]], made))
    near = {d: swap(far[d], "seq", 1) for d in (0, *order)}
    blocks = [block for d in range(len(message)) for block in (far[d], near[d])]
    return blocks, made


def load_kernel(block, out):
    out[...] = block[...]


def join_kernel(first, second, out):
    out[0 : first.shape[0]] = first[...]
    out[first.shape[0] :] = second[...]


def gather_small(block, between):
    n = lax.axis_size("seq")
    known, distance = kernel_call(load_kernel, jax.ShapeDtypeStruct(block.shape, block.dtype), [VMEM])(block), 1
    while distance < n // 2:
        shape = jax.ShapeDtypeStruct((2 * known.shape[0], known.shape[1]), known.dtype)
        known = kernel_call(join_kernel, shape, [VMEM] * 2)(known, swap(block if distance == 1 else known, "seq", distance))
        distance *= 2
    known, made = lax.optimization_barrier((known, between()))
    return [known, swap(known, "seq", distance)], made


def head_plan(qkvu, w_out, head_coef, item_table, neg_ids, send_order, recv_order, tile_len):
    n = lax.axis_size("seq")
    groups = lax.axis_size("dp")
    rows = qkvu.shape[0]
    width = w_out.shape[0]
    head_dim = width // HEADS
    negs = head_coef.shape[1]
    per = neg_ids.shape[0]
    wide = PARTS * head_dim
    live_cap = -(-(n * rows // 3) // 128) * 128
    sds = jax.ShapeDtypeStruct
    me = lax.axis_index("seq")
    meta = jnp.concatenate([jnp.stack([me, lax.axis_index("dp")]).astype(jnp.int32), tile_len[0]])
    head_coef_t = head_coef.T

    half = n // 2
    quarter = rows // PARTS
    below = (negs * rows + per * width) // wide

    def passes(slots, pool):
        span = -(-slots // 8) * 8
        reach = -(-pool // rows) * rows
        def prep():
            return kernel_call(
                prep_kernel,
                (sds(qkvu.shape, BF16), sds((below, wide), BF16), sds((rows, rows), BF16)),
                [SMEM] + [ANY] * 4,
                [
                    pltpu.VMEM((1, rows), jnp.int32),
                    pltpu.VMEM((negs, rows), BF16),
                    pltpu.VMEM((per, 16, width), BF16),
                    pltpu.VMEM((8, width), F32),
                    pltpu.SemaphoreType.DMA((3 + per,)),
                ],
            )(neg_ids, send_order, head_coef_t, item_table, qkvu)

        orders, prepared = gather_small(recv_order, prep)
        *message, pick = kernel_call(
            functools.partial(pack_kernel, (n, rows, slots)),
            (sds((2 * slots + below, wide), BF16),) * half + (sds((rows, rows), BF16),),
            [SMEM] + [VMEM] * 5,
            [pltpu.VMEM((n, 1, rows), F32)],
        )(meta, *orders, *prepared)

        def index():
            return kernel_call(
                functools.partial(index_kernel, (n, rows, slots, pool)),
                (
                    sds((live_cap, n * span), BF16),
                    sds((half * pool, live_cap), BF16),
                    sds((rows, reach), BF16),
                    sds((rows, reach), BF16),
                    sds((rows, 2 * rows), BF16),
                    sds((live_cap, live_cap), F32),
                    sds((8, 128), F32),
                    sds((width, head_dim), BF16),
                ),
                [SMEM] + [VMEM] * 3 + [ANY],
                [pltpu.VMEM((n, 1, rows), F32), pltpu.VMEM((head_dim, width), BF16), pltpu.SemaphoreType.DMA],
            )(meta, *orders, pick, w_out)

        received, (pick_in, pick_out, even, odd, tile, live, most, w_cols) = exchange(message, index)
        compact, weights, att, stats, coef_c, d_mixed, negatives = kernel_call(
            functools.partial(forward_kernel, (n, rows, slots, per)),
            (
                sds((live_cap, wide), BF16),
                sds((live_cap, live_cap), BF16),
                sds((live_cap, head_dim), F32),
                sds((8, live_cap), F32),
                sds((negs, live_cap), BF16),
                sds((live_cap, head_dim), F32),
                sds((negs, width), BF16),
            ),
            [SMEM] + [VMEM] * (3 + n),
            [pltpu.VMEM((n, 8, width), F32)],
        )(meta, pick_in, live, w_cols, *received)
        paired = merge_stats(stats, swap(stats, "seq", 1), head_dim)
        paired = jnp.stack(list(paired) + [jnp.zeros_like(stats[0])] * 4)
        far = [swap(paired, "seq", d) for d in range(n - 2, 0, -2)]
        *back, mixed = kernel_call(
            functools.partial(backward_kernel, (n, rows, pool)),
            (sds((pool, wide), BF16),) * half + (sds((live_cap, head_dim), BF16),),
            [SMEM] + [VMEM] * 10,
            [pltpu.VMEM((live_cap + 2 * rows, head_dim), F32)],
        )(meta, compact, weights, att, d_mixed, paired, *far, pick_out, live)

        def group_sums():
            sums = kernel_call(sums_kernel, sds((negs + 8, head_dim), F32), [VMEM] * 3)(coef_c, mixed, most)
            sums = [sums] + [swap(sums, "dp", d) for d in (2, 3, 1)]
            d_w, most_of_all, kit = kernel_call(
                total_kernel,
                (sds((head_dim, width // groups), F32), sds((8, 128), F32), sds((width + rows, width), BF16)),
                [SMEM] + [VMEM] * 4 + [ANY] + [VMEM] * groups,
                [pltpu.SemaphoreType.DMA],
            )(meta, even, odd, tile, negatives, w_out, *sums)
            return d_w, kit, most_of_all

        returned, (d_w, kit, most_of_all) = exchange(back, group_sums)
        return most_of_all[0, 0] > 0.0, (d_w, kit, *returned)

    def finish(d_w, *parts):
        outs = kernel_call(
            functools.partial(finish_kernel, (n, rows)),
            (sds((rows, PARTS * width), BF16), sds((rows, width), BF16)),
            [SMEM] + [VMEM] * (1 + n),
        )(meta, *parts)
        return (*outs, d_w)

    overflow, parts = passes(SLOTS, POOL)
    d_home, layer_out, d_w_out = lax.cond(
        overflow, lambda *_: finish(*passes(rows, 2 * rows + 2 * quarter)[1]), lambda *outs: outs, *finish(*parts)
    )
    return (layer_out, d_home, d_w_out)


def solution(mesh):
    placed = (
        P(("dp", "seq"), None),
        P(),
        P(("dp", "seq"), None),
        P("seq", None),
        P("seq"),
        P(("dp", "seq"), None),
        P(("dp", "seq"), None),
        P("dp", None),
    )
    return jax.shard_map(
        head_plan if mesh.shape["seq"] == HEADS else tile_plan,
        mesh=mesh,
        in_specs=placed,
        out_specs=(P(("dp", "seq"), None), P(("dp", "seq"), None), P("seq", "dp")),
        check_vma=False,
    )
```
